128 devices in a mesh: row: 16 (over z_hi, y, core), col: 8 (over z_lo, x).
Axes of the slice: x: 4, y: 4, z: 4 (z_hi: 2, z_lo: 2; z = z_hi * 2 + z_lo), core: 2. Of those that a mesh axis runs over, the one named last changes fastest.
Arguments:
- field: float32 [512, 1024, 128], P('row', 'col'), may hold values from -6 to 6
- context: float32 [128, 256, 128], P('row', 'col'), may hold values from -6 to 6
- ctx_weight: float32 [128, 128], replicated, may hold values from -0.5 to 0.5
- norm_gains: float32 [5, 128], replicated, may hold values from 0.1 to 1.9
- expand_weight: float32 [128, 512], replicated, may hold values from -0.5 to 0.5
- depth_weight: float32 [3, 3, 512], replicated, may hold values from -2 to 2
- se_reduce: float32 [512, 32], replicated, may hold values from -4 to 4
- se_expand: float32 [32, 512], replicated, may hold values from -6 to 6
- project_weight: float32 [512, 128], replicated, may hold values from -0.25 to 0.25
- attn_qkv: float32 [2, 128, 384], replicated, may hold values from -3 to 3, as said below
- attn_out: float32 [2, 128, 128], replicated, may hold values from -0.5 to 0.5
- mlp_in: float32 [2, 128, 512], replicated, may hold values from -0.5 to 0.5
- mlp_out: float32 [2, 512, 128], replicated, may hold values from -0.25 to 0.25
Outputs:
- refined: float32 [512, 1024, 128], P('row', 'col')
The draws below stay inside these ranges and needn't reach their ends.
Inputs may be any that keep to these rules, and one draw needn't show every extreme that they name: `attn_qkv`: projection weights.
All inputs are finite; a program needn't handle non-finite values.
Results may differ from the reference program's by a relative error of at most 0.0003.
Values sent between devices are 32-bit elements; how exact they have to be, the bound alone decides.
No kernel may reach another device: no remote copies, remote signals or barrier semaphores. Data moves between devices by JAX's collectives and lax.ppermute only.
A program may use at most 128 MiB of HBM per device.

```python
import math
import jax
import jax.numpy as jnp
from jax import lax

CHANNELS = 128
HEADS = 4
EXPANDED = 512
MLP_HIDDEN = 512
SQUEEZE = 32
CONTEXT_CH = 128
WINDOW = 8
FIELD_ROWS = 512
FIELD_COLS = 1024


def draw_field(key, part):
    key = jax.random.fold_in(key, 11)
    latitude = jnp.arange(FIELD_ROWS, dtype=jnp.float32) / (FIELD_ROWS - 1)
    rising = 0.5 * jnp.exp(latitude * jnp.log(3.0))
    values = jnp.clip(jax.random.normal(key, (FIELD_ROWS, FIELD_COLS, CHANNELS), jnp.float32), -4.0, 4.0)
    return values * rising[:, None, None]


def draw_attn_qkv(key, part):
    key = jax.random.fold_in(key, 23)
    drawn = jax.random.normal(key, (2, CHANNELS, 3 * CHANNELS), jnp.float32) * CHANNELS ** (-0.5)
    return jnp.clip(drawn, -3.0, 3.0)


def steps_of(own_key, dims, split, low, largest):
    def one(dim, blocks):
        steps = jax.random.uniform(jax.random.fold_in(jax.random.fold_in(own_key, 6), dim), (blocks,), jnp.float32, low / len(split), largest / len(split))
        return jnp.repeat(jnp.exp(steps), dims[dim] // blocks).reshape((-1,) + (1,) * (len(dims) - dim - 1))

    factor_of = one(*split[0])
    for cut in split[1:]:
        factor_of = factor_of * one(*cut)
    return factor_of


def centred(stream_key, extent, width, limit, shards=(), kind=jnp.bfloat16):
    gain = steps_of(stream_key, extent, shards, -0.22, 0.18) if shards else 1.0
    values = jax.random.normal(stream_key, extent, jnp.float32) * width * gain
    return jnp.minimum(jnp.maximum(values, -limit), limit).astype(kind)


def setup_inputs(seed: int = 0) -> dict:
    key_list = jax.random.split(jax.random.key(seed), 14)
    field = draw_field(jax.random.fold_in(key_list[13], 71), 0)
    context = centred(key_list[1], (FIELD_ROWS // 4, FIELD_COLS // 4, CONTEXT_CH), 1.0, 6.0, ((0, 16), (1, 8)), jnp.float32)
    ctx_weight = centred(key_list[2], (CONTEXT_CH, CHANNELS), CONTEXT_CH ** -0.5, 0.5, (), jnp.float32)
    norm_gains = jnp.clip(1.0 + 0.18 * jax.random.normal(key_list[3], (5, CHANNELS), jnp.float32), 0.1, 1.9)
    expand_weight = centred(key_list[4], (CHANNELS, EXPANDED), CHANNELS ** -0.5, 0.5, (), jnp.float32)
    depth_weight = centred(key_list[5], (3, 3, EXPANDED), 9 ** -0.5, 2.0, (), jnp.float32)
    se_reduce = centred(key_list[6], (EXPANDED, SQUEEZE), 0.25, 4.0, (), jnp.float32)
    se_expand = centred(key_list[7], (SQUEEZE, EXPANDED), 0.5, 6.0, (), jnp.float32)
    project_weight = centred(key_list[8], (EXPANDED, CHANNELS), EXPANDED ** -0.5, 0.25, (), jnp.float32)
    attn_qkv = draw_attn_qkv(jax.random.fold_in(key_list[13], 71), 0)
    attn_out = centred(key_list[10], (2, CHANNELS, CHANNELS), CHANNELS ** -0.5, 0.5, (), jnp.float32)
    mlp_in = centred(key_list[11], (2, CHANNELS, MLP_HIDDEN), CHANNELS ** -0.5, 0.5, (), jnp.float32)
    mlp_out = centred(key_list[12], (2, MLP_HIDDEN, CHANNELS), MLP_HIDDEN ** -0.5, 0.25, (), jnp.float32)
    return dict(field=field, context=context, ctx_weight=ctx_weight, norm_gains=norm_gains, expand_weight=expand_weight, depth_weight=depth_weight, se_reduce=se_reduce, se_expand=se_expand, project_weight=project_weight, attn_qkv=attn_qkv, attn_out=attn_out, mlp_in=mlp_in, mlp_out=mlp_out)


PRECISE = lax.Precision.HIGHEST
EPSILON = 1e-05

def layer_norm(values, norm_gain):
    centre = lax.optimization_barrier(jnp.mean(values, axis=-1, keepdims=True))
    shifted = values - centre
    spread = lax.optimization_barrier(jnp.mean(shifted * shifted, axis=-1, keepdims=True))
    return shifted * lax.rsqrt(spread + EPSILON) * norm_gain

def interpolate(coarse_in, along):
    length = coarse_in.shape[along]
    before = lax.slice_in_dim(coarse_in, 0, length - 2, axis=along)
    middle = lax.slice_in_dim(coarse_in, 1, length - 1, axis=along)
    after_cell = lax.slice_in_dim(coarse_in, 2, length, axis=along)
    phases = [0.375 * before + 0.625 * middle, 0.125 * before + 0.875 * middle, 0.875 * middle + 0.125 * after_cell, 0.625 * middle + 0.375 * after_cell]
    stacked = jnp.stack(phases, axis=along + 1)
    new_shape = list(coarse_in.shape)
    new_shape[along] = 4 * (length - 2)
    return stacked.reshape(new_shape)

def upsample(rimmed):
    return interpolate(interpolate(rimmed, 0), 1)

def depthwise(padded, kernel):
    out_rows = padded.shape[0] - 2
    out_cols = padded.shape[1] - 2
    summed = jnp.zeros((out_rows, out_cols, padded.shape[2]), jnp.float32)
    for row_off in range(3):
        for col_off in range(3):
            summed = summed + padded[row_off:row_off + out_rows, col_off:col_off + out_cols] * kernel[row_off, col_off]
    return summed

def attend(windows, norm_gain, qkv_weight, out_weight):
    number, length, channels = windows.shape
    head_dim = channels // HEADS
    normed = layer_norm(windows, norm_gain)
    projected = jnp.einsum('nlc,cd->nld', normed, qkv_weight, precision=PRECISE)
    queries = projected[:, :, :channels].reshape(number, length, HEADS, head_dim)
    keyed = projected[:, :, channels:2 * channels].reshape(number, length, HEADS, head_dim)
    valued = projected[:, :, 2 * channels:].reshape(number, length, HEADS, head_dim)
    scores = jnp.einsum('nqhd,nkhd->nhqk', queries, keyed, precision=PRECISE) / math.sqrt(head_dim)
    weights = jax.nn.softmax(scores, axis=-1)
    blended = jnp.einsum('nhqk,nkhd->nqhd', weights, valued, precision=PRECISE).reshape(number, length, channels)
    return windows + jnp.einsum('nlc,cd->nld', blended, out_weight, precision=PRECISE)

def feed_forward(stream, norm_gain, weight_in, weight_out):
    inner = jax.nn.gelu(jnp.einsum('hwc,cf->hwf', layer_norm(stream, norm_gain), weight_in, precision=PRECISE))
    return stream + jnp.einsum('hwf,fc->hwc', inner, weight_out, precision=PRECISE)

def to_blocks(stream):
    all_rows, all_cols, channels = stream.shape
    shaped = stream.reshape(all_rows // WINDOW, WINDOW, all_cols // WINDOW, WINDOW, channels)
    return shaped.transpose(0, 2, 1, 3, 4).reshape(-1, WINDOW * WINDOW, channels)

def from_blocks(windows, all_rows, all_cols):
    channels = windows.shape[-1]
    shaped = windows.reshape(all_rows // WINDOW, all_cols // WINDOW, WINDOW, WINDOW, channels)
    return shaped.transpose(0, 2, 1, 3, 4).reshape(all_rows, all_cols, channels)

def to_grid(stream):
    all_rows, all_cols, channels = stream.shape
    shaped = stream.reshape(WINDOW, all_rows // WINDOW, WINDOW, all_cols // WINDOW, channels)
    return shaped.transpose(1, 3, 0, 2, 4).reshape(-1, WINDOW * WINDOW, channels)

def from_grid(windows, all_rows, all_cols):
    channels = windows.shape[-1]
    shaped = windows.reshape(all_rows // WINDOW, all_cols // WINDOW, WINDOW, WINDOW, channels)
    return shaped.transpose(2, 0, 3, 1, 4).reshape(all_rows, all_cols, channels)

def reference(field, context, ctx_weight, norm_gains, expand_weight, depth_weight, se_reduce, se_expand, project_weight, attn_qkv, attn_out, mlp_in, mlp_out):
    coarse = jnp.einsum('hwk,kc->hwc', context, ctx_weight, precision=PRECISE)
    stream = field + upsample(jnp.pad(coarse, ((1, 1), (1, 1), (0, 0))))
    hidden = jax.nn.gelu(jnp.einsum('hwc,ce->hwe', layer_norm(stream, norm_gains[0]), expand_weight, precision=PRECISE))
    active = jax.nn.gelu(depthwise(jnp.pad(hidden, ((1, 1), (1, 1), (0, 0))), depth_weight))
    pooled = lax.optimization_barrier(jnp.sum(active, axis=(0, 1))) / (FIELD_ROWS * FIELD_COLS)
    squeezed = jax.nn.silu(jnp.dot(pooled, se_reduce, precision=PRECISE))
    gate_vec = jax.nn.sigmoid(jnp.dot(squeezed, se_expand, precision=PRECISE))
    stream = stream + jnp.einsum('hwe,ec->hwc', active * gate_vec, project_weight, precision=PRECISE)
    stream = from_blocks(attend(to_blocks(stream), norm_gains[1], attn_qkv[0], attn_out[0]), FIELD_ROWS, FIELD_COLS)
    stream = feed_forward(stream, norm_gains[2], mlp_in[0], mlp_out[0])
    stream = from_grid(attend(to_grid(stream), norm_gains[3], attn_qkv[1], attn_out[1]), FIELD_ROWS, FIELD_COLS)
    return feed_forward(stream, norm_gains[4], mlp_in[1], mlp_out[1])
```

```python
import math

import jax
import jax.numpy as jnp
import numpy as np
from jax import lax
from jax.experimental import pallas as pl
from jax.experimental.pallas import tpu as pltpu
from jax.sharding import Mesh
from jax.sharding import PartitionSpec as P

HEADS = 4
WINDOW = 8
CHANNELS = 128
EXPANDED = 512
MLP_HIDDEN = 512
SQUEEZE = 32
HEAD_DIM = CHANNELS // HEADS
CELLS = WINDOW * WINDOW
GROUP = 64
WIDE = 136
EPSILON = 1e-05
F32 = jnp.float32
BF16 = jnp.bfloat16
HIGHEST = lax.Precision.HIGHEST
CHUNKS = 2
STEP = 512
VMEM_LIMIT = 56 * 1024 * 1024

GELU_A = 2.0 * math.sqrt(2.0 / math.pi)
GELU_B = 4.0 * GELU_A * 0.044715


def gelu_of_half(half):
    return half * jnp.tanh(half * (GELU_A + GELU_B * (half * half))) + half


def split(x):
    high = x.astype(BF16)
    low = (x - high.astype(F32)).astype(BF16)
    return high, low


def dot(a, b):
    return jnp.dot(a, b, preferred_element_type=F32)


def rows_of(parts):
    return jnp.concatenate(parts, axis=0)


def lanes_of(parts):
    return jnp.concatenate(parts, axis=1)


def normed(x, gain):
    centre = jnp.mean(x, axis=-1, keepdims=True)
    shifted = x - centre
    spread = jnp.mean(shifted * shifted, axis=-1, keepdims=True)
    return shifted * lax.rsqrt(spread + EPSILON) * gain


def three(x):
    high, low = split(x)
    return lanes_of([high, low, high])


def stack_rows(weight):
    high, low = split(weight)
    return rows_of([high, high, low])


def deep_weight(weight):
    return lanes_of(split(weight))


def prepare_weights(qkv_ref, out_ref, in_ref, mlp_ref, k3, qv3, out3, in3, mlp_pair):
    scale = math.log2(math.e) / math.sqrt(HEAD_DIM)
    k3[...] = stack_rows(qkv_ref[0, :, CHANNELS : 2 * CHANNELS])
    turned = rows_of(
        [(qkv_ref[0, :, :CHANNELS] * scale).T, qkv_ref[0, :, 2 * CHANNELS :].T]
    )
    high, low = split(turned)
    qv3[...] = lanes_of([high, high, low])
    out3[...] = stack_rows(out_ref[0])
    in3[...] = stack_rows(0.5 * in_ref[0])
    mlp_pair[...] = deep_weight(mlp_ref[0])


PAIR = 2 * CELLS


def attention(pairs, gain, k3, qv3, out3):
    zero = jnp.zeros((HEAD_DIM, PAIR), F32)
    zero_block = jnp.zeros((2 * HEAD_DIM, PAIR), BF16)
    left = lax.broadcasted_iota(jnp.int32, (HEAD_DIM, PAIR), 1) < CELLS
    left_all = lax.broadcasted_iota(jnp.int32, (CHANNELS, PAIR), 1) < CELLS
    natural, turned = [], []
    for x in pairs:
        n = normed(x, gain)
        natural.append(three(n))
        high, low = split(n.T)
        turned.append(rows_of([high, low, high]))
    keys = dot(rows_of(natural), k3)
    both = dot(qv3, lanes_of(turned))
    scores = []
    for p in range(len(pairs)):
        key3 = three(keys[p * PAIR : (p + 1) * PAIR])
        query = both[:CHANNELS, p * PAIR : (p + 1) * PAIR]
        swapped = pltpu.roll(query, CELLS, 1)
        for second in range(2):
            here, there = (swapped, query) if second else (query, swapped)
            blocks_high, blocks_low = [], []
            for group in range(2):
                at = [slice(h * HEAD_DIM, (h + 1) * HEAD_DIM) for h in (2 * group, 2 * group + 1)]
                block = rows_of([jnp.where(left, here[at[0]], zero), jnp.where(left, zero, there[at[1]])])
                high, low = split(block)
                order = (lambda b: [b, zero_block]) if group == 0 else (lambda b: [zero_block, b])
                blocks_high.append(lanes_of(order(high)))
                blocks_low.append(lanes_of(order(low)))
            high, low = rows_of(blocks_high), rows_of(blocks_low)
            scores.append(dot(key3[second * CELLS : (second + 1) * CELLS], rows_of([high, high, low])))
    weights, scales = [], []
    for score in scores:
        weight = jnp.exp2(score - jnp.max(score, axis=0, keepdims=True))
        scales.append(1.0 / jnp.sum(weight, axis=0, keepdims=True))
        high, low = split(weight)
        weights.append(rows_of([high, high, low, low]))
    mixed = []
    for p in range(len(pairs)):
        value = both[CHANNELS:, p * PAIR : (p + 1) * PAIR]
        high = value.astype(BF16).astype(F32)
        low = pltpu.roll(value - high, CELLS, 1)
        first = jnp.where(left_all, high, low).astype(BF16)
        second = jnp.where(left_all, low, high).astype(BF16)
        mixed.append(dot(lanes_of([first, first]), weights[2 * p]))
        mixed.append(dot(lanes_of([second, second]), weights[2 * p + 1]))
    blended = []
    for p in range(len(pairs)):
        parts = []
        for h in range(HEADS):
            lanes = slice(128 * (h // 2), 128 * (h // 2) + 128)
            of_a, of_b = (
                mixed[2 * p + i][h * HEAD_DIM : (h + 1) * HEAD_DIM, lanes]
                * scales[2 * p + i][:, lanes]
                for i in range(2)
            )
            if h % 2:
                of_a = pltpu.roll(of_a, CELLS, 1)
            else:
                of_b = pltpu.roll(of_b, CELLS, 1)
            parts.append(jnp.where(left, of_a, of_b))
        blended.append(three(rows_of(parts).T))
    added = dot(rows_of(blended), out3)
    return [x + added[p * PAIR : (p + 1) * PAIR] for p, x in enumerate(pairs)]


def split_blocks(x, rows, make):
    highs, lows = [], []
    for r in range(0, x.shape[0], rows):
        made = [split(make(x[r : r + rows, c : c + 128])) for c in range(0, x.shape[1], 128)]
        highs.append(lanes_of([m[0] for m in made]))
        lows.append(lanes_of([m[1] for m in made]))
    return rows_of(highs), rows_of(lows)


def feed_forward(pairs, gain, in3, mlp_pair):
    inner = dot(rows_of([three(normed(x, gain)) for x in pairs]), in3)
    high, low = split_blocks(inner, 64, gelu_of_half)
    wide = dot(high, mlp_pair)
    rest = dot(low, mlp_pair[:, :CHANNELS])
    out = []
    for p, x in enumerate(pairs):
        at = slice(p * PAIR, (p + 1) * PAIR)
        out.append(x + (wide[at, :CHANNELS] + (wide[at, CHANNELS:] + rest[at])))
    return out


def column_weights():
    fine = np.zeros((WIDE, 40), np.float32)
    table = ((0.375, 0.625, 0.0), (0.125, 0.875, 0.0), (0.0, 0.875, 0.125), (0.0, 0.625, 0.375))

    def fill(at, column):
        k, o = column // 4, column % 4
        for step, weight in zip((-1, 0, 1), table[o]):
            if weight:
                fine[at, (k + step) % 40] = weight

    for column in range(129):
        fill(column, column)
    fill(135, -1)
    return np.concatenate([fine, fine], axis=1)


ROW_WEIGHTS = ((0.375, 0.625, -1), (0.125, 0.875, -1), (0.875, 0.125, 0), (0.625, 0.375, 0))


def lift_kernel(
    place_ref, field_ref, context_ref, above_ref, below_ref, before_ref, after_ref, up_ref,
    ctxw_ref, gains_ref, expand_ref, depth_ref, reduce_ref, lifted_ref, active_ref, sum_ref,
    lift, ctx, coarse, hid, expand3, total,
):
    step = pl.program_id(0)
    sublane = lax.broadcasted_iota(jnp.int32, (8, 128), 0)
    first_row, last_row = sublane == 0, sublane == 7

    @pl.when(step == 0)
    def _():
        expand3[...] = stack_rows(0.5 * expand_ref[...])
        total[...] = jnp.zeros_like(total)
        lift[0, :128] = above_ref[:128]
        lift[33, :128] = below_ref[:128]
        lift[1:33, :128] = field_ref[...]
        ctx[0, :32] = above_ref[128:]
        ctx[9, :32] = below_ref[128:]
        ctx[1:9, :32] = context_ref[...]
        zero = jnp.zeros((8, 128), F32)
        for e in range(44):
            after = jnp.broadcast_to(after_ref[e : e + 1], (8, 128))
            before = jnp.broadcast_to(before_ref[e : e + 1], (8, 128))
            group = jnp.where(first_row, after, jnp.where(last_row, before, zero))
            if e < 34:
                lift[e, 128:] = group
            else:
                ctx[e - 34, 32:] = group
        weight = stack_rows(ctxw_ref[...])
        projected = dot(three(ctx[...].reshape(400, CHANNELS)), weight)
        for k in range(10):
            high, low = split(projected[40 * k : 40 * k + 40])
            coarse[k] = dot(up_ref[...], rows_of([high, low]))

    has_after = jnp.where(place_ref[1] < 7, 1.0, 0.0)
    has_before = jnp.where(place_ref[1] > 0, 1.0, 0.0)
    inside = jnp.where(first_row, has_after, has_before)

    def hidden_rows(first, fine_first, k_first, count):
        parts = []
        for i in range(0, count, 2):
            two = []
            for j in (i, i + 1):
                k, o = (fine_first + j) // 4, (fine_first + j) % 4
                lower, upper, shift = ROW_WEIGHTS[o]
                at = k_first + k + shift
                x = lift[first + j] + (lower * coarse[at] + upper * coarse[at + 1])
                lift[first + j] = x
                two.append(x)
            parts.append(three(normed(rows_of(two), gains_ref[0:1])))
        made = dot(rows_of(parts), expand3[...])
        for i in range(count):
            for c in range(0, EXPANDED, 128):
                out = gelu_of_half(made[i * WIDE : (i + 1) * WIDE, c : c + 128])
                hid[first + i, :128, c : c + 128] = out[:128]
                hid[first + i, 128:, c : c + 128] = out[128:] * inside

    @pl.when(step == 0)
    def _():
        hidden_rows(0, -1, 1, 2)

        @pl.when(place_ref[0] == 0)
        def _():
            hid[0] = jnp.zeros((WIDE, EXPANDED), F32)

    hidden_rows(8 * step + 2, 1, 2 * step + 1, 4)
    hidden_rows(8 * step + 6, 5, 2 * step + 1, 4)

    @pl.when((step == 3) & (place_ref[0] == 15))
    def _():
        hid[33] = jnp.zeros((WIDE, EXPANDED), F32)

    lifted_ref[...] = lift[pl.ds(8 * step + 1, 8), :128]

    for part in range(EXPANDED // 128):
        lanes = slice(part * 128, (part + 1) * 128)
        taps = [
            [jnp.broadcast_to(0.5 * depth_ref[i, j : j + 1, lanes], (8, 128)) for j in range(3)]
            for i in range(3)
        ]

        def row(r, summed):
            def columns(g):
                seen = [hid[8 * step + r + i, 8 * g : 8 * g + 8, lanes] for i in range(3)]
                a, b, c = (
                    seen[0] * taps[0][j] + seen[1] * taps[1][j] + seen[2] * taps[2][j]
                    for j in range(3)
                )
                return pltpu.roll(a, 1, 0), b, pltpu.roll(c, 7, 0)

            halo = columns(16)
            held, here = halo[0], columns(0)
            for g in range(16):
                following = columns(g + 1) if g < 15 else halo
                out = gelu_of_half(
                    here[1]
                    + jnp.where(first_row, held, here[0])
                    + jnp.where(last_row, following[2], here[2])
                )
                active_ref[r, 8 * g : 8 * g + 8, lanes] = out
                summed = summed + out
                held, here = here[0], following
            return summed

        total[:, lanes] = lax.fori_loop(0, 8, row, total[:, lanes])

    @pl.when(step == 3)
    def _():
        squeezed = lax.dot_general(
            total[...], reduce_ref[...], (((1,), (1,)), ((), ())), precision=HIGHEST,
            preferred_element_type=F32,
        )
        squeezed = jnp.sum(squeezed, axis=0, keepdims=True)
        padded = lanes_of([squeezed, jnp.zeros((1, 128 - SQUEEZE), F32)])
        sum_ref[...] = jnp.broadcast_to(padded, sum_ref.shape)


def whole(shape):
    return pl.BlockSpec(shape, lambda *_: (0,) * len(shape))


def of_layer(array, layer):
    shape = (1,) + array.shape[1:]
    return pl.BlockSpec(shape, lambda *_: (layer,) + (0,) * (len(shape) - 1))


def lift_stage(place, args, copies):
    up = jnp.asarray(column_weights(), BF16)
    args = args[:6] + (up,) + args[6:]
    return pl.pallas_call(
        lift_kernel,
        grid=(4,),
        in_specs=[pl.BlockSpec(memory_space=pltpu.SMEM)] + [whole(a.shape) for a in args],
        out_specs=[
            pl.BlockSpec((8, 128, CHANNELS), lambda s: (s, 0, 0)),
            pl.BlockSpec((8, 128, EXPANDED), lambda s: (s, 0, 0)),
            whole((copies, 128)),
        ],
        out_shape=[
            jax.ShapeDtypeStruct((32, 128, CHANNELS), F32),
            jax.ShapeDtypeStruct((32, 128, EXPANDED), F32),
            jax.ShapeDtypeStruct((copies, 128), F32),
        ],
        scratch_shapes=[
            pltpu.VMEM((34, WIDE, CHANNELS), F32),
            pltpu.VMEM((10, 40, CHANNELS), F32),
            pltpu.VMEM((10, WIDE, CHANNELS), F32),
            pltpu.VMEM((34, WIDE, EXPANDED), F32),
            pltpu.VMEM((3 * CHANNELS, EXPANDED), BF16),
            pltpu.VMEM((8, EXPANDED), F32),
        ],
        compiler_params=pltpu.CompilerParams(vmem_limit_bytes=VMEM_LIMIT),
        cost_estimate=pl.CostEstimate(
            flops=8_000_000_000, bytes_accessed=14_000_000, transcendentals=0
        ),
    )(place, *args)


def block_kernel(
    cells_total, lifted_ref, active_ref, sums_ref, sexp_ref, project_ref, gains_ref, qkv_ref,
    aout_ref, min_ref, mout_ref, out_ref, project, *weights,
):
    @pl.when(pl.program_id(0) == 0)
    def _():
        pooled = jnp.sum(sums_ref[...], axis=0, keepdims=True) * (1.0 / cells_total)
        squeezed = pooled[:, :SQUEEZE]
        squeezed = squeezed * jax.nn.sigmoid(squeezed)
        wide = jnp.broadcast_to(squeezed, (CHANNELS, SQUEEZE))
        gate = jnp.dot(wide, sexp_ref[...], precision=HIGHEST, preferred_element_type=F32)
        project[...] = deep_weight(project_ref[...] * jax.nn.sigmoid(gate).T)
        prepare_weights(qkv_ref, aout_ref, min_ref, mout_ref, *weights)

    k3, qv3, out3, in3, mlp_pair = (w[...] for w in weights)
    highs, lows = [], []
    for w in range(STEP // CELLS):
        cells = active_ref[:, 8 * w : 8 * w + 8, :].reshape(CELLS, EXPANDED)
        high, low = split(cells)
        highs.append(high)
        lows.append(low)
    wide = dot(rows_of(highs), project[...])
    rest = dot(rows_of(lows), project[:, :CHANNELS])
    pairs = []
    for p in range(STEP // PAIR):
        at = slice(p * PAIR, (p + 1) * PAIR)
        x = rows_of(
            [lifted_ref[:, 8 * w : 8 * w + 8, :].reshape(CELLS, CHANNELS) for w in (2 * p, 2 * p + 1)]
        )
        pairs.append(x + (wide[at, :CHANNELS] + (wide[at, CHANNELS:] + rest[at])))
    pairs = attention(pairs, gains_ref[1:2], k3, qv3, out3)
    pairs = feed_forward(pairs, gains_ref[2:3], in3, mlp_pair)
    for p, x in enumerate(pairs):
        out_ref[p * PAIR : (p + 1) * PAIR] = x


WEIGHT_SCRATCH = [
    pltpu.VMEM((3 * CHANNELS, CHANNELS), BF16),
    pltpu.VMEM((2 * CHANNELS, 3 * CHANNELS), BF16),
    pltpu.VMEM((3 * CHANNELS, CHANNELS), BF16),
    pltpu.VMEM((3 * CHANNELS, MLP_HIDDEN), BF16),
    pltpu.VMEM((MLP_HIDDEN, 2 * CHANNELS), BF16),
]


def block_stage(chunk, lifted, active, sums, se_expand, project, gains, weights, cells_total):
    per_row = 128 // (STEP // 8)
    steps = 4 // CHUNKS * per_row
    row_base = chunk * (4 // CHUNKS)
    rest = (sums, se_expand, project, gains)

    def strip(channels):
        return pl.BlockSpec(
            (8, STEP // 8, channels), lambda s: (row_base + s // per_row, s % per_row, 0)
        )

    def body(*refs):
        block_kernel(cells_total, *refs)

    return pl.pallas_call(
        body,
        grid=(steps,),
        in_specs=[strip(CHANNELS), strip(EXPANDED)]
        + [whole(a.shape) for a in rest]
        + [of_layer(w, 0) for w in weights],
        out_specs=pl.BlockSpec((STEP, CHANNELS), lambda s: (s, 0)),
        out_shape=jax.ShapeDtypeStruct((steps * STEP, CHANNELS), F32),
        scratch_shapes=[pltpu.VMEM((EXPANDED, 2 * CHANNELS), BF16)] + WEIGHT_SCRATCH,
        compiler_params=pltpu.CompilerParams(vmem_limit_bytes=VMEM_LIMIT),
        cost_estimate=pl.CostEstimate(
            flops=14_000_000_000, bytes_accessed=8_000_000, transcendentals=0
        ),
    )(lifted, active, *rest, *weights)


def grid_kernel(x_ref, gains_ref, qkv_ref, aout_ref, min_ref, mout_ref, out_ref, *weights):
    @pl.when(pl.program_id(0) == 0)
    def _():
        prepare_weights(qkv_ref, aout_ref, min_ref, mout_ref, *weights)

    k3, qv3, out3, in3, mlp_pair = (w[...] for w in weights)
    flat_in = x_ref.reshape(STEP, CHANNELS)
    flat_out = out_ref.reshape(STEP, CHANNELS)
    windows = [flat_in[pl.ds(p, GROUP, stride=8), :] for p in range(8)]
    pairs = [rows_of(windows[i : i + 2]) for i in range(0, 8, 2)]
    pairs = attention(pairs, gains_ref[3:4], k3, qv3, out3)
    pairs = feed_forward(pairs, gains_ref[4:5], in3, mlp_pair)
    for p in range(8):
        flat_out[pl.ds(p, GROUP, stride=8), :] = pairs[p // 2][(p % 2) * GROUP : (p % 2 + 1) * GROUP]


def grid_stage(received, gains, weights):
    per_device = received.shape[1]
    block = pl.BlockSpec((GROUP, 8, CHANNELS), lambda s: (0, s, 0))
    return pl.pallas_call(
        grid_kernel,
        grid=(per_device // 8,),
        in_specs=[block, whole(gains.shape)] + [of_layer(w, 1) for w in weights],
        out_specs=block,
        out_shape=jax.ShapeDtypeStruct(received.shape, F32),
        scratch_shapes=WEIGHT_SCRATCH,
        compiler_params=pltpu.CompilerParams(vmem_limit_bytes=VMEM_LIMIT),
        cost_estimate=pl.CostEstimate(
            flops=14_000_000_000, bytes_accessed=4_000_000, transcendentals=0
        ),
    )(received, gains, *weights)


def neighbours(low_edge, high_edge, axis, count):
    forward = [(i, i + 1) for i in range(count - 1)]
    backward = [(i + 1, i) for i in range(count - 1)]
    return lax.ppermute(high_edge, axis, forward), lax.ppermute(low_edge, axis, backward)


def per_device(
    field, context, ctx_weight, norm_gains, expand_weight, depth_weight, se_reduce, se_expand,
    project_weight, attn_qkv, attn_out, mlp_in, mlp_out,
):
    row_axis = ("rg", "core")
    rows, cols = 16, 8
    row = lax.axis_index(row_axis)
    col = lax.axis_index("col")

    above, below = neighbours(
        jnp.concatenate([field[0], context[0]], axis=0),
        jnp.concatenate([field[-1], context[-1]], axis=0),
        row_axis,
        rows,
    )

    def edge(at, coarse_at):
        ends = [
            above[at : at + 1], field[:, at], below[at : at + 1],
            above[coarse_at : coarse_at + 1], context[:, coarse_at - 128],
            below[coarse_at : coarse_at + 1],
        ]
        return jnp.concatenate(ends, axis=0)

    before, after = neighbours(edge(0, 128), edge(127, 159), "col", cols)
    place = jnp.stack([row, col]).astype(jnp.int32)
    lifted, active, partial = lift_stage(
        place,
        (
            field, context, above, below, before, after, ctx_weight, norm_gains, expand_weight,
            depth_weight, se_reduce.T,
        ),
        rows,
    )

    def exchange(x, axes):
        return lax.all_to_all(x, axes, split_axis=0, concat_axis=0, tiled=True)

    partial = jnp.sum(exchange(partial[:, None, :], row_axis), axis=0, keepdims=True)
    sums = exchange(jnp.broadcast_to(partial, (cols, 1, 128)), "col")[:, 0, :]

    weights = (attn_qkv, attn_out, mlp_in, mlp_out)
    cells_total = rows * cols * field.shape[0] * field.shape[1]
    group = ("rg", "col")
    pieces = []
    for chunk in range(CHUNKS):
        mine = block_stage(
            chunk, lifted, active, sums, se_expand, project_weight, norm_gains, weights, cells_total
        )
        sent = exchange(mine.reshape(GROUP, -1, CHANNELS), group)
        back = exchange(grid_stage(sent, norm_gains, weights), group)
        windows = back.reshape(4 // CHUNKS, 16, WINDOW, WINDOW, CHANNELS)
        pieces.append(windows.transpose(0, 2, 1, 3, 4).reshape(-1, 128, CHANNELS))
    return jnp.concatenate(pieces, axis=0)


def solution(mesh):
    fine = Mesh(mesh.devices.reshape(8, 2, 8), ("rg", "core", "col"))
    tiled = P(("rg", "core"), "col", None)
    return jax.shard_map(
        per_device,
        mesh=fine,
        in_specs=(tiled, tiled) + (P(),) * 11,
        out_specs=tiled,
        check_vma=False,
    )
```

```python
import math

import jax
import jax.numpy as jnp
import numpy as np
from jax import lax
from jax.experimental import pallas as pl
from jax.experimental.pallas import tpu as pltpu
from jax.sharding import Mesh
from jax.sharding import PartitionSpec as P

HEADS = 4
WINDOW = 8
CHANNELS = 128
EXPANDED = 512
MLP_HIDDEN = 512
SQUEEZE = 32
HEAD_DIM = CHANNELS // HEADS
CELLS = WINDOW * WINDOW
GROUP = 64
WIDE = 136
EPSILON = 1e-05
F32 = jnp.float32
BF16 = jnp.bfloat16
HIGHEST = lax.Precision.HIGHEST
CHUNKS = 2
STEP = 512
VMEM_LIMIT = 56 * 1024 * 1024

GELU_A = 2.0 * math.sqrt(2.0 / math.pi)
GELU_B = 4.0 * GELU_A * 0.044715


def gelu_of_half(half):
    return half * jnp.tanh(half * (GELU_A + GELU_B * (half * half))) + half


def split(x):
    high = x.astype(BF16)
    low = (x - high.astype(F32)).astype(BF16)
    return high, low


def dot(a, b):
    return jnp.dot(a, b, preferred_element_type=F32)


def rows_of(parts):
    return jnp.concatenate(parts, axis=0)


def lanes_of(parts):
    return jnp.concatenate(parts, axis=1)


def normed(x, gain):
    centre = jnp.mean(x, axis=-1, keepdims=True)
    shifted = x - centre
    spread = jnp.mean(shifted * shifted, axis=-1, keepdims=True)
    return shifted * lax.rsqrt(spread + EPSILON) * gain


def normed_by_product(x, gain):
    averaging = jnp.full((2 * CHANNELS, CHANNELS), 1.0 / CHANNELS, BF16)
    shifted = x - dot(lanes_of(split(x)), averaging)
    spread = dot(lanes_of(split(shifted * shifted)), averaging)
    return shifted * lax.rsqrt(spread + EPSILON) * gain


def three(x):
    high, low = split(x)
    return lanes_of([high, low, high])


def stack_rows(weight):
    high, low = split(weight)
    return rows_of([high, high, low])


def deep_weight(weight):
    return lanes_of(split(weight))


def prepare_weights(qkv_ref, out_ref, in_ref, mlp_ref, k3, qv3, out3, in3, mlp_pair):
    scale = math.log2(math.e) / math.sqrt(HEAD_DIM)
    k3[...] = stack_rows(qkv_ref[0, :, CHANNELS : 2 * CHANNELS])
    turned = rows_of(
        [(qkv_ref[0, :, :CHANNELS] * scale).T, qkv_ref[0, :, 2 * CHANNELS :].T]
    )
    high, low = split(turned)
    qv3[...] = lanes_of([high, high, low])
    out3[...] = stack_rows(out_ref[0])
    in3[...] = stack_rows(0.5 * in_ref[0])
    mlp_pair[...] = deep_weight(mlp_ref[0])


PAIR = 2 * CELLS
PART = 256


def attend_and_feed(pairs, gains, k3, qv3, out3, in3, mlp_pair, finish):
    zero = jnp.zeros((HEAD_DIM, PAIR), F32)
    zero_block = jnp.zeros((2 * HEAD_DIM, PAIR), BF16)
    left = lax.broadcasted_iota(jnp.int32, (HEAD_DIM, PAIR), 1) < CELLS
    left_all = lax.broadcasted_iota(jnp.int32, (CHANNELS, PAIR), 1) < CELLS
    if not isinstance(pairs, list):
        pairs = yield from pairs
    natural, turned = [], []
    for x in pairs:
        n = normed(x, gains[0])
        natural.append(three(n))
        high, low = split(n.T)
        turned.append(rows_of([high, low, high]))
    yield
    keys = dot(rows_of(natural), k3[...])
    both = dot(qv3[...], lanes_of(turned))
    yield
    sides, value_sides = [], []
    for p in range(len(pairs)):
        key3 = three(keys[p * PAIR : (p + 1) * PAIR])
        query = both[:CHANNELS, p * PAIR : (p + 1) * PAIR]
        swapped = pltpu.roll(query, CELLS, 1)
        for second in range(2):
            here, there = (swapped, query) if second else (query, swapped)
            blocks_high, blocks_low = [], []
            for group in range(2):
                at = [slice(h * HEAD_DIM, (h + 1) * HEAD_DIM) for h in (2 * group, 2 * group + 1)]
                block = [jnp.where(left, here[at[0]], zero), jnp.where(left, zero, there[at[1]])]
                high, low = split(rows_of(block))
                order = (lambda b: [b, zero_block]) if group == 0 else (lambda b: [zero_block, b])
                blocks_high.append(lanes_of(order(high)))
                blocks_low.append(lanes_of(order(low)))
            high, low = rows_of(blocks_high), rows_of(blocks_low)
            sides.append((key3[second * CELLS : (second + 1) * CELLS], rows_of([high, high, low])))
        value = both[CHANNELS:, p * PAIR : (p + 1) * PAIR]
        high = value.astype(BF16).astype(F32)
        low = pltpu.roll(value - high, CELLS, 1)
        first = jnp.where(left_all, high, low).astype(BF16)
        second = jnp.where(left_all, low, high).astype(BF16)
        value_sides += [lanes_of([first, first]), lanes_of([second, second])]
    yield
    scores = [dot(key, query) for key, query in sides]
    yield
    weights, scales = [], []
    for score in scores:
        weight = jnp.exp2(score - jnp.max(score, axis=0, keepdims=True))
        scales.append(1.0 / jnp.sum(weight, axis=0, keepdims=True))
        high, low = split(weight)
        weights.append(rows_of([high, high, low, low]))
    yield
    mixed = [dot(value, weight) for value, weight in zip(value_sides, weights)]
    yield
    blended = []
    for p in range(len(pairs)):
        parts = []
        for h in range(HEADS):
            lanes = slice(128 * (h // 2), 128 * (h // 2) + 128)
            of_a, of_b = (
                mixed[2 * p + i][h * HEAD_DIM : (h + 1) * HEAD_DIM, lanes]
                * scales[2 * p + i][:, lanes]
                for i in range(2)
            )
            if h % 2:
                of_a = pltpu.roll(of_a, CELLS, 1)
            else:
                of_b = pltpu.roll(of_b, CELLS, 1)
            parts.append(jnp.where(left, of_a, of_b))
        blended.append(three(rows_of(parts).T))
    yield
    added = dot(rows_of(blended), out3[...])
    yield
    pairs = [x + added[p * PAIR : (p + 1) * PAIR] for p, x in enumerate(pairs)]
    parts = [three(normed(x, gains[1])) for x in pairs]
    yield
    inner = dot(rows_of(parts), in3[...])
    yield
    high, low = split_blocks(inner, 64, gelu_of_half)
    yield
    wide = dot(high, mlp_pair[...])
    rest = dot(low, mlp_pair[:, :CHANNELS])
    yield
    for p, x in enumerate(pairs):
        at = slice(p * PAIR, (p + 1) * PAIR)
        finish(p, x + (wide[at, :CHANNELS] + (wide[at, CHANNELS:] + rest[at])))


def staggered(groups):
    waiting, running = list(groups), []
    while waiting or running:
        if waiting:
            running.append(waiting.pop(0))
        for group in list(running):
            try:
                next(group)
            except StopIteration:
                running.remove(group)


def split_blocks(x, rows, make):
    highs, lows = [], []
    for r in range(0, x.shape[0], rows):
        made = [split(make(x[r : r + rows, c : c + 128])) for c in range(0, x.shape[1], 128)]
        highs.append(lanes_of([m[0] for m in made]))
        lows.append(lanes_of([m[1] for m in made]))
    return rows_of(highs), rows_of(lows)


def column_weights():
    fine = np.zeros((WIDE, 40), np.float32)
    table = ((0.375, 0.625, 0.0), (0.125, 0.875, 0.0), (0.0, 0.875, 0.125), (0.0, 0.625, 0.375))

    def fill(at, column):
        k, o = column // 4, column % 4
        for step, weight in zip((-1, 0, 1), table[o]):
            if weight:
                fine[at, (k + step) % 40] = weight

    for column in range(129):
        fill(column, column)
    fill(135, -1)
    return np.concatenate([fine, fine], axis=1)


ROW_WEIGHTS = ((0.375, 0.625, -1), (0.125, 0.875, -1), (0.875, 0.125, 0), (0.625, 0.375, 0))


def lift_kernel(
    place_ref, field_ref, context_ref, above_ref, below_ref, before_ref, after_ref, up_ref,
    ctxw_ref, gains_ref, expand_ref, depth_ref, reduce_ref, lifted_ref, active_ref, sum_ref,
    lift, ctx, coarse, hid, expand3, total,
):
    step = pl.program_id(0)
    sublane = lax.broadcasted_iota(jnp.int32, (8, 128), 0)
    first_row, last_row = sublane == 0, sublane == 7

    @pl.when(step == 0)
    def _():
        expand3[...] = stack_rows(0.5 * expand_ref[...])
        total[...] = jnp.zeros_like(total)
        lift[0, :128] = above_ref[:128]
        lift[33, :128] = below_ref[:128]
        lift[1:33, :128] = field_ref[...]
        ctx[0, :32] = above_ref[128:]
        ctx[9, :32] = below_ref[128:]
        ctx[1:9, :32] = context_ref[...]
        zero = jnp.zeros((8, 128), F32)
        for e in range(44):
            after = jnp.broadcast_to(after_ref[e : e + 1], (8, 128))
            before = jnp.broadcast_to(before_ref[e : e + 1], (8, 128))
            group = jnp.where(first_row, after, jnp.where(last_row, before, zero))
            if e < 34:
                lift[e, 128:] = group
            else:
                ctx[e - 34, 32:] = group
        weight = stack_rows(ctxw_ref[...])
        projected = dot(three(ctx[...].reshape(400, CHANNELS)), weight)
        for k in range(10):
            high, low = split(projected[40 * k : 40 * k + 40])
            coarse[k] = dot(up_ref[...], rows_of([high, low]))

    has_after = jnp.where(place_ref[1] < 7, 1.0, 0.0)
    has_before = jnp.where(place_ref[1] > 0, 1.0, 0.0)
    inside = jnp.where(first_row, has_after, has_before)

    def hidden_rows(first, fine_first, k_first, count):
        parts = []
        for i in range(0, count, 2):
            two = []
            for j in (i, i + 1):
                k, o = (fine_first + j) // 4, (fine_first + j) % 4
                lower, upper, shift = ROW_WEIGHTS[o]
                at = k_first + k + shift
                x = lift[first + j] + (lower * coarse[at] + upper * coarse[at + 1])
                lift[first + j] = x
                two.append(x)
            parts.append(three(normed_by_product(rows_of(two), gains_ref[0:1])))
        made = dot(rows_of(parts), expand3[...])
        for i in range(count):
            for c in range(0, EXPANDED, 128):
                out = gelu_of_half(made[i * WIDE : (i + 1) * WIDE, c : c + 128])
                hid[first + i, :128, c : c + 128] = out[:128]
                hid[first + i, 128:, c : c + 128] = out[128:] * inside

    @pl.when(step == 0)
    def _():
        hidden_rows(0, -1, 1, 2)

        @pl.when(place_ref[0] == 0)
        def _():
            hid[0] = jnp.zeros((WIDE, EXPANDED), F32)

    def four_hidden(t, carry):
        hidden_rows(8 * step + 2 + 4 * t, 1, 2 * step + 1 + t, 4)
        return carry

    lax.fori_loop(0, 2, four_hidden, 0)

    @pl.when((step == 3) & (place_ref[0] == 15))
    def _():
        hid[33] = jnp.zeros((WIDE, EXPANDED), F32)

    lifted_ref[...] = lift[pl.ds(8 * step + 1, 8), :128]

    for part in range(EXPANDED // 128):
        lanes = slice(part * 128, (part + 1) * 128)
        taps = [
            [jnp.broadcast_to(0.5 * depth_ref[i, j : j + 1, lanes], (8, 128)) for j in range(3)]
            for i in range(3)
        ]

        def row(r, summed):
            def columns(g):
                seen = [hid[8 * step + r + i, 8 * g : 8 * g + 8, lanes] for i in range(3)]
                a, b, c = (
                    seen[0] * taps[0][j] + seen[1] * taps[1][j] + seen[2] * taps[2][j]
                    for j in range(3)
                )
                return pltpu.roll(a, 1, 0), b, pltpu.roll(c, 7, 0)

            halo = columns(16)
            held, here = halo[0], columns(0)
            for g in range(16):
                following = columns(g + 1) if g < 15 else halo
                out = gelu_of_half(
                    here[1]
                    + jnp.where(first_row, held, here[0])
                    + jnp.where(last_row, following[2], here[2])
                )
                active_ref[r, 8 * g : 8 * g + 8, lanes] = out
                summed = summed + out
                held, here = here[0], following
            return summed

        def four_rows(t, summed):
            for i in range(4):
                summed = row(4 * t + i, summed)
            return summed

        total[:, lanes] = lax.fori_loop(0, 2, four_rows, total[:, lanes])

    @pl.when(step == 3)
    def _():
        squeezed = lax.dot_general(
            total[...], reduce_ref[...], (((1,), (1,)), ((), ())), precision=HIGHEST,
            preferred_element_type=F32,
        )
        squeezed = jnp.sum(squeezed, axis=0, keepdims=True)
        padded = lanes_of([squeezed, jnp.zeros((1, 128 - SQUEEZE), F32)])
        sum_ref[...] = jnp.broadcast_to(padded, sum_ref.shape)


def whole(shape):
    return pl.BlockSpec(shape, lambda *_: (0,) * len(shape))


def of_layer(array, layer):
    shape = (1,) + array.shape[1:]
    return pl.BlockSpec(shape, lambda *_: (layer,) + (0,) * (len(shape) - 1))


def lift_stage(place, args, copies):
    up = jnp.asarray(column_weights(), BF16)
    args = args[:6] + (up,) + args[6:]
    return pl.pallas_call(
        lift_kernel,
        grid=(4,),
        in_specs=[pl.BlockSpec(memory_space=pltpu.SMEM)] + [whole(a.shape) for a in args],
        out_specs=[
            pl.BlockSpec((8, 128, CHANNELS), lambda s: (s, 0, 0)),
            pl.BlockSpec((8, 128, EXPANDED), lambda s: (s, 0, 0)),
            whole((copies, 128)),
        ],
        out_shape=[
            jax.ShapeDtypeStruct((32, 128, CHANNELS), F32),
            jax.ShapeDtypeStruct((32, 128, EXPANDED), F32),
            jax.ShapeDtypeStruct((copies, 128), F32),
        ],
        scratch_shapes=[
            pltpu.VMEM((34, WIDE, CHANNELS), F32),
            pltpu.VMEM((10, 40, CHANNELS), F32),
            pltpu.VMEM((10, WIDE, CHANNELS), F32),
            pltpu.VMEM((34, WIDE, EXPANDED), F32),
            pltpu.VMEM((3 * CHANNELS, EXPANDED), BF16),
            pltpu.VMEM((8, EXPANDED), F32),
        ],
        compiler_params=pltpu.CompilerParams(vmem_limit_bytes=VMEM_LIMIT),
        cost_estimate=pl.CostEstimate(
            flops=8_000_000_000, bytes_accessed=14_000_000, transcendentals=0
        ),
    )(place, *args)


def block_kernel(
    cells_total, lifted_ref, active_ref, sums_ref, sexp_ref, project_ref, gains_ref, qkv_ref,
    aout_ref, min_ref, mout_ref, out_ref, project, *weights,
):
    @pl.when(pl.program_id(0) == 0)
    def _():
        pooled = jnp.sum(sums_ref[...], axis=0, keepdims=True) * (1.0 / cells_total)
        squeezed = pooled[:, :SQUEEZE]
        squeezed = squeezed * jax.nn.sigmoid(squeezed)
        wide = jnp.broadcast_to(squeezed, (CHANNELS, SQUEEZE))
        gate = jnp.dot(wide, sexp_ref[...], precision=HIGHEST, preferred_element_type=F32)
        project[...] = deep_weight(project_ref[...] * jax.nn.sigmoid(gate).T)
        prepare_weights(qkv_ref, aout_ref, min_ref, mout_ref, *weights)

    def cells_of(ref, w, channels):
        at = pl.ds(pl.multiple_of(8 * w, 8), 8)
        return ref[:, at, :].reshape(CELLS, channels)

    def projected(start):
        highs, lows = [], []
        for w in range(PART // CELLS):
            high, low = split(cells_of(active_ref, start + w, EXPANDED))
            highs.append(high)
            lows.append(low)
        yield
        wide = dot(rows_of(highs), project[...])
        rest = dot(rows_of(lows), project[:, :CHANNELS])
        yield
        pairs = []
        for p in range(PART // PAIR):
            at = slice(p * PAIR, (p + 1) * PAIR)
            x = rows_of([cells_of(lifted_ref, start + 2 * p + i, CHANNELS) for i in range(2)])
            pairs.append(x + (wide[at, :CHANNELS] + (wide[at, CHANNELS:] + rest[at])))
        return pairs

    def group(part, carry):
        def finish(p, x):
            out_ref[pl.ds(pl.multiple_of(part * PART + p * PAIR, PAIR), PAIR)] = x

        both_gains = (gains_ref[1:2], gains_ref[2:3])
        start = part * (PART // CELLS)
        staggered([attend_and_feed(projected(start), both_gains, *weights, finish)])
        return carry

    lax.fori_loop(0, STEP // PART, group, 0)


WEIGHT_SCRATCH = [
    pltpu.VMEM((3 * CHANNELS, CHANNELS), BF16),
    pltpu.VMEM((2 * CHANNELS, 3 * CHANNELS), BF16),
    pltpu.VMEM((3 * CHANNELS, CHANNELS), BF16),
    pltpu.VMEM((3 * CHANNELS, MLP_HIDDEN), BF16),
    pltpu.VMEM((MLP_HIDDEN, 2 * CHANNELS), BF16),
]


def block_stage(chunk, lifted, active, sums, se_expand, project, gains, weights, cells_total):
    per_row = 128 // (STEP // 8)
    steps = 4 // CHUNKS * per_row
    row_base = chunk * (4 // CHUNKS)
    rest = (sums, se_expand, project, gains)

    def strip(channels):
        return pl.BlockSpec(
            (8, STEP // 8, channels), lambda s: (row_base + s // per_row, s % per_row, 0)
        )

    def body(*refs):
        block_kernel(cells_total, *refs)

    return pl.pallas_call(
        body,
        grid=(steps,),
        in_specs=[strip(CHANNELS), strip(EXPANDED)]
        + [whole(a.shape) for a in rest]
        + [of_layer(w, 0) for w in weights],
        out_specs=pl.BlockSpec((STEP, CHANNELS), lambda s: (s, 0)),
        out_shape=jax.ShapeDtypeStruct((steps * STEP, CHANNELS), F32),
        scratch_shapes=[pltpu.VMEM((EXPANDED, 2 * CHANNELS), BF16)] + WEIGHT_SCRATCH,
        compiler_params=pltpu.CompilerParams(vmem_limit_bytes=VMEM_LIMIT),
        cost_estimate=pl.CostEstimate(
            flops=14_000_000_000, bytes_accessed=8_000_000, transcendentals=0
        ),
    )(lifted, active, *rest, *weights)


def grid_kernel(x_ref, gains_ref, qkv_ref, aout_ref, min_ref, mout_ref, *rest):
    out_ref, *weights = rest[-6:]

    @pl.when(pl.program_id(0) == 0)
    def _():
        prepare_weights(qkv_ref, aout_ref, min_ref, mout_ref, *weights)

    flat_in = x_ref.reshape(STEP, CHANNELS)
    flat_out = out_ref.reshape(STEP, CHANNELS)

    def group(part, carry):
        first = part * 2
        pairs = [rows_of([flat_in[pl.ds(first + p, GROUP, stride=8), :] for p in range(2)])]

        def finish(p, x):
            for i in range(2):
                flat_out[pl.ds(first + i, GROUP, stride=8), :] = x[i * GROUP : (i + 1) * GROUP]

        staggered([attend_and_feed(pairs, (gains_ref[3:4], gains_ref[4:5]), *weights, finish)])
        return carry

    lax.fori_loop(0, 4, group, 0)


def grid_stage(received, gains, weights, chunk, earlier):
    per_device = received.shape[1]
    steps = per_device // 8
    in_specs = [pl.BlockSpec((GROUP, 8, CHANNELS), lambda s: (0, s, 0)), whole(gains.shape)]
    in_specs += [of_layer(w, 1) for w in weights]
    args = (received, gains) + weights
    aliases = {}
    if earlier is not None:
        in_specs.append(pl.BlockSpec(memory_space=pl.ANY))
        aliases = {len(args): 0}
        args += (earlier,)
    return pl.pallas_call(
        grid_kernel,
        grid=(steps,),
        in_specs=in_specs,
        out_specs=pl.BlockSpec((GROUP, 8, CHANNELS), lambda s: (0, chunk * steps + s, 0)),
        out_shape=jax.ShapeDtypeStruct((GROUP, CHUNKS * per_device, CHANNELS), F32),
        scratch_shapes=WEIGHT_SCRATCH,
        input_output_aliases=aliases,
        compiler_params=pltpu.CompilerParams(vmem_limit_bytes=VMEM_LIMIT),
        cost_estimate=pl.CostEstimate(
            flops=14_000_000_000, bytes_accessed=4_000_000, transcendentals=0
        ),
    )(*args)


def neighbours(low_edge, high_edge, axis, count):
    forward = [(i, i + 1) for i in range(count - 1)]
    backward = [(i + 1, i) for i in range(count - 1)]
    return lax.ppermute(high_edge, axis, forward), lax.ppermute(low_edge, axis, backward)


def per_device(
    field, context, ctx_weight, norm_gains, expand_weight, depth_weight, se_reduce, se_expand,
    project_weight, attn_qkv, attn_out, mlp_in, mlp_out,
):
    row_axis = ("rg", "core")
    rows, cols = 16, 8
    row = lax.axis_index(row_axis)
    col = lax.axis_index("col")

    above, below = neighbours(
        jnp.concatenate([field[0], context[0]], axis=0),
        jnp.concatenate([field[-1], context[-1]], axis=0),
        row_axis,
        rows,
    )

    def edge(at, coarse_at):
        ends = [
            above[at : at + 1], field[:, at], below[at : at + 1],
            above[coarse_at : coarse_at + 1], context[:, coarse_at - 128],
            below[coarse_at : coarse_at + 1],
        ]
        return jnp.concatenate(ends, axis=0)

    before, after = neighbours(edge(0, 128), edge(127, 159), "col", cols)
    place = jnp.stack([row, col]).astype(jnp.int32)
    lifted, active, partial = lift_stage(
        place,
        (
            field, context, above, below, before, after, ctx_weight, norm_gains, expand_weight,
            depth_weight, se_reduce.T,
        ),
        rows * cols,
    )

    def exchange(x, axes):
        return lax.all_to_all(x, axes, split_axis=0, concat_axis=0, tiled=True)

    sums = exchange(partial[:, None, :], ("rg", "core", "col"))[:, 0, :]

    weights = (attn_qkv, attn_out, mlp_in, mlp_out)
    cells_total = rows * cols * field.shape[0] * field.shape[1]
    group = ("rg", "col")
    sent = []
    for chunk in range(CHUNKS):
        mine = block_stage(
            chunk, lifted, active, sums, se_expand, project_weight, norm_gains, weights, cells_total
        )
        sent.append(exchange(mine.reshape(GROUP, -1, CHANNELS), group))
    attended = None
    for chunk in range(CHUNKS):
        attended = grid_stage(sent[chunk], norm_gains, weights, chunk, attended)
    back = exchange(attended, group)
    halves = back.reshape(4 // CHUNKS, 16, 2, CHUNKS, WINDOW // 2, WINDOW, CHANNELS)
    return halves.transpose(3, 0, 2, 4, 1, 5, 6).reshape(field.shape)


def solution(mesh):
    fine = Mesh(mesh.devices.reshape(8, 2, 8), ("rg", "core", "col"))
    tiled = P(("rg", "core"), "col", None)
    return jax.shard_map(
        per_device,
        mesh=fine,
        in_specs=(tiled, tiled) + (P(),) * 11,
        out_specs=tiled,
        check_vma=False,
    )
```

```python
import math

import jax
import jax.numpy as jnp
import numpy as np
from jax import lax
from jax.experimental import pallas as pl
from jax.experimental.pallas import tpu as pltpu
from jax.sharding import Mesh
from jax.sharding import PartitionSpec as P

HEADS = 4
WINDOW = 8
CHANNELS = 128
EXPANDED = 512
MLP_HIDDEN = 512
SQUEEZE = 32
HEAD_DIM = CHANNELS // HEADS
CELLS = WINDOW * WINDOW
GROUP = 64
WIDE = 136
EPSILON = 1e-05
F32 = jnp.float32
BF16 = jnp.bfloat16
HIGHEST = lax.Precision.HIGHEST
CHUNKS = 2
BLOCK_STEP = 1024
GRID_STEP = 2048
VMEM_LIMIT = 56 * 1024 * 1024

GELU_A = 2.0 * math.sqrt(2.0 / math.pi)
GELU_B = 4.0 * GELU_A * 0.044715


def gelu_of_half(half):
    return half * jnp.tanh(half * (GELU_A + GELU_B * (half * half))) + half


def split(x):
    high = x.astype(BF16)
    low = (x - high.astype(F32)).astype(BF16)
    return high, low


def dot(a, b):
    return jnp.dot(a, b, preferred_element_type=F32)


def rows_of(parts):
    return jnp.concatenate(parts, axis=0)


def lanes_of(parts):
    return jnp.concatenate(parts, axis=1)


def normed(x):
    shifted = x - jnp.mean(x, axis=-1, keepdims=True)
    spread = jnp.sum(shifted * shifted, axis=-1, keepdims=True)
    return shifted * lax.rsqrt(spread + CHANNELS * EPSILON)


def gained(weight, gain):
    column = jnp.broadcast_to(gain * math.sqrt(CHANNELS), (CHANNELS, CHANNELS)).T
    return lanes_of([weight[:, c : c + 128] * column for c in range(0, weight.shape[1], 128)])


def three(x):
    high, low = split(x)
    return lanes_of([high, low, high])


def stack_rows(weight):
    high, low = split(weight)
    return rows_of([high, high, low])


def deep_weight(weight):
    return lanes_of(split(weight))


def prepare_attention(qkv_ref, out_ref, gain, k3, qv3, out3):
    scale = math.log2(math.e) / math.sqrt(HEAD_DIM)
    k3[...] = stack_rows(gained(qkv_ref[0, :, CHANNELS : 2 * CHANNELS], gain))
    row_gain = gain * math.sqrt(CHANNELS)
    queries = qkv_ref[0, :, :CHANNELS].T * (row_gain * scale)
    values = qkv_ref[0, :, 2 * CHANNELS :].T * row_gain
    high, low = split(rows_of([queries, values]))
    qv3[...] = lanes_of([high, high, low])
    out3[...] = stack_rows(out_ref[0])


def prepare_feed(in_ref, mlp_ref, gain, in3, mlp_pair):
    in3[...] = stack_rows(gained(0.5 * in_ref[0], gain))
    mlp_pair[...] = deep_weight(mlp_ref[0])


PAIR = 2 * CELLS
PART = 512


def attend(pairs, k3, qv3, out3):
    left = lax.broadcasted_iota(jnp.int32, (HEAD_DIM, PAIR), 1) < CELLS
    left_all = lax.broadcasted_iota(jnp.int32, (CHANNELS, PAIR), 1) < CELLS
    zero = jnp.zeros((HEAD_DIM, PAIR), BF16)
    zero_block = jnp.zeros((2 * HEAD_DIM, PAIR), BF16)
    natural, turned = [], []
    for x in pairs:
        high, low = split(normed(x))
        natural.append(lanes_of([high, low, high]))
        high, low = high.T, low.T
        turned.append(rows_of([high, low, high]))
    yield
    keys = dot(rows_of(natural), k3[...])
    both = dot(qv3[...], lanes_of(turned))
    yield
    sides, value_sides = [], []

    def by_heads(straight, swapped):
        blocks = []
        for group in range(2):
            at = [slice(h * HEAD_DIM, (h + 1) * HEAD_DIM) for h in (2 * group, 2 * group + 1)]
            block = rows_of(
                [jnp.where(left, straight[at[0]], zero), jnp.where(left, zero, swapped[at[1]])]
            )
            blocks.append(lanes_of([zero_block, block] if group else [block, zero_block]))
        return rows_of(blocks)

    for p in range(len(pairs)):
        at = slice(p * PAIR, (p + 1) * PAIR)
        key3 = three(keys[at])
        high, low = split(both[:CHANNELS, at])
        high_swapped, low_swapped = pltpu.roll(high, CELLS, 1), pltpu.roll(low, CELLS, 1)
        for second in range(2):
            if second:
                h, l = by_heads(high_swapped, high), by_heads(low_swapped, low)
            else:
                h, l = by_heads(high, high_swapped), by_heads(low, low_swapped)
            sides.append((key3[second * CELLS : (second + 1) * CELLS], rows_of([h, h, l])))
        high, low = split(both[CHANNELS:, at])
        low = pltpu.roll(low, CELLS, 1)
        first, second = jnp.where(left_all, high, low), jnp.where(left_all, low, high)
        value_sides += [lanes_of([first, first]), lanes_of([second, second])]
    yield
    scores = [dot(key, query) for key, query in sides]
    yield
    weights, scales = [], []
    for score in scores:
        weight = jnp.exp2(score - jnp.max(score, axis=0, keepdims=True))
        scales.append(1.0 / jnp.sum(weight, axis=0, keepdims=True))
        high, low = split(weight)
        weights.append(rows_of([high, high, low, low]))
    yield
    mixed = [
        [dot(value[64 * g : 64 * g + 64], weight[:, 128 * g : 128 * g + 128]) for g in range(2)]
        for value, weight in zip(value_sides, weights)
    ]
    yield
    blended = []
    for p in range(len(pairs)):
        parts = []
        for h in range(HEADS):
            lanes = slice(128 * (h // 2), 128 * (h // 2) + 128)
            at = slice((h % 2) * HEAD_DIM, (h % 2 + 1) * HEAD_DIM)
            of_a, of_b = (
                mixed[2 * p + i][h // 2][at] * scales[2 * p + i][:, lanes] for i in range(2)
            )
            if h % 2:
                of_a = pltpu.roll(of_a, CELLS, 1)
            else:
                of_b = pltpu.roll(of_b, CELLS, 1)
            parts.append(jnp.where(left, of_a, of_b))
        blended.append(three(rows_of(parts).T))
    yield
    added = dot(rows_of(blended), out3[...])
    yield
    return [x + added[p * PAIR : (p + 1) * PAIR] for p, x in enumerate(pairs)]


def feed(pairs, in3, mlp_pair):
    parts = [three(normed(x)) for x in pairs]
    yield
    inner = dot(rows_of(parts), in3[...])
    yield
    high, low = split_blocks(inner, 64, gelu_of_half)
    yield
    wide = dot(high, mlp_pair[...])
    rest = dot(low, mlp_pair[:, :CHANNELS])
    yield
    out = []
    for p, x in enumerate(pairs):
        at = slice(p * PAIR, (p + 1) * PAIR)
        out.append(x + (wide[at, :CHANNELS] + (wide[at, CHANNELS:] + rest[at])))
    return out


def staggered(groups):
    waiting, running = list(groups), []
    while waiting or running:
        if waiting:
            running.append(waiting.pop(0))
        for group in list(running):
            try:
                next(group)
            except StopIteration:
                running.remove(group)


def split_blocks(x, rows, make):
    highs, lows = [], []
    for r in range(0, x.shape[0], rows):
        made = [split(make(x[r : r + rows, c : c + 128])) for c in range(0, x.shape[1], 128)]
        highs.append(lanes_of([m[0] for m in made]))
        lows.append(lanes_of([m[1] for m in made]))
    return rows_of(highs), rows_of(lows)


def column_weights():
    fine = np.zeros((WIDE, 40), np.float32)
    table = ((0.375, 0.625, 0.0), (0.125, 0.875, 0.0), (0.0, 0.875, 0.125), (0.0, 0.625, 0.375))

    def fill(at, column):
        k, o = column // 4, column % 4
        for step, weight in zip((-1, 0, 1), table[o]):
            if weight:
                fine[at, (k + step) % 40] = weight

    for column in range(129):
        fill(column, column)
    fill(135, -1)
    return np.concatenate([fine, fine], axis=1)


ROW_WEIGHTS = ((0.375, 0.625, -1), (0.125, 0.875, -1), (0.875, 0.125, 0), (0.625, 0.375, 0))


def lift_kernel(
    place_ref, field_ref, context_ref, rows_a_ref, rows_b_ref, cols_a_ref, cols_b_ref, up_ref,
    ctxw_ref, gains_ref, expand_ref, depth_ref, reduce_ref, lifted_ref, active_ref, sum_ref,
    lift, ctx, coarse, hid, expand3, total,
):
    step = pl.program_id(0)
    sublane = lax.broadcasted_iota(jnp.int32, (8, 128), 0)
    first_row, last_row = sublane == 0, sublane == 7

    @pl.when(step == 0)
    def _():
        expand3[...] = stack_rows(gained(0.5 * expand_ref[...], gains_ref[0:1]))
        total[...] = jnp.zeros_like(total)
        lift[1:33, :128] = field_ref[...]
        ctx[1:9, :32] = context_ref[...]

        def take_rows(above_ref, below_ref):
            lift[0, :128] = above_ref[:128]
            lift[33, :128] = below_ref[:128]
            ctx[0, :32] = above_ref[128:]
            ctx[9, :32] = below_ref[128:]

        def take_columns(before_ref, after_ref):
            zero = jnp.zeros((8, 128), F32)
            for e in range(44):
                after = jnp.broadcast_to(after_ref[e : e + 1], (8, 128))
                before = jnp.broadcast_to(before_ref[e : e + 1], (8, 128))
                group = jnp.where(first_row, after, jnp.where(last_row, before, zero))
                if e < 34:
                    lift[e, 128:] = group
                else:
                    ctx[e - 34, 32:] = group

        pl.when(place_ref[0] % 2 == 0)(lambda: take_rows(rows_b_ref, rows_a_ref))
        pl.when(place_ref[0] % 2 == 1)(lambda: take_rows(rows_a_ref, rows_b_ref))
        pl.when(place_ref[1] % 2 == 0)(lambda: take_columns(cols_b_ref, cols_a_ref))
        pl.when(place_ref[1] % 2 == 1)(lambda: take_columns(cols_a_ref, cols_b_ref))
        weight = stack_rows(ctxw_ref[...])
        projected = dot(three(ctx[...].reshape(400, CHANNELS)), weight)
        for k in range(10):
            high, low = split(projected[40 * k : 40 * k + 40])
            coarse[k] = dot(up_ref[...], rows_of([high, low]))

    has_after = jnp.where(place_ref[1] < 7, 1.0, 0.0)
    has_before = jnp.where(place_ref[1] > 0, 1.0, 0.0)
    inside = jnp.where(first_row, has_after, has_before)

    def hidden_rows(first, fine_first, k_first, count):
        parts = []
        for i in range(0, count, 2):
            two = []
            for j in (i, i + 1):
                k, o = (fine_first + j) // 4, (fine_first + j) % 4
                lower, upper, shift = ROW_WEIGHTS[o]
                at = k_first + k + shift
                x = lift[first + j] + (lower * coarse[at] + upper * coarse[at + 1])
                lift[first + j] = x
                two.append(x)
            parts.append(three(normed(rows_of(two))))
        made = dot(rows_of(parts), expand3[...])
        for i in range(count):
            for c in range(0, EXPANDED, 128):
                out = gelu_of_half(made[i * WIDE : (i + 1) * WIDE, c : c + 128])
                hid[first + i, :128, c : c + 128] = out[:128]
                hid[first + i, 128:, c : c + 128] = out[128:] * inside

    @pl.when(step == 0)
    def _():
        hidden_rows(0, -1, 1, 2)

        @pl.when(place_ref[0] == 0)
        def _():
            hid[0] = jnp.zeros((WIDE, EXPANDED), F32)

    hidden_rows(8 * step + 2, 1, 2 * step + 1, 4)
    hidden_rows(8 * step + 6, 5, 2 * step + 1, 4)

    @pl.when((step == 3) & (place_ref[0] == 15))
    def _():
        hid[33] = jnp.zeros((WIDE, EXPANDED), F32)

    lifted_ref[...] = lift[pl.ds(8 * step + 1, 8), :128]

    for part in range(EXPANDED // 128):
        lanes = slice(part * 128, (part + 1) * 128)
        taps = [
            [jnp.broadcast_to(0.5 * depth_ref[i, j : j + 1, lanes], (8, 128)) for j in range(3)]
            for i in range(3)
        ]

        def row(r, summed):
            def columns(g):
                seen = [hid[8 * step + r + i, 8 * g : 8 * g + 8, lanes] for i in range(3)]
                a, b, c = (
                    seen[0] * taps[0][j] + seen[1] * taps[1][j] + seen[2] * taps[2][j]
                    for j in range(3)
                )
                return pltpu.roll(a, 1, 0), b, pltpu.roll(c, 7, 0)

            halo = columns(16)
            held, here = halo[0], columns(0)
            for g in range(16):
                following = columns(g + 1) if g < 15 else halo
                out = gelu_of_half(
                    here[1]
                    + jnp.where(first_row, held, here[0])
                    + jnp.where(last_row, following[2], here[2])
                )
                active_ref[r, 8 * g : 8 * g + 8, lanes] = out
                summed = summed + out
                held, here = here[0], following
            return summed

        summed = total[:, lanes]
        for r in range(8):
            summed = row(r, summed)
        total[:, lanes] = summed

    @pl.when(step == 3)
    def _():
        squeezed = lax.dot_general(
            total[...], reduce_ref[...], (((1,), (1,)), ((), ())), precision=HIGHEST,
            preferred_element_type=F32,
        )
        squeezed = jnp.sum(squeezed, axis=0, keepdims=True)
        padded = lanes_of([squeezed, jnp.zeros((1, 128 - SQUEEZE), F32)])
        sum_ref[...] = jnp.broadcast_to(padded, sum_ref.shape)


def whole(shape):
    return pl.BlockSpec(shape, lambda *_: (0,) * len(shape))


def of_layer(array, layer):
    shape = (1,) + array.shape[1:]
    return pl.BlockSpec(shape, lambda *_: (layer,) + (0,) * (len(shape) - 1))


def lift_stage(place, args, copies):
    up = jnp.asarray(column_weights(), BF16)
    args = args[:6] + (up,) + args[6:]
    return pl.pallas_call(
        lift_kernel,
        grid=(4,),
        in_specs=[pl.BlockSpec(memory_space=pltpu.SMEM)] + [whole(a.shape) for a in args],
        out_specs=[
            pl.BlockSpec((8, 128, CHANNELS), lambda s: (s, 0, 0)),
            pl.BlockSpec((8, 128, EXPANDED), lambda s: (s, 0, 0)),
            whole((copies, 128)),
        ],
        out_shape=[
            jax.ShapeDtypeStruct((32, 128, CHANNELS), F32),
            jax.ShapeDtypeStruct((32, 128, EXPANDED), F32),
            jax.ShapeDtypeStruct((copies, 128), F32),
        ],
        scratch_shapes=[
            pltpu.VMEM((34, WIDE, CHANNELS), F32),
            pltpu.VMEM((10, 40, CHANNELS), F32),
            pltpu.VMEM((10, WIDE, CHANNELS), F32),
            pltpu.VMEM((34, WIDE, EXPANDED), F32),
            pltpu.VMEM((3 * CHANNELS, EXPANDED), BF16),
            pltpu.VMEM((8, EXPANDED), F32),
        ],
        compiler_params=pltpu.CompilerParams(vmem_limit_bytes=VMEM_LIMIT),
        cost_estimate=pl.CostEstimate(
            flops=8_000_000_000, bytes_accessed=14_000_000, transcendentals=0
        ),
    )(place, *args)


def block_kernel(
    cells_total, fed, lifted_ref, active_ref, sums_ref, sexp_ref, project_ref, gains_ref, qkv_ref,
    aout_ref, min_ref, mout_ref, out_ref, project, k3, qv3, out3, *feed_weights,
):
    @pl.when(pl.program_id(0) == 0)
    def _():
        pooled = jnp.sum(sums_ref[...], axis=0, keepdims=True) * (1.0 / cells_total)
        squeezed = pooled[:, :SQUEEZE]
        squeezed = squeezed * jax.nn.sigmoid(squeezed)
        wide = jnp.broadcast_to(squeezed, (CHANNELS, SQUEEZE))
        gate = jnp.dot(wide, sexp_ref[...], precision=HIGHEST, preferred_element_type=F32)
        project[...] = deep_weight(project_ref[...] * jax.nn.sigmoid(gate).T)
        prepare_attention(qkv_ref, aout_ref, gains_ref[1:2], k3, qv3, out3)
        if fed:
            prepare_feed(min_ref, mout_ref, gains_ref[2:3], *feed_weights)

    def projected(start):
        highs, lows = [], []
        for w in range(start, start + PART // CELLS):
            cells = active_ref[:, 8 * w : 8 * w + 8, :].reshape(CELLS, EXPANDED)
            high, low = split(cells)
            highs.append(high)
            lows.append(low)
        yield
        wide = dot(rows_of(highs), project[...])
        rest = dot(rows_of(lows), project[:, :CHANNELS])
        yield
        pairs = []
        for p in range(PART // PAIR):
            at = slice(p * PAIR, (p + 1) * PAIR)
            x = rows_of(
                [
                    lifted_ref[:, 8 * w : 8 * w + 8, :].reshape(CELLS, CHANNELS)
                    for w in (start + 2 * p, start + 2 * p + 1)
                ]
            )
            pairs.append(x + (wide[at, :CHANNELS] + (wide[at, CHANNELS:] + rest[at])))
        return pairs

    def group(part):
        pairs = yield from projected(part * PART // CELLS)
        pairs = yield from attend(pairs, k3, qv3, out3)
        if fed:
            pairs = yield from feed(pairs, *feed_weights)
        for p, x in enumerate(pairs):
            out_ref[part * PART + p * PAIR : part * PART + (p + 1) * PAIR] = x

    staggered(group(part) for part in range(BLOCK_STEP // PART))


ATTENTION_SCRATCH = [
    pltpu.VMEM((3 * CHANNELS, CHANNELS), BF16),
    pltpu.VMEM((2 * CHANNELS, 3 * CHANNELS), BF16),
    pltpu.VMEM((3 * CHANNELS, CHANNELS), BF16),
]
FEED_SCRATCH = [
    pltpu.VMEM((3 * CHANNELS, MLP_HIDDEN), BF16),
    pltpu.VMEM((MLP_HIDDEN, 2 * CHANNELS), BF16),
]


def block_stage(chunk, fed, lifted, active, sums, se_expand, project, gains, weights, cells_total):
    per_row = 128 // (BLOCK_STEP // 8)
    steps = 4 // CHUNKS * per_row
    row_base = chunk * (4 // CHUNKS)
    rest = (sums, se_expand, project, gains)

    def strip(channels):
        return pl.BlockSpec(
            (8, BLOCK_STEP // 8, channels), lambda s: (row_base + s // per_row, s % per_row, 0)
        )

    def body(*refs):
        block_kernel(cells_total, fed, *refs)

    return pl.pallas_call(
        body,
        grid=(steps,),
        in_specs=[strip(CHANNELS), strip(EXPANDED)]
        + [whole(a.shape) for a in rest]
        + [of_layer(w, 0) for w in weights],
        out_specs=pl.BlockSpec((BLOCK_STEP, CHANNELS), lambda s: (s, 0)),
        out_shape=jax.ShapeDtypeStruct((steps * BLOCK_STEP, CHANNELS), F32),
        scratch_shapes=[pltpu.VMEM((EXPANDED, 2 * CHANNELS), BF16)]
        + ATTENTION_SCRATCH
        + (FEED_SCRATCH if fed else []),
        compiler_params=pltpu.CompilerParams(vmem_limit_bytes=VMEM_LIMIT),
        cost_estimate=pl.CostEstimate(
            flops=14_000_000_000, bytes_accessed=8_000_000, transcendentals=0
        ),
    )(lifted, active, *rest, *weights)


def grid_kernel(fed, x_ref, gains_ref, *refs):
    scratch = 5 if fed else 7
    out_ref, k3, qv3, out3, *feeds = refs[-scratch - 1 :]
    qkv_ref, aout_ref, *feed_refs = refs[: 4 if fed else 6]

    @pl.when(pl.program_id(0) == 0)
    def _():
        prepare_attention(qkv_ref, aout_ref, gains_ref[3:4], k3, qv3, out3)
        prepare_feed(*feed_refs[:2], gains_ref[4:5], *feeds[:2])
        if not fed:
            prepare_feed(*feed_refs[2:], gains_ref[2:3], *feeds[2:])

    stride = GRID_STEP // GROUP
    flat_in = x_ref.reshape(GRID_STEP, CHANNELS)
    flat_out = out_ref.reshape(GRID_STEP, CHANNELS)

    def group(part):
        first = part * PART // GROUP
        windows = [flat_in[pl.ds(first + p, GROUP, stride=stride), :] for p in range(PART // GROUP)]
        pairs = [rows_of(windows[i : i + 2]) for i in range(0, len(windows), 2)]
        if not fed:
            pairs = yield from feed(pairs, *feeds[2:])
        pairs = yield from attend(pairs, k3, qv3, out3)
        pairs = yield from feed(pairs, *feeds[:2])
        for p, x in enumerate(pairs):
            for i in range(2):
                window = first + 2 * p + i
                flat_out[pl.ds(window, GROUP, stride=stride), :] = x[i * GROUP : (i + 1) * GROUP]

    staggered(group(part) for part in range(GRID_STEP // PART))


def grid_stage(received, fed, gains, weights, chunk, earlier):
    per_device = received.shape[1]
    steps = per_device * GROUP // GRID_STEP
    shape = (GROUP, GRID_STEP // GROUP, CHANNELS)
    in_specs = [pl.BlockSpec(shape, lambda s: (0, s, 0)), whole(gains.shape)]
    in_specs += [of_layer(w, 1) for w in weights]
    args = (received, gains) + weights
    if not fed:
        in_specs += [of_layer(w, 0) for w in weights[2:]]
        args += weights[2:]
    aliases = {}
    if earlier is not None:
        in_specs.append(pl.BlockSpec(memory_space=pl.ANY))
        aliases = {len(args): 0}
        args += (earlier,)

    def body(*refs):
        grid_kernel(fed, *refs)

    return pl.pallas_call(
        body,
        grid=(steps,),
        in_specs=in_specs,
        out_specs=pl.BlockSpec(shape, lambda s: (0, chunk * steps + s, 0)),
        out_shape=jax.ShapeDtypeStruct((GROUP, CHUNKS * per_device, CHANNELS), F32),
        scratch_shapes=ATTENTION_SCRATCH + FEED_SCRATCH + ([] if fed else FEED_SCRATCH),
        input_output_aliases=aliases,
        compiler_params=pltpu.CompilerParams(vmem_limit_bytes=VMEM_LIMIT),
        cost_estimate=pl.CostEstimate(
            flops=14_000_000_000, bytes_accessed=4_000_000, transcendentals=0
        ),
    )(*args)


def by_pairs(edge, at, axis, count):
    even = at % 2 == 0
    swaps = []
    for first, last in ((0, even), (1, jnp.logical_not(even))):
        lower = [(i, i + 1) for i in range(first, count - 1, 2)]
        pairs = lower + [(b, a) for a, b in lower]
        swaps.append(lax.ppermute(edge(last), axis, pairs))
    return swaps


def per_device(
    field, context, ctx_weight, norm_gains, expand_weight, depth_weight, se_reduce, se_expand,
    project_weight, attn_qkv, attn_out, mlp_in, mlp_out,
):
    row_axis = ("rg", "core")
    rows, cols = 16, 8
    row = lax.axis_index(row_axis)
    col = lax.axis_index("col")

    def row_edge(last):
        fine = lax.dynamic_index_in_dim(field, jnp.where(last, 31, 0), 0, keepdims=False)
        of_context = lax.dynamic_index_in_dim(context, jnp.where(last, 7, 0), 0, keepdims=False)
        return jnp.concatenate([fine, of_context], axis=0)

    rows_a, rows_b = by_pairs(row_edge, row, row_axis, rows)
    odd = row % 2 == 1

    def column_edge(last):
        fine_at, coarse_at = jnp.where(last, 127, 0), jnp.where(last, 31, 0)

        def one(x, at):
            return lax.dynamic_slice_in_dim(x, at, 1, axis=x.ndim - 2).reshape(-1, CHANNELS)

        parts = []
        for start, stop, tile, at in ((0, 128, field, fine_at), (128, 160, context, coarse_at)):
            of_a, of_b = one(rows_a[start:stop], at), one(rows_b[start:stop], at)
            parts += [jnp.where(odd, of_a, of_b), one(tile, at), jnp.where(odd, of_b, of_a)]
        return jnp.concatenate(parts, axis=0)

    cols_a, cols_b = by_pairs(column_edge, col, "col", cols)
    place = jnp.stack([row, col]).astype(jnp.int32)
    lifted, active, partial = lift_stage(
        place,
        (
            field, context, rows_a, rows_b, cols_a, cols_b, ctx_weight, norm_gains, expand_weight,
            depth_weight, se_reduce.T,
        ),
        rows * cols,
    )

    def exchange(x, axes):
        return lax.all_to_all(x, axes, split_axis=0, concat_axis=0, tiled=True)

    sums = exchange(partial[:, None, :], ("rg", "core", "col"))[:, 0, :]

    weights = (attn_qkv, attn_out, mlp_in, mlp_out)
    cells_total = rows * cols * field.shape[0] * field.shape[1]
    group = ("rg", "col")
    sent = []
    for chunk in range(CHUNKS):
        mine = block_stage(
            chunk, chunk > 0, lifted, active, sums, se_expand, project_weight, norm_gains, weights,
            cells_total,
        )
        sent.append(exchange(mine.reshape(GROUP, -1, CHANNELS), group))
    attended = None
    for chunk in range(CHUNKS):
        attended = grid_stage(sent[chunk], chunk > 0, norm_gains, weights, chunk, attended)
    back = exchange(attended, group)
    halves = back.reshape(4 // CHUNKS, 16, 2, CHUNKS, WINDOW // 2, WINDOW, CHANNELS)
    return halves.transpose(3, 0, 2, 4, 1, 5, 6).reshape(field.shape)


def solution(mesh):
    fine = Mesh(mesh.devices.reshape(8, 2, 8), ("rg", "core", "col"))
    tiled = P(("rg", "core"), "col", None)
    return jax.shard_map(
        per_device,
        mesh=fine,
        in_specs=(tiled, tiled) + (P(),) * 11,
        out_specs=tiled,
        check_vma=False,
    )
```

```python
import math

import jax
import jax.numpy as jnp
import numpy as np
from jax import lax
from jax.experimental import pallas as pl
from jax.experimental.pallas import tpu as pltpu
from jax.sharding import Mesh
from jax.sharding import PartitionSpec as P

HEADS = 4
WINDOW = 8
CHANNELS = 128
EXPANDED = 512
MLP_HIDDEN = 512
SQUEEZE = 32
HEAD_DIM = CHANNELS // HEADS
CELLS = WINDOW * WINDOW
GROUP = 64
WIDE = 136
EPSILON = 1e-05
F32 = jnp.float32
BF16 = jnp.bfloat16
HIGHEST = lax.Precision.HIGHEST
CHUNKS = 2
BLOCK_STEP = 1024
GRID_STEP = 2048
LIFT_VMEM = 32 * 1024 * 1024
VMEM_LIMIT = 24 * 1024 * 1024

GELU_A = 2.0 * math.sqrt(2.0 / math.pi)
GELU_B = 4.0 * GELU_A * 0.044715


def gelu_of_half(half):
    return half * jnp.tanh(half * (GELU_A + GELU_B * (half * half))) + half


def split(x):
    high = x.astype(BF16)
    low = (x - high.astype(F32)).astype(BF16)
    return high, low


def dot(a, b):
    return jnp.dot(a, b, preferred_element_type=F32)


def rows_of(parts):
    return jnp.concatenate(parts, axis=0)


def lanes_of(parts):
    return jnp.concatenate(parts, axis=1)


def normed(x):
    shifted = x - jnp.mean(x, axis=-1, keepdims=True)
    spread = jnp.sum(shifted * shifted, axis=-1, keepdims=True)
    return shifted * lax.rsqrt(spread + CHANNELS * EPSILON)


def gained(weight, gain):
    column = jnp.broadcast_to(gain * math.sqrt(CHANNELS), (CHANNELS, CHANNELS)).T
    return lanes_of([weight[:, c : c + 128] * column for c in range(0, weight.shape[1], 128)])


def three(x):
    high, low = split(x)
    return lanes_of([high, low, high])


def stack_rows(weight):
    high, low = split(weight)
    return rows_of([high, high, low])


def deep_weight(weight):
    return lanes_of(split(weight))


def prepare_attention(qkv_ref, out_ref, gain, k3, qv3, out3):
    scale = math.log2(math.e) / math.sqrt(HEAD_DIM)
    k3[...] = stack_rows(gained(qkv_ref[0, :, CHANNELS : 2 * CHANNELS], gain))
    row_gain = gain * math.sqrt(CHANNELS)
    queries = qkv_ref[0, :, :CHANNELS].T * (row_gain * scale)
    values = qkv_ref[0, :, 2 * CHANNELS :].T * row_gain
    high, low = split(rows_of([queries, values]))
    qv3[...] = lanes_of([high, high, low])
    out3[...] = stack_rows(out_ref[0])


def prepare_feed(in_ref, mlp_ref, gain, in3, mlp_pair):
    in3[...] = stack_rows(gained(0.5 * in_ref[0], gain))
    mlp_pair[...] = deep_weight(mlp_ref[0])


PAIR = 2 * CELLS
PART = 512


def attend(pairs, k3, qv3, out3):
    left = lax.broadcasted_iota(jnp.int32, (HEAD_DIM, PAIR), 1) < CELLS
    left_all = lax.broadcasted_iota(jnp.int32, (CHANNELS, PAIR), 1) < CELLS
    zero = jnp.zeros((HEAD_DIM, PAIR), BF16)
    zero_block = jnp.zeros((2 * HEAD_DIM, PAIR), BF16)
    natural, turned = [], []
    for x in pairs:
        high, low = split(normed(x))
        natural.append(lanes_of([high, low, high]))
        high, low = high.T, low.T
        turned.append(rows_of([high, low, high]))
    yield
    keys = dot(rows_of(natural), k3[...])
    both = dot(qv3[...], lanes_of(turned))
    yield
    sides, value_sides = [], []

    def by_heads(straight, swapped):
        blocks = []
        for group in range(2):
            at = [slice(h * HEAD_DIM, (h + 1) * HEAD_DIM) for h in (2 * group, 2 * group + 1)]
            block = rows_of(
                [jnp.where(left, straight[at[0]], zero), jnp.where(left, zero, swapped[at[1]])]
            )
            blocks.append(lanes_of([zero_block, block] if group else [block, zero_block]))
        return rows_of(blocks)

    for p in range(len(pairs)):
        at = slice(p * PAIR, (p + 1) * PAIR)
        key3 = three(keys[at])
        high, low = split(both[:CHANNELS, at])
        high_swapped, low_swapped = pltpu.roll(high, CELLS, 1), pltpu.roll(low, CELLS, 1)
        for second in range(2):
            if second:
                h, l = by_heads(high_swapped, high), by_heads(low_swapped, low)
            else:
                h, l = by_heads(high, high_swapped), by_heads(low, low_swapped)
            sides.append((key3[second * CELLS : (second + 1) * CELLS], rows_of([h, h, l])))
        high, low = split(both[CHANNELS:, at])
        low = pltpu.roll(low, CELLS, 1)
        first, second = jnp.where(left_all, high, low), jnp.where(left_all, low, high)
        value_sides += [lanes_of([first, first]), lanes_of([second, second])]
    yield
    scores = [dot(key, query) for key, query in sides]
    yield
    weights, scales = [], []
    for score in scores:
        weight = jnp.exp2(score - jnp.max(score, axis=0, keepdims=True))
        scales.append(1.0 / jnp.sum(weight, axis=0, keepdims=True))
        high, low = split(weight)
        weights.append(rows_of([high, high, low, low]))
    yield
    mixed = [
        [dot(value[64 * g : 64 * g + 64], weight[:, 128 * g : 128 * g + 128]) for g in range(2)]
        for value, weight in zip(value_sides, weights)
    ]
    yield
    blended = []
    for p in range(len(pairs)):
        parts = []
        for h in range(HEADS):
            lanes = slice(128 * (h // 2), 128 * (h // 2) + 128)
            at = slice((h % 2) * HEAD_DIM, (h % 2 + 1) * HEAD_DIM)
            of_a, of_b = (
                mixed[2 * p + i][h // 2][at] * scales[2 * p + i][:, lanes] for i in range(2)
            )
            if h % 2:
                of_a = pltpu.roll(of_a, CELLS, 1)
            else:
                of_b = pltpu.roll(of_b, CELLS, 1)
            parts.append(jnp.where(left, of_a, of_b))
        blended.append(three(rows_of(parts).T))
    yield
    added = dot(rows_of(blended), out3[...])
    yield
    return [x + added[p * PAIR : (p + 1) * PAIR] for p, x in enumerate(pairs)]


def feed(pairs, in3, mlp_pair):
    parts = [three(normed(x)) for x in pairs]
    yield
    inner = dot(rows_of(parts), in3[...])
    yield
    high, low = split_blocks(inner, 64, gelu_of_half)
    yield
    wide = dot(high, mlp_pair[...])
    rest = dot(low, mlp_pair[:, :CHANNELS])
    yield
    out = []
    for p, x in enumerate(pairs):
        at = slice(p * PAIR, (p + 1) * PAIR)
        out.append(x + (wide[at, :CHANNELS] + (wide[at, CHANNELS:] + rest[at])))
    return out


def staggered(groups):
    waiting, running = list(groups), []
    while waiting or running:
        if waiting:
            running.append(waiting.pop(0))
        for group in list(running):
            try:
                next(group)
            except StopIteration:
                running.remove(group)


def split_blocks(x, rows, make):
    highs, lows = [], []
    for r in range(0, x.shape[0], rows):
        made = [split(make(x[r : r + rows, c : c + 128])) for c in range(0, x.shape[1], 128)]
        highs.append(lanes_of([m[0] for m in made]))
        lows.append(lanes_of([m[1] for m in made]))
    return rows_of(highs), rows_of(lows)


def column_weights():
    fine = np.zeros((WIDE, 40), np.float32)
    table = ((0.375, 0.625, 0.0), (0.125, 0.875, 0.0), (0.0, 0.875, 0.125), (0.0, 0.625, 0.375))

    def fill(at, column):
        k, o = column // 4, column % 4
        for step, weight in zip((-1, 0, 1), table[o]):
            if weight:
                fine[at, (k + step) % 40] = weight

    for column in range(128):
        fill(8 * (column % 16) + column // 16, column)
    fill(128, -1)
    fill(135, 128)
    return np.concatenate([fine, fine], axis=1)


ROW_WEIGHTS = ((0.375, 0.625, -1), (0.125, 0.875, -1), (0.875, 0.125, 0), (0.625, 0.375, 0))


def lift_kernel(
    place_ref, field_ref, context_ref, rows_a_ref, rows_b_ref, cols_a_ref, cols_b_ref, up_ref,
    ctxw_ref, gains_ref, expand_ref, depth_ref, reduce_ref, lifted_ref, active_ref, sum_ref,
    lift, ctx, coarse, hid, expand3, total,
):
    step = pl.program_id(0)
    sublane = lax.broadcasted_iota(jnp.int32, (8, 128), 0)
    first_row, last_row = sublane == 0, sublane == 7

    @pl.when(step == 0)
    def _():
        expand3[...] = stack_rows(gained(0.5 * expand_ref[...], gains_ref[0:1]))
        total[...] = jnp.zeros_like(total)
        for t in range(16):
            lift[1:33, 8 * t : 8 * t + 8] = field_ref[:, pl.ds(t, 8, stride=16), :]
        ctx[1:9, :32] = context_ref[...]

        def take_rows(above_ref, below_ref):
            for t in range(16):
                lift[0, 8 * t : 8 * t + 8] = above_ref[pl.ds(t, 8, stride=16), :]
                lift[33, 8 * t : 8 * t + 8] = below_ref[pl.ds(t, 8, stride=16), :]
            ctx[0, :32] = above_ref[128:]
            ctx[9, :32] = below_ref[128:]

        def take_columns(before_ref, after_ref):
            zero = jnp.zeros((8, 128), F32)
            for e in range(44):
                after = jnp.broadcast_to(after_ref[e : e + 1], (8, 128))
                before = jnp.broadcast_to(before_ref[e : e + 1], (8, 128))
                if e < 34:
                    lift[e, 128:] = jnp.where(first_row, before, jnp.where(last_row, after, zero))
                else:
                    ctx[e - 34, 32:] = jnp.where(first_row, after, jnp.where(last_row, before, zero))

        pl.when(place_ref[0] % 2 == 0)(lambda: take_rows(rows_b_ref, rows_a_ref))
        pl.when(place_ref[0] % 2 == 1)(lambda: take_rows(rows_a_ref, rows_b_ref))
        pl.when(place_ref[1] % 2 == 0)(lambda: take_columns(cols_b_ref, cols_a_ref))
        pl.when(place_ref[1] % 2 == 1)(lambda: take_columns(cols_a_ref, cols_b_ref))
        weight = stack_rows(ctxw_ref[...])
        projected = dot(three(ctx[...].reshape(400, CHANNELS)), weight)
        for k in range(10):
            high, low = split(projected[40 * k : 40 * k + 40])
            coarse[k] = dot(up_ref[...], rows_of([high, low]))

    has_after = jnp.where(place_ref[1] < 7, 1.0, 0.0)
    has_before = jnp.where(place_ref[1] > 0, 1.0, 0.0)
    inside = jnp.where(first_row, has_before, has_after)

    def hidden_rows(first, fine_first, k_first, count):
        parts = []
        for i in range(0, count, 2):
            two = []
            for j in (i, i + 1):
                k, o = (fine_first + j) // 4, (fine_first + j) % 4
                lower, upper, shift = ROW_WEIGHTS[o]
                at = k_first + k + shift
                x = lift[first + j] + (lower * coarse[at] + upper * coarse[at + 1])
                lift[first + j] = x
                two.append(x)
            parts.append(three(normed(rows_of(two))))
        made = dot(rows_of(parts), expand3[...])
        for i in range(count):
            for c in range(0, EXPANDED, 128):
                out = gelu_of_half(made[i * WIDE : (i + 1) * WIDE, c : c + 128])
                hid[first + i, :128, c : c + 128] = out[:128]
                hid[first + i, 128:, c : c + 128] = out[128:] * inside

    @pl.when(step == 0)
    def _():
        hidden_rows(0, -1, 1, 2)

        @pl.when(place_ref[0] == 0)
        def _():
            hid[0] = jnp.zeros((WIDE, EXPANDED), F32)

    hidden_rows(8 * step + 2, 1, 2 * step + 1, 4)
    hidden_rows(8 * step + 6, 5, 2 * step + 1, 4)

    @pl.when((step == 3) & (place_ref[0] == 15))
    def _():
        hid[33] = jnp.zeros((WIDE, EXPANDED), F32)

    for t in range(16):
        lifted_ref[:, pl.ds(t, 8, stride=16), :] = lift[pl.ds(8 * step + 1, 8), 8 * t : 8 * t + 8]

    for part in range(EXPANDED // 128):
        lanes = slice(part * 128, (part + 1) * 128)
        taps = [
            [jnp.broadcast_to(0.5 * depth_ref[i, j : j + 1, lanes], (8, 128)) for j in range(3)]
            for i in range(3)
        ]

        def row(r, summed):
            def column(t):
                seen = [hid[8 * step + r + i, 8 * t : 8 * t + 8, lanes] for i in range(3)]
                return [
                    seen[0] * taps[0][j] + seen[1] * taps[1][j] + seen[2] * taps[2][j]
                    for j in range(3)
                ]

            first, last, halo = column(0), column(15), column(16)
            before = jnp.where(first_row, halo[0], pltpu.roll(last[0], 1, 0))
            end = jnp.where(last_row, halo[2], pltpu.roll(first[2], 7, 0))
            here = first
            for t in range(16):
                following = column(t + 1) if t < 14 else last
                out = gelu_of_half(here[1] + before + (following[2] if t < 15 else end))
                active_ref[r, part, pl.ds(t, 8, stride=16), :] = out
                summed = summed + out
                before, here = here[0], following
            return summed

        summed = total[:, lanes]
        for r in range(8):
            summed = row(r, summed)
        total[:, lanes] = summed

    @pl.when(step == 3)
    def _():
        squeezed = lax.dot_general(
            total[...], reduce_ref[...], (((1,), (1,)), ((), ())), precision=HIGHEST,
            preferred_element_type=F32,
        )
        squeezed = jnp.sum(squeezed, axis=0, keepdims=True)
        padded = lanes_of([squeezed, jnp.zeros((1, 128 - SQUEEZE), F32)])
        sum_ref[...] = jnp.broadcast_to(padded, sum_ref.shape)


def whole(shape):
    return pl.BlockSpec(shape, lambda *_: (0,) * len(shape))


def of_layer(array, layer):
    shape = (1,) + array.shape[1:]
    return pl.BlockSpec(shape, lambda *_: (layer,) + (0,) * (len(shape) - 1))


def lift_stage(place, args, copies):
    up = jnp.asarray(column_weights(), BF16)
    args = args[:6] + (up,) + args[6:]
    return pl.pallas_call(
        lift_kernel,
        grid=(4,),
        in_specs=[pl.BlockSpec(memory_space=pltpu.SMEM)] + [whole(a.shape) for a in args],
        out_specs=[
            pl.BlockSpec((8, 128, CHANNELS), lambda s: (s, 0, 0)),
            pl.BlockSpec((8, EXPANDED // 128, 128, 128), lambda s: (s, 0, 0, 0)),
            whole((copies, 128)),
        ],
        out_shape=[
            jax.ShapeDtypeStruct((32, 128, CHANNELS), F32),
            jax.ShapeDtypeStruct((32, EXPANDED // 128, 128, 128), F32),
            jax.ShapeDtypeStruct((copies, 128), F32),
        ],
        scratch_shapes=[
            pltpu.VMEM((34, WIDE, CHANNELS), F32),
            pltpu.VMEM((10, 40, CHANNELS), F32),
            pltpu.VMEM((10, WIDE, CHANNELS), F32),
            pltpu.VMEM((34, WIDE, EXPANDED), F32),
            pltpu.VMEM((3 * CHANNELS, EXPANDED), BF16),
            pltpu.VMEM((8, EXPANDED), F32),
        ],
        compiler_params=pltpu.CompilerParams(vmem_limit_bytes=LIFT_VMEM),
        cost_estimate=pl.CostEstimate(
            flops=8_000_000_000, bytes_accessed=14_000_000, transcendentals=0
        ),
    )(place, *args)


def block_kernel(
    cells_total, fed, lifted_ref, active_ref, sums_ref, sexp_ref, project_ref, gains_ref, qkv_ref,
    aout_ref, min_ref, mout_ref, out_ref, project, k3, qv3, out3, *feed_weights,
):
    @pl.when(pl.program_id(0) == 0)
    def _():
        pooled = jnp.sum(sums_ref[...], axis=0, keepdims=True) * (1.0 / cells_total)
        squeezed = pooled[:, :SQUEEZE]
        squeezed = squeezed * jax.nn.sigmoid(squeezed)
        wide = jnp.broadcast_to(squeezed, (CHANNELS, SQUEEZE))
        gate = jnp.dot(wide, sexp_ref[...], precision=HIGHEST, preferred_element_type=F32)
        project[...] = deep_weight(project_ref[...] * jax.nn.sigmoid(gate).T)
        prepare_attention(qkv_ref, aout_ref, gains_ref[1:2], k3, qv3, out3)
        if fed:
            prepare_feed(min_ref, mout_ref, gains_ref[2:3], *feed_weights)

    def projected(start):
        highs, lows = [], []
        for w in range(start, start + PART // CELLS):
            cells = [
                active_ref[:, k, 8 * w : 8 * w + 8, :].reshape(CELLS, 128)
                for k in range(EXPANDED // 128)
            ]
            high, low = split(lanes_of(cells))
            highs.append(high)
            lows.append(low)
        yield
        wide = dot(rows_of(highs), project[...])
        rest = dot(rows_of(lows), project[:, :CHANNELS])
        yield
        pairs = []
        for p in range(PART // PAIR):
            at = slice(p * PAIR, (p + 1) * PAIR)
            x = rows_of(
                [
                    lifted_ref[:, 8 * w : 8 * w + 8, :].reshape(CELLS, CHANNELS)
                    for w in (start + 2 * p, start + 2 * p + 1)
                ]
            )
            pairs.append(x + (wide[at, :CHANNELS] + (wide[at, CHANNELS:] + rest[at])))
        return pairs

    def group(part):
        pairs = yield from projected(part * PART // CELLS)
        pairs = yield from attend(pairs, k3, qv3, out3)
        if fed:
            pairs = yield from feed(pairs, *feed_weights)
        for p, x in enumerate(pairs):
            out_ref[part * PART + p * PAIR : part * PART + (p + 1) * PAIR] = x

    staggered(group(part) for part in range(BLOCK_STEP // PART))


ATTENTION_SCRATCH = [
    pltpu.VMEM((3 * CHANNELS, CHANNELS), BF16),
    pltpu.VMEM((2 * CHANNELS, 3 * CHANNELS), BF16),
    pltpu.VMEM((3 * CHANNELS, CHANNELS), BF16),
]
FEED_SCRATCH = [
    pltpu.VMEM((3 * CHANNELS, MLP_HIDDEN), BF16),
    pltpu.VMEM((MLP_HIDDEN, 2 * CHANNELS), BF16),
]


def block_stage(chunk, fed, lifted, active, sums, se_expand, project, gains, weights, cells_total):
    per_row = 128 // (BLOCK_STEP // 8)
    steps = 4 // CHUNKS * per_row
    row_base = chunk * (4 // CHUNKS)
    rest = (sums, se_expand, project, gains)

    columns = BLOCK_STEP // 8
    strips = [
        pl.BlockSpec((8, columns, CHANNELS), lambda s: (row_base + s // per_row, s % per_row, 0)),
        pl.BlockSpec(
            (8, EXPANDED // 128, columns, 128),
            lambda s: (row_base + s // per_row, 0, s % per_row, 0),
        ),
    ]

    def body(*refs):
        block_kernel(cells_total, fed, *refs)

    return pl.pallas_call(
        body,
        grid=(steps,),
        in_specs=strips
        + [whole(a.shape) for a in rest]
        + [of_layer(w, 0) for w in weights],
        out_specs=pl.BlockSpec((BLOCK_STEP, CHANNELS), lambda s: (s, 0)),
        out_shape=jax.ShapeDtypeStruct((steps * BLOCK_STEP, CHANNELS), F32),
        scratch_shapes=[pltpu.VMEM((EXPANDED, 2 * CHANNELS), BF16)]
        + ATTENTION_SCRATCH
        + (FEED_SCRATCH if fed else []),
        compiler_params=pltpu.CompilerParams(vmem_limit_bytes=VMEM_LIMIT),
        cost_estimate=pl.CostEstimate(
            flops=14_000_000_000, bytes_accessed=8_000_000, transcendentals=0
        ),
    )(lifted, active, *rest, *weights)


def grid_kernel(fed, x_ref, gains_ref, *refs):
    scratch = 5 if fed else 7
    out_ref, k3, qv3, out3, *feeds = refs[-scratch - 1 :]
    qkv_ref, aout_ref, *feed_refs = refs[: 4 if fed else 6]

    @pl.when(pl.program_id(0) == 0)
    def _():
        prepare_attention(qkv_ref, aout_ref, gains_ref[3:4], k3, qv3, out3)
        prepare_feed(*feed_refs[:2], gains_ref[4:5], *feeds[:2])
        if not fed:
            prepare_feed(*feed_refs[2:], gains_ref[2:3], *feeds[2:])

    stride = GRID_STEP // GROUP
    flat_in = x_ref.reshape(GRID_STEP, CHANNELS)
    flat_out = out_ref.reshape(GRID_STEP, CHANNELS)

    def group(part):
        first = part * PART // GROUP
        windows = [flat_in[pl.ds(first + p, GROUP, stride=stride), :] for p in range(PART // GROUP)]
        pairs = [rows_of(windows[i : i + 2]) for i in range(0, len(windows), 2)]
        if not fed:
            pairs = yield from feed(pairs, *feeds[2:])
        pairs = yield from attend(pairs, k3, qv3, out3)
        pairs = yield from feed(pairs, *feeds[:2])
        for p, x in enumerate(pairs):
            for i in range(2):
                window = first + 2 * p + i
                flat_out[pl.ds(window, GROUP, stride=stride), :] = x[i * GROUP : (i + 1) * GROUP]

    staggered(group(part) for part in range(GRID_STEP // PART))


def grid_stage(received, fed, gains, weights, chunk, earlier):
    per_device = received.shape[1]
    steps = per_device * GROUP // GRID_STEP
    shape = (GROUP, GRID_STEP // GROUP, CHANNELS)
    in_specs = [pl.BlockSpec(shape, lambda s: (0, s, 0)), whole(gains.shape)]
    in_specs += [of_layer(w, 1) for w in weights]
    args = (received, gains) + weights
    if not fed:
        in_specs += [of_layer(w, 0) for w in weights[2:]]
        args += weights[2:]
    aliases = {}
    if earlier is not None:
        in_specs.append(pl.BlockSpec(memory_space=pl.ANY))
        aliases = {len(args): 0}
        args += (earlier,)

    def body(*refs):
        grid_kernel(fed, *refs)

    return pl.pallas_call(
        body,
        grid=(steps,),
        in_specs=in_specs,
        out_specs=pl.BlockSpec(shape, lambda s: (0, chunk * steps + s, 0)),
        out_shape=jax.ShapeDtypeStruct((GROUP, CHUNKS * per_device, CHANNELS), F32),
        scratch_shapes=ATTENTION_SCRATCH + FEED_SCRATCH + ([] if fed else FEED_SCRATCH),
        input_output_aliases=aliases,
        compiler_params=pltpu.CompilerParams(vmem_limit_bytes=VMEM_LIMIT),
        cost_estimate=pl.CostEstimate(
            flops=14_000_000_000, bytes_accessed=4_000_000, transcendentals=0
        ),
    )(*args)


def by_pairs(edge, at, axis, count):
    even = at % 2 == 0
    swaps = []
    for first, last in ((0, even), (1, jnp.logical_not(even))):
        lower = [(i, i + 1) for i in range(first, count - 1, 2)]
        pairs = lower + [(b, a) for a, b in lower]
        swaps.append(lax.ppermute(edge(last), axis, pairs))
    return swaps


def per_device(
    field, context, ctx_weight, norm_gains, expand_weight, depth_weight, se_reduce, se_expand,
    project_weight, attn_qkv, attn_out, mlp_in, mlp_out,
):
    row_axis = ("rg", "core")
    rows, cols = 16, 8
    row = lax.axis_index(row_axis)
    col = lax.axis_index("col")

    def row_edge(last):
        fine = lax.dynamic_index_in_dim(field, jnp.where(last, 31, 0), 0, keepdims=False)
        of_context = lax.dynamic_index_in_dim(context, jnp.where(last, 7, 0), 0, keepdims=False)
        return jnp.concatenate([fine, of_context], axis=0)

    rows_a, rows_b = by_pairs(row_edge, row, row_axis, rows)
    odd = row % 2 == 1

    def column_edge(last):
        fine_at, coarse_at = jnp.where(last, 127, 0), jnp.where(last, 31, 0)

        def one(x, at):
            return lax.dynamic_slice_in_dim(x, at, 1, axis=x.ndim - 2).reshape(-1, CHANNELS)

        parts = []
        for start, stop, tile, at in ((0, 128, field, fine_at), (128, 160, context, coarse_at)):
            of_a, of_b = one(rows_a[start:stop], at), one(rows_b[start:stop], at)
            parts += [jnp.where(odd, of_a, of_b), one(tile, at), jnp.where(odd, of_b, of_a)]
        return jnp.concatenate(parts, axis=0)

    cols_a, cols_b = by_pairs(column_edge, col, "col", cols)
    place = jnp.stack([row, col]).astype(jnp.int32)
    lifted, active, partial = lift_stage(
        place,
        (
            field, context, rows_a, rows_b, cols_a, cols_b, ctx_weight, norm_gains, expand_weight,
            depth_weight, se_reduce.T,
        ),
        rows * cols,
    )

    def exchange(x, axes):
        return lax.all_to_all(x, axes, split_axis=0, concat_axis=0, tiled=True)

    sums = exchange(partial[:, None, :], ("rg", "core", "col"))[:, 0, :]

    weights = (attn_qkv, attn_out, mlp_in, mlp_out)
    cells_total = rows * cols * field.shape[0] * field.shape[1]
    group = ("rg", "col")
    sent = []
    for chunk in range(CHUNKS):
        mine = block_stage(
            chunk, chunk > 0, lifted, active, sums, se_expand, project_weight, norm_gains, weights,
            cells_total,
        )
        sent.append(exchange(mine.reshape(GROUP, -1, CHANNELS), group))
    attended = None
    for chunk in range(CHUNKS):
        attended = grid_stage(sent[chunk], chunk > 0, norm_gains, weights, chunk, attended)
    back = exchange(attended, group)
    halves = back.reshape(4 // CHUNKS, 16, 2, CHUNKS, WINDOW // 2, WINDOW, CHANNELS)
    return halves.transpose(3, 0, 2, 4, 1, 5, 6).reshape(field.shape)


def solution(mesh):
    fine = Mesh(mesh.devices.reshape(8, 2, 8), ("rg", "core", "col"))
    tiled = P(("rg", "core"), "col", None)
    return jax.shard_map(
        per_device,
        mesh=fine,
        in_specs=(tiled, tiled) + (P(),) * 11,
        out_specs=tiled,
        check_vma=False,
    )
```

```python
import math

import jax
import jax.numpy as jnp
import numpy as np
from jax import lax
from jax.experimental import pallas as pl
from jax.experimental.pallas import tpu as pltpu
from jax.sharding import Mesh
from jax.sharding import PartitionSpec as P

HEADS = 4
WINDOW = 8
CHANNELS = 128
EXPANDED = 512
MLP_HIDDEN = 512
SQUEEZE = 32
HEAD_DIM = CHANNELS // HEADS
CELLS = WINDOW * WINDOW
GROUP = 64
WIDE = 136
COARSE_WIDE = 48
EPSILON = 1e-05
F32 = jnp.float32
BF16 = jnp.bfloat16
HIGHEST = lax.Precision.HIGHEST
CHUNKS = 2
BLOCK_STEP = 1024
GRID_STEP = 2048
VMEM_LIMIT = 56 * 1024 * 1024

GELU_A = 2.0 * math.sqrt(2.0 / math.pi)
GELU_B = 4.0 * GELU_A * 0.044715


def gelu_of_half(half):
    return half * jnp.tanh(half * (GELU_A + GELU_B * (half * half))) + half


def split(x):
    high = x.astype(BF16)
    low = (x - high.astype(F32)).astype(BF16)
    return high, low


def dot(a, b):
    return jnp.dot(a, b, preferred_element_type=F32)


def rows_of(parts):
    return jnp.concatenate(parts, axis=0)


def lanes_of(parts):
    return jnp.concatenate(parts, axis=1)


def normed(x):
    shifted = x - jnp.mean(x, axis=-1, keepdims=True)
    spread = jnp.sum(shifted * shifted, axis=-1, keepdims=True)
    return shifted * lax.rsqrt(spread + CHANNELS * EPSILON)


def gained(weight, gain):
    column = jnp.broadcast_to(gain * math.sqrt(CHANNELS), (CHANNELS, CHANNELS)).T
    return lanes_of([weight[:, c : c + 128] * column for c in range(0, weight.shape[1], 128)])


def three(x):
    high, low = split(x)
    return lanes_of([high, low, high])


def stack_rows(weight):
    high, low = split(weight)
    return rows_of([high, high, low])


def deep_weight(weight):
    return lanes_of(split(weight))


def prepare_kernel(
    gains_ref, qkv_ref, out_ref, in_ref, mlp_ref, k3, qv3, out3, in3, mlp_pair
):
    scale = math.log2(math.e) / math.sqrt(HEAD_DIM)
    for layer in range(2):
        gain = gains_ref[2 * layer + 1 : 2 * layer + 2]
        k3[layer] = stack_rows(gained(qkv_ref[layer, :, CHANNELS : 2 * CHANNELS], gain))
        row_gain = gain * math.sqrt(CHANNELS)
        queries = qkv_ref[layer, :, :CHANNELS].T * (row_gain * scale)
        values = qkv_ref[layer, :, 2 * CHANNELS :].T * row_gain
        high, low = split(rows_of([queries, values]))
        qv3[layer] = lanes_of([high, high, low])
        out3[layer] = stack_rows(out_ref[layer])
        in3[layer] = stack_rows(gained(0.5 * in_ref[layer], gains_ref[2 * layer + 2 : 2 * layer + 3]))
        mlp_pair[layer] = deep_weight(mlp_ref[layer])


def prepare_stage(*args):
    shapes = [
        (3 * CHANNELS, CHANNELS), (2 * CHANNELS, 3 * CHANNELS), (3 * CHANNELS, CHANNELS),
        (3 * CHANNELS, MLP_HIDDEN), (MLP_HIDDEN, 2 * CHANNELS),
    ]
    return pl.pallas_call(
        prepare_kernel,
        out_shape=[jax.ShapeDtypeStruct((2,) + shape, BF16) for shape in shapes],
        compiler_params=pltpu.CompilerParams(vmem_limit_bytes=VMEM_LIMIT),
        cost_estimate=pl.CostEstimate(
            flops=1_000_000_000, bytes_accessed=4_000_000, transcendentals=0
        ),
    )(*args)


PAIR = 2 * CELLS
PART = 512


def attend(pairs, k3, qv3, out3):
    left = lax.broadcasted_iota(jnp.int32, (HEAD_DIM, PAIR), 1) < CELLS
    left_all = lax.broadcasted_iota(jnp.int32, (CHANNELS, PAIR), 1) < CELLS
    zero = jnp.zeros((HEAD_DIM, PAIR), BF16)
    zero_block = jnp.zeros((2 * HEAD_DIM, PAIR), BF16)
    natural, turned = [], []
    for x in pairs:
        high, low = split(normed(x))
        natural.append(lanes_of([high, low, high]))
        high, low = high.T, low.T
        turned.append(rows_of([high, low, high]))
    yield
    keys = dot(rows_of(natural), k3[...])
    both = dot(qv3[...], lanes_of(turned))
    yield
    sides, value_sides = [], []

    def by_heads(straight, swapped):
        blocks = []
        for group in range(2):
            at = [slice(h * HEAD_DIM, (h + 1) * HEAD_DIM) for h in (2 * group, 2 * group + 1)]
            block = rows_of(
                [jnp.where(left, straight[at[0]], zero), jnp.where(left, zero, swapped[at[1]])]
            )
            blocks.append(lanes_of([zero_block, block] if group else [block, zero_block]))
        return rows_of(blocks)

    for p in range(len(pairs)):
        at = slice(p * PAIR, (p + 1) * PAIR)
        key3 = three(keys[at])
        high, low = split(both[:CHANNELS, at])
        high_swapped, low_swapped = pltpu.roll(high, CELLS, 1), pltpu.roll(low, CELLS, 1)
        for second in range(2):
            if second:
                h, l = by_heads(high_swapped, high), by_heads(low_swapped, low)
            else:
                h, l = by_heads(high, high_swapped), by_heads(low, low_swapped)
            sides.append((key3[second * CELLS : (second + 1) * CELLS], rows_of([h, h, l])))
        high, low = split(both[CHANNELS:, at])
        low = pltpu.roll(low, CELLS, 1)
        first, second = jnp.where(left_all, high, low), jnp.where(left_all, low, high)
        value_sides += [lanes_of([first, first]), lanes_of([second, second])]
    yield
    scores = [dot(key, query) for key, query in sides]
    yield
    weights, scales = [], []
    for score in scores:
        weight = jnp.exp2(score - jnp.max(score, axis=0, keepdims=True))
        scales.append(1.0 / jnp.sum(weight, axis=0, keepdims=True))
        high, low = split(weight)
        weights.append(rows_of([high, high, low, low]))
    yield
    mixed = [
        [dot(value[64 * g : 64 * g + 64], weight[:, 128 * g : 128 * g + 128]) for g in range(2)]
        for value, weight in zip(value_sides, weights)
    ]
    yield
    blended = []
    for p in range(len(pairs)):
        parts = []
        for h in range(HEADS):
            lanes = slice(128 * (h // 2), 128 * (h // 2) + 128)
            at = slice((h % 2) * HEAD_DIM, (h % 2 + 1) * HEAD_DIM)
            of_a, of_b = (
                mixed[2 * p + i][h // 2][at] * scales[2 * p + i][:, lanes] for i in range(2)
            )
            if h % 2:
                of_a = pltpu.roll(of_a, CELLS, 1)
            else:
                of_b = pltpu.roll(of_b, CELLS, 1)
            parts.append(jnp.where(left, of_a, of_b))
        blended.append(three(rows_of(parts).T))
    yield
    added = dot(rows_of(blended), out3[...])
    yield
    return [x + added[p * PAIR : (p + 1) * PAIR] for p, x in enumerate(pairs)]


def feed(pairs, in3, mlp_pair):
    parts = [three(normed(x)) for x in pairs]
    yield
    inner = dot(rows_of(parts), in3[...])
    yield
    high, low = split_blocks(inner, 64, gelu_of_half)
    yield
    wide = dot(high, mlp_pair[...])
    rest = dot(low, mlp_pair[:, :CHANNELS])
    yield
    out = []
    for p, x in enumerate(pairs):
        at = slice(p * PAIR, (p + 1) * PAIR)
        out.append(x + (wide[at, :CHANNELS] + (wide[at, CHANNELS:] + rest[at])))
    return out


def staggered(groups):
    waiting, running = list(groups), []
    while waiting or running:
        if waiting:
            running.append(waiting.pop(0))
        for group in list(running):
            try:
                next(group)
            except StopIteration:
                running.remove(group)


def split_blocks(x, rows, make):
    highs, lows = [], []
    for r in range(0, x.shape[0], rows):
        made = [split(make(x[r : r + rows, c : c + 128])) for c in range(0, x.shape[1], 128)]
        highs.append(lanes_of([m[0] for m in made]))
        lows.append(lanes_of([m[1] for m in made]))
    return rows_of(highs), rows_of(lows)


def column_weights():
    fine = np.zeros((WIDE, COARSE_WIDE), np.float32)
    table = ((0.375, 0.625, 0.0), (0.125, 0.875, 0.0), (0.0, 0.875, 0.125), (0.0, 0.625, 0.375))

    def fill(at, column):
        k, o = column // 4, column % 4
        for step, weight in zip((-1, 0, 1), table[o]):
            if weight:
                fine[at, (k + step) % 40] = weight

    for column in range(129):
        fill(column, column)
    fill(135, -1)
    return np.concatenate([fine, fine], axis=1)


ROW_WEIGHTS = ((0.375, 0.625, -1), (0.125, 0.875, -1), (0.875, 0.125, 0), (0.625, 0.375, 0))


def lift_kernel(
    place_ref, field_ref, context_ref, rows_a_ref, rows_b_ref, cols_a_ref, cols_b_ref, up_ref,
    ctxw_ref, gains_ref, expand_ref, depth_ref, reduce_ref, lifted_hbm, active_hbm, sum_ref,
    lifted, active, ends, sides, ctx, coarse, expand3, hid_top, hid_0, hid_1, hid_2, hid_3, sems,
):
    sublane = lax.broadcasted_iota(jnp.int32, (8, 128), 0)
    first_row, last_row = sublane == 0, sublane == 7
    zero = jnp.zeros((8, 128), F32)

    def take_rows(above_ref, below_ref):
        ends[0] = above_ref[:128]
        ends[1] = below_ref[:128]
        ctx[0, :32] = above_ref[128:]
        ctx[9, :32] = below_ref[128:]

    def take_columns(before_ref, after_ref):
        for e in range(44):
            after = jnp.broadcast_to(after_ref[e : e + 1], (8, 128))
            before = jnp.broadcast_to(before_ref[e : e + 1], (8, 128))
            group = jnp.where(first_row, after, jnp.where(last_row, before, zero))
            if e < 34:
                sides[e] = group
            else:
                ctx[e - 34, 32:40] = group
                ctx[e - 34, 40:] = zero

    pl.when(place_ref[0] % 2 == 0)(lambda: take_rows(rows_b_ref, rows_a_ref))
    pl.when(place_ref[0] % 2 == 1)(lambda: take_rows(rows_a_ref, rows_b_ref))
    pl.when(place_ref[1] % 2 == 0)(lambda: take_columns(cols_b_ref, cols_a_ref))
    pl.when(place_ref[1] % 2 == 1)(lambda: take_columns(cols_a_ref, cols_b_ref))
    ctx[1:9, :32] = context_ref[...]
    expand3[...] = stack_rows(gained(0.5 * expand_ref[...], gains_ref[0:1]))
    weight = stack_rows(ctxw_ref[...])
    projected = dot(three(ctx[...].reshape(10 * COARSE_WIDE, CHANNELS)), weight)
    for k in range(10):
        high, low = split(projected[COARSE_WIDE * k : COARSE_WIDE * (k + 1)])
        coarse[k] = dot(up_ref[...], rows_of([high, low]))

    has_after = jnp.where(place_ref[1] < 7, 1.0, 0.0)
    has_before = jnp.where(place_ref[1] > 0, 1.0, 0.0)
    inside = jnp.where(first_row, has_after, has_before)
    has_end = {
        0: jnp.where(place_ref[0] > 0, 1.0, 0.0),
        33: jnp.where(place_ref[0] < 15, 1.0, 0.0),
    }
    strips = (hid_0, hid_1, hid_2, hid_3)

    def hid(e):
        return hid_top.at[e] if e < 2 else strips[(e - 2) // 8].at[(e - 2) % 8]

    def two_hidden(first):
        rows = []
        for e in (first, first + 1):
            k, o = (e - 1) // 4, (e - 1) % 4
            lower, upper, shift = ROW_WEIGHTS[o]
            up = lower * coarse[k + 1 + shift] + upper * coarse[k + 2 + shift]
            own = ends[0] if e == 0 else ends[1] if e == 33 else field_ref[e - 1]
            x = rows_of([own, sides[e]]) + up
            if 0 < e < 33:
                lifted[e - 1] = x[:128]
            rows.append(x)
        made = dot(three(normed(rows_of(rows))), expand3[...])
        for i, e in enumerate((first, first + 1)):
            for c in range(0, EXPANDED, 128):
                out = gelu_of_half(made[i * WIDE : (i + 1) * WIDE, c : c + 128])
                if e in has_end:
                    out = out * has_end[e]
                hid(e)[:128, c : c + 128] = out[:128]
                hid(e)[128:, c : c + 128] = out[128:] * inside

    taps = [
        [
            [
                jnp.broadcast_to(0.5 * depth_ref[i, j : j + 1, c : c + 128], (8, 128))
                for j in range(3)
            ]
            for i in range(3)
        ]
        for c in range(0, EXPANDED, 128)
    ]

    def depthwise(r, part, summed):
        lanes = slice(part * 128, (part + 1) * 128)
        tap = taps[part]

        def columns(g):
            seen = [hid(r + i)[8 * g : 8 * g + 8, lanes] for i in range(3)]
            a, b, c = (
                seen[0] * tap[0][j] + seen[1] * tap[1][j] + seen[2] * tap[2][j] for j in range(3)
            )
            return pltpu.roll(a, 1, 0), b, pltpu.roll(c, 7, 0)

        halo = columns(16)
        held, here = halo[0], columns(0)
        for g in range(16):
            following = columns(g + 1) if g < 15 else halo
            out = gelu_of_half(
                here[1]
                + jnp.where(first_row, held, here[0])
                + jnp.where(last_row, following[2], here[2])
            )
            active[r, 8 * g : 8 * g + 8, lanes] = out
            summed = summed + out
            held, here = here[0], following
        return summed

    def leave(i):
        at = pl.ds(8 * i, 8)
        return (
            pltpu.make_async_copy(lifted.at[at], lifted_hbm.at[at], sems.at[0, i]),
            pltpu.make_async_copy(active.at[at], active_hbm.at[at], sems.at[1, i]),
        )

    totals = [zero] * 4
    for e in range(0, 10, 2):
        two_hidden(e)
    for i in range(4):
        for j in range(4):
            if i < 3:
                two_hidden(8 * i + 10 + 2 * j)
            for r in (8 * i + 2 * j, 8 * i + 2 * j + 1):
                totals = [depthwise(r, part, totals[part]) for part in range(4)]
        for copy in leave(i):
            copy.start()
    squeezed = lax.dot_general(
        lanes_of(totals), reduce_ref[...], (((1,), (1,)), ((), ())), precision=HIGHEST,
        preferred_element_type=F32,
    )
    squeezed = jnp.sum(squeezed, axis=0, keepdims=True)
    padded = lanes_of([squeezed, jnp.zeros((1, 128 - SQUEEZE), F32)])
    sum_ref[...] = jnp.broadcast_to(padded, sum_ref.shape)
    for i in range(4):
        for copy in leave(i):
            copy.wait()


def whole(shape):
    return pl.BlockSpec(shape, lambda *_: (0,) * len(shape))


def of_layer(array, layer):
    shape = (1,) + array.shape[1:]
    return pl.BlockSpec(shape, lambda *_: (layer,) + (0,) * (len(shape) - 1))


def lift_stage(place, args, copies):
    up = jnp.asarray(column_weights(), BF16)
    args = args[:6] + (up,) + args[6:]
    in_vmem, in_hbm = pl.BlockSpec(memory_space=pltpu.VMEM), pl.BlockSpec(memory_space=pl.ANY)
    strip = pltpu.VMEM((8, WIDE, EXPANDED), F32)
    return pl.pallas_call(
        lift_kernel,
        in_specs=[pl.BlockSpec(memory_space=pltpu.SMEM)] + [in_vmem] * len(args),
        out_specs=[in_hbm, in_hbm, in_vmem],
        out_shape=[
            jax.ShapeDtypeStruct((32, 128, CHANNELS), F32),
            jax.ShapeDtypeStruct((32, 128, EXPANDED), F32),
            jax.ShapeDtypeStruct((copies, 128), F32),
        ],
        scratch_shapes=[
            pltpu.VMEM((32, 128, CHANNELS), F32),
            pltpu.VMEM((32, 128, EXPANDED), F32),
            pltpu.VMEM((2, 128, CHANNELS), F32),
            pltpu.VMEM((34, 8, CHANNELS), F32),
            pltpu.VMEM((10, COARSE_WIDE, CHANNELS), F32),
            pltpu.VMEM((10, WIDE, CHANNELS), F32),
            pltpu.VMEM((3 * CHANNELS, EXPANDED), BF16),
            pltpu.VMEM((2, WIDE, EXPANDED), F32),
            strip,
            strip,
            strip,
            strip,
            pltpu.SemaphoreType.DMA((2, 4)),
        ],
        compiler_params=pltpu.CompilerParams(vmem_limit_bytes=VMEM_LIMIT),
        cost_estimate=pl.CostEstimate(
            flops=8_000_000_000, bytes_accessed=14_000_000, transcendentals=0
        ),
    )(place, *args)


def block_kernel(
    cells_total, lifted_ref, active_ref, sums_ref, sexp_ref, project_ref, k3, qv3, out3, *rest
):
    *feeds, out_ref, project = rest

    @pl.when(pl.program_id(0) == 0)
    def _():
        pooled = jnp.sum(sums_ref[...], axis=0, keepdims=True) * (1.0 / cells_total)
        squeezed = pooled[:, :SQUEEZE]
        squeezed = squeezed * jax.nn.sigmoid(squeezed)
        wide = jnp.broadcast_to(squeezed, (CHANNELS, SQUEEZE))
        gate = jnp.dot(wide, sexp_ref[...], precision=HIGHEST, preferred_element_type=F32)
        project[...] = deep_weight(project_ref[...] * jax.nn.sigmoid(gate).T)

    def window(w):
        rows, columns = divmod(w, 4)
        return slice(8 * rows, 8 * rows + 8), slice(8 * columns, 8 * columns + 8)

    def cells(ref, w):
        rows, columns = window(w)
        return ref[rows, columns, :].reshape(CELLS, ref.shape[2])

    def projected(start):
        halves = [split(cells(active_ref, w)) for w in range(start, start + PART // CELLS)]
        yield
        wide = dot(rows_of([h[0] for h in halves]), project[...])
        rest = dot(rows_of([h[1] for h in halves]), project[:, :CHANNELS])
        yield
        pairs = []
        for p in range(PART // PAIR):
            at = slice(p * PAIR, (p + 1) * PAIR)
            x = rows_of([cells(lifted_ref, start + 2 * p + i) for i in range(2)])
            pairs.append(x + (wide[at, :CHANNELS] + (wide[at, CHANNELS:] + rest[at])))
        return pairs

    def group(part):
        start = part * PART // CELLS
        pairs = yield from projected(start)
        pairs = yield from attend(pairs, k3.at[0], qv3.at[0], out3.at[0])
        if feeds:
            pairs = yield from feed(pairs, feeds[0].at[0], feeds[1].at[0])
        for p, x in enumerate(pairs):
            for i in range(2):
                rows, columns = window(start + 2 * p + i)
                of_one = x[i * CELLS : (i + 1) * CELLS].reshape(WINDOW, WINDOW, CHANNELS)
                out_ref[rows, 0, columns, :] = of_one

    staggered(group(part) for part in range(BLOCK_STEP // PART))


def block_stage(chunk, fed, lifted, active, sums, se_expand, project, weights, cells_total):
    rest = (sums, se_expand, project)
    layer = weights if fed else weights[:3]
    columns = BLOCK_STEP // 32

    def body(*refs):
        block_kernel(cells_total, *refs)

    return pl.pallas_call(
        body,
        grid=(2,),
        in_specs=[
            pl.BlockSpec((32, columns, CHANNELS), lambda s: (0, 2 * s + chunk, 0)),
            pl.BlockSpec((32, columns, EXPANDED), lambda s: (0, 2 * s + chunk, 0)),
        ]
        + [whole(a.shape) for a in rest]
        + [of_layer(w, 0) for w in layer],
        out_specs=pl.BlockSpec((32, 1, columns, CHANNELS), lambda s: (0, s, 0, 0)),
        out_shape=jax.ShapeDtypeStruct((32, 2, columns, CHANNELS), F32),
        scratch_shapes=[pltpu.VMEM((EXPANDED, 2 * CHANNELS), BF16)],
        compiler_params=pltpu.CompilerParams(vmem_limit_bytes=VMEM_LIMIT),
        cost_estimate=pl.CostEstimate(
            flops=14_000_000_000, bytes_accessed=8_000_000, transcendentals=0
        ),
    )(lifted, active, *rest, *layer)


def grid_kernel(fed, x_ref, k3, qv3, out3, in3, mlp_pair, *rest):
    out_ref = rest[-1]
    stride = GRID_STEP // GROUP
    flat_in = x_ref.reshape(GRID_STEP, CHANNELS)
    flat_out = out_ref.reshape(GRID_STEP, CHANNELS)

    def group(part):
        first = part * PART // GROUP
        windows = [flat_in[pl.ds(first + p, GROUP, stride=stride), :] for p in range(PART // GROUP)]
        pairs = [rows_of(windows[i : i + 2]) for i in range(0, len(windows), 2)]
        if not fed:
            pairs = yield from feed(pairs, rest[0].at[0], rest[1].at[0])
        pairs = yield from attend(pairs, k3.at[0], qv3.at[0], out3.at[0])
        pairs = yield from feed(pairs, in3.at[0], mlp_pair.at[0])
        for p, x in enumerate(pairs):
            for i in range(2):
                window = first + 2 * p + i
                flat_out[pl.ds(window, GROUP, stride=stride), :] = x[i * GROUP : (i + 1) * GROUP]

    staggered(group(part) for part in range(GRID_STEP // PART))


def grid_stage(received, fed, weights, chunk, earlier):
    per_device = received.shape[1]
    shape = (GROUP, GRID_STEP // GROUP, CHANNELS)
    in_specs = [whole(shape)] + [of_layer(w, 1) for w in weights]
    args = (received,) + weights
    if not fed:
        in_specs += [of_layer(w, 0) for w in weights[3:]]
        args += weights[3:]
    aliases = {}
    if earlier is not None:
        in_specs.append(pl.BlockSpec(memory_space=pl.ANY))
        aliases = {len(args): 0}
        args += (earlier,)

    def body(*refs):
        grid_kernel(fed, *refs)

    return pl.pallas_call(
        body,
        grid=(1,),
        in_specs=in_specs,
        out_specs=pl.BlockSpec(shape, lambda s: (0, chunk, 0)),
        out_shape=jax.ShapeDtypeStruct((GROUP, CHUNKS * per_device, CHANNELS), F32),
        input_output_aliases=aliases,
        compiler_params=pltpu.CompilerParams(vmem_limit_bytes=VMEM_LIMIT),
        cost_estimate=pl.CostEstimate(
            flops=14_000_000_000, bytes_accessed=4_000_000, transcendentals=0
        ),
    )(*args)


def by_pairs(edge, at, axis, count):
    even = at % 2 == 0
    swaps = []
    for first, last in ((0, even), (1, jnp.logical_not(even))):
        lower = [(i, i + 1) for i in range(first, count - 1, 2)]
        pairs = lower + [(b, a) for a, b in lower]
        swaps.append(lax.ppermute(edge(last), axis, pairs))
    return swaps


def per_device(
    field, context, ctx_weight, norm_gains, expand_weight, depth_weight, se_reduce, se_expand,
    project_weight, attn_qkv, attn_out, mlp_in, mlp_out,
):
    row_axis = ("rg", "core")
    rows, cols = 16, 8
    row = lax.axis_index(row_axis)
    col = lax.axis_index("col")

    def row_edge(last):
        fine = lax.dynamic_index_in_dim(field, jnp.where(last, 31, 0), 0, keepdims=False)
        of_context = lax.dynamic_index_in_dim(context, jnp.where(last, 7, 0), 0, keepdims=False)
        return jnp.concatenate([fine, of_context], axis=0)

    rows_a, rows_b = by_pairs(row_edge, row, row_axis, rows)
    odd = row % 2 == 1

    def column_edge(last):
        fine_at, coarse_at = jnp.where(last, 127, 0), jnp.where(last, 31, 0)

        def one(x, at):
            return lax.dynamic_slice_in_dim(x, at, 1, axis=x.ndim - 2).reshape(-1, CHANNELS)

        parts = []
        for start, stop, tile, at in ((0, 128, field, fine_at), (128, 160, context, coarse_at)):
            of_a, of_b = one(rows_a[start:stop], at), one(rows_b[start:stop], at)
            parts += [jnp.where(odd, of_a, of_b), one(tile, at), jnp.where(odd, of_b, of_a)]
        return jnp.concatenate(parts, axis=0)

    cols_a, cols_b = by_pairs(column_edge, col, "col", cols)
    place = jnp.stack([row, col]).astype(jnp.int32)
    lifted, active, partial = lift_stage(
        place,
        (
            field, context, rows_a, rows_b, cols_a, cols_b, ctx_weight, norm_gains, expand_weight,
            depth_weight, se_reduce.T,
        ),
        rows * cols,
    )

    def exchange(x, axes):
        return lax.all_to_all(x, axes, split_axis=0, concat_axis=0, tiled=True)

    sums = exchange(partial[:, None, :], ("rg", "core", "col"))[:, 0, :]

    weights = tuple(prepare_stage(norm_gains, attn_qkv, attn_out, mlp_in, mlp_out))
    cells_total = rows * cols * field.shape[0] * field.shape[1]
    group = ("rg", "col")
    sent = []
    for chunk in range(CHUNKS):
        mine = block_stage(
            chunk, chunk > 0, lifted, active, sums, se_expand, project_weight, weights, cells_total
        )
        sent.append(exchange(mine.reshape(GROUP, -1, CHANNELS), group))
    attended = None
    for chunk in range(CHUNKS):
        attended = grid_stage(sent[chunk], chunk > 0, weights, chunk, attended)
    back = exchange(attended, group)
    return back.reshape(field.shape)


def solution(mesh):
    fine = Mesh(mesh.devices.reshape(8, 2, 8), ("rg", "core", "col"))
    tiled = P(("rg", "core"), "col", None)
    return jax.shard_map(
        per_device,
        mesh=fine,
        in_specs=(tiled, tiled) + (P(),) * 11,
        out_specs=tiled,
        check_vma=False,
    )
```

```python
import math

import jax
import jax.numpy as jnp
import numpy as np
from jax import lax
from jax.experimental import pallas as pl
from jax.experimental.pallas import tpu as pltpu
from jax.sharding import Mesh
from jax.sharding import PartitionSpec as P

HEADS = 4
WINDOW = 8
CHANNELS = 128
EXPANDED = 512
MLP_HIDDEN = 512
SQUEEZE = 32
HEAD_DIM = CHANNELS // HEADS
CELLS = WINDOW * WINDOW
GROUP = 64
WIDE = 136
COARSE_WIDE = 48
EPSILON = 1e-05
F32 = jnp.float32
BF16 = jnp.bfloat16
HIGHEST = lax.Precision.HIGHEST
CHUNKS = 2
BLOCK_STEP = 1024
GRID_STEP = 2048
VMEM_LIMIT = 56 * 1024 * 1024

GELU_IN = (math.sqrt(2.0 / math.pi) * 0.044715) ** (1.0 / 3.0)
GELU_OUT = 0.5 / GELU_IN
GELU_LINEAR = math.sqrt(2.0 / math.pi) / GELU_IN


def bend(s):
    return s * (1.0 + jnp.tanh(s * (GELU_LINEAR + s * s)))


def split(x):
    high = x.astype(BF16)
    low = (x - high.astype(F32)).astype(BF16)
    return high, low


def dot(a, b):
    return jnp.dot(a, b, preferred_element_type=F32)


def rows_of(parts):
    return jnp.concatenate(parts, axis=0)


def lanes_of(parts):
    return jnp.concatenate(parts, axis=1)


def normed(x):
    shifted = x - jnp.mean(x, axis=-1, keepdims=True)
    spread = jnp.sum(shifted * shifted, axis=-1, keepdims=True)
    return shifted * lax.rsqrt(spread + CHANNELS * EPSILON)


def gained(weight, gain):
    column = jnp.broadcast_to(gain * math.sqrt(CHANNELS), (CHANNELS, CHANNELS)).T
    return lanes_of([weight[:, c : c + 128] * column for c in range(0, weight.shape[1], 128)])


def three(x):
    high, low = split(x)
    return lanes_of([high, low, high])


def stack_rows(weight):
    high, low = split(weight)
    return rows_of([high, high, low])


def deep_weight(weight):
    return lanes_of(split(weight))


def prepare_attention(qkv_ref, out_ref, gain, k3, qv3, out3):
    scale = math.log2(math.e) / math.sqrt(HEAD_DIM)
    k3[...] = stack_rows(gained(qkv_ref[0, :, CHANNELS : 2 * CHANNELS], gain))
    row_gain = gain * math.sqrt(CHANNELS)
    queries = qkv_ref[0, :, :CHANNELS].T * (row_gain * scale)
    values = qkv_ref[0, :, 2 * CHANNELS :].T * row_gain
    high, low = split(rows_of([queries, values]))
    qv3[...] = lanes_of([high, high, low])
    out3[...] = stack_rows(out_ref[0])


def prepare_feed(in_ref, mlp_ref, gain, in3, mlp_pair):
    in3[...] = stack_rows(gained(GELU_IN * in_ref[0], gain))
    mlp_pair[...] = deep_weight(GELU_OUT * mlp_ref[0])


PAIR = 2 * CELLS
PART = 512


def attend(pairs, k3, qv3, out3):
    left = lax.broadcasted_iota(jnp.int32, (HEAD_DIM, PAIR), 1) < CELLS
    left_all = lax.broadcasted_iota(jnp.int32, (CHANNELS, PAIR), 1) < CELLS
    zero = jnp.zeros((HEAD_DIM, PAIR), BF16)
    zero_block = jnp.zeros((2 * HEAD_DIM, PAIR), BF16)
    natural, turned = [], []
    for x in pairs:
        high, low = split(normed(x))
        natural.append(lanes_of([high, low, high]))
        high, low = high.T, low.T
        turned.append(rows_of([high, low, high]))
    yield
    keys = dot(rows_of(natural), k3[...])
    both = dot(qv3[...], lanes_of(turned))
    yield
    sides, value_sides = [], []

    def by_heads(straight, swapped):
        blocks = []
        for group in range(2):
            at = [slice(h * HEAD_DIM, (h + 1) * HEAD_DIM) for h in (2 * group, 2 * group + 1)]
            block = rows_of(
                [jnp.where(left, straight[at[0]], zero), jnp.where(left, zero, swapped[at[1]])]
            )
            blocks.append(lanes_of([zero_block, block] if group else [block, zero_block]))
        return rows_of(blocks)

    for p in range(len(pairs)):
        at = slice(p * PAIR, (p + 1) * PAIR)
        key3 = three(keys[at])
        high, low = split(both[:CHANNELS, at])
        high_swapped, low_swapped = pltpu.roll(high, CELLS, 1), pltpu.roll(low, CELLS, 1)
        for second in range(2):
            if second:
                h, l = by_heads(high_swapped, high), by_heads(low_swapped, low)
            else:
                h, l = by_heads(high, high_swapped), by_heads(low, low_swapped)
            sides.append((key3[second * CELLS : (second + 1) * CELLS], rows_of([h, h, l])))
        high, low = split(both[CHANNELS:, at])
        low = pltpu.roll(low, CELLS, 1)
        first, second = jnp.where(left_all, high, low), jnp.where(left_all, low, high)
        value_sides += [lanes_of([first, first]), lanes_of([second, second])]
    yield
    scores = [dot(key, query) for key, query in sides]
    yield
    weights, scales = [], []
    for score in scores:
        weight = jnp.exp2(score - jnp.max(score, axis=0, keepdims=True))
        scales.append(1.0 / jnp.sum(weight, axis=0, keepdims=True))
        high, low = split(weight)
        weights.append(rows_of([high, high, low, low]))
    yield
    mixed = [
        [dot(value[64 * g : 64 * g + 64], weight[:, 128 * g : 128 * g + 128]) for g in range(2)]
        for value, weight in zip(value_sides, weights)
    ]
    yield
    blended = []
    for p in range(len(pairs)):
        parts = []
        for h in range(HEADS):
            lanes = slice(128 * (h // 2), 128 * (h // 2) + 128)
            at = slice((h % 2) * HEAD_DIM, (h % 2 + 1) * HEAD_DIM)
            of_a, of_b = (
                mixed[2 * p + i][h // 2][at] * scales[2 * p + i][:, lanes] for i in range(2)
            )
            if h % 2:
                of_a = pltpu.roll(of_a, CELLS, 1)
            else:
                of_b = pltpu.roll(of_b, CELLS, 1)
            parts.append(jnp.where(left, of_a, of_b))
        blended.append(three(rows_of(parts).T))
    yield
    added = dot(rows_of(blended), out3[...])
    yield
    return [x + added[p * PAIR : (p + 1) * PAIR] for p, x in enumerate(pairs)]


def feed(pairs, in3, mlp_pair):
    parts = [three(normed(x)) for x in pairs]
    yield
    inner = dot(rows_of(parts), in3[...])
    yield
    high, low = split_blocks(inner, 64, bend)
    yield
    wide = dot(high, mlp_pair[...])
    rest = dot(low, mlp_pair[:, :CHANNELS])
    yield
    out = []
    for p, x in enumerate(pairs):
        at = slice(p * PAIR, (p + 1) * PAIR)
        out.append(x + (wide[at, :CHANNELS] + (wide[at, CHANNELS:] + rest[at])))
    return out


def staggered(groups):
    waiting, running = list(groups), []
    while waiting or running:
        if waiting:
            running.append(waiting.pop(0))
        for group in list(running):
            try:
                next(group)
            except StopIteration:
                running.remove(group)


def split_blocks(x, rows, make):
    highs, lows = [], []
    for r in range(0, x.shape[0], rows):
        made = [split(make(x[r : r + rows, c : c + 128])) for c in range(0, x.shape[1], 128)]
        highs.append(lanes_of([m[0] for m in made]))
        lows.append(lanes_of([m[1] for m in made]))
    return rows_of(highs), rows_of(lows)


PHASES = ((0.375, 0.625, 0.0), (0.125, 0.875, 0.0), (0.0, 0.875, 0.125), (0.0, 0.625, 0.375))


def lifting():
    fine = np.zeros((WIDE + 8, COARSE_WIDE), np.float32)

    def fill(at, column):
        k, o = column // 4, column % 4
        for step, weight in zip((-1, 0, 1), PHASES[o]):
            if weight:
                fine[at, (k + step) % 40] = weight

    for column in range(128):
        fill(8 * (column % 16) + column // 16, column)
    fill(128, -1)
    fill(135, 128)
    both = np.concatenate([fine, fine], axis=1)
    pairs = (weights[:2] if weights[0] else weights[1:] for weights in PHASES)
    return np.stack([np.concatenate([a * both, b * both], axis=1) for a, b in pairs])


def lift_kernel(
    place_ref, field_ref, context_ref, rows_a_ref, rows_b_ref, cols_a_ref, cols_b_ref, up_ref,
    ctxw_ref, gains_ref, expand_ref, depth_ref, reduce_ref, lifted_ref, active_ref, sum_ref,
    lift, ctx, coarse, hid, expand3, total,
):
    step = pl.program_id(0)
    sublane = lax.broadcasted_iota(jnp.int32, (8, 128), 0)
    first_row, last_row = sublane == 0, sublane == 7

    @pl.when(step == 0)
    def _():
        expand3[...] = stack_rows(gained(GELU_IN * expand_ref[...], gains_ref[0:1]))
        total[...] = jnp.zeros_like(total)
        for t in range(16):
            lift[1:33, 8 * t : 8 * t + 8] = field_ref[:, pl.ds(t, 8, stride=16), :]
        ctx[1:9, :32] = context_ref[...]

        def take_rows(above_ref, below_ref):
            for t in range(16):
                lift[0, 8 * t : 8 * t + 8] = above_ref[pl.ds(t, 8, stride=16), :]
                lift[33, 8 * t : 8 * t + 8] = below_ref[pl.ds(t, 8, stride=16), :]
            ctx[0, :32] = above_ref[128:]
            ctx[9, :32] = below_ref[128:]

        def take_columns(before_ref, after_ref):
            zero = jnp.zeros((8, 128), F32)
            for e in range(44):
                after = jnp.broadcast_to(after_ref[e : e + 1], (8, 128))
                before = jnp.broadcast_to(before_ref[e : e + 1], (8, 128))
                if e < 34:
                    lift[e, 128:] = jnp.where(first_row, before, jnp.where(last_row, after, zero))
                else:
                    ctx[e - 34, 32:40] = jnp.where(
                        first_row, after, jnp.where(last_row, before, zero)
                    )
                    ctx[e - 34, 40:] = zero

        pl.when(place_ref[0] % 2 == 0)(lambda: take_rows(rows_b_ref, rows_a_ref))
        pl.when(place_ref[0] % 2 == 1)(lambda: take_rows(rows_a_ref, rows_b_ref))
        pl.when(place_ref[1] % 2 == 0)(lambda: take_columns(cols_b_ref, cols_a_ref))
        pl.when(place_ref[1] % 2 == 1)(lambda: take_columns(cols_a_ref, cols_b_ref))
        weight = stack_rows(ctxw_ref[...])
        projected = dot(three(ctx[...].reshape(10 * COARSE_WIDE, CHANNELS)), weight)
        for k in range(10):
            high, low = split(projected[COARSE_WIDE * k : COARSE_WIDE * (k + 1)])
            coarse[2 * COARSE_WIDE * k : 2 * COARSE_WIDE * (k + 1)] = rows_of([high, low])

    has_after = jnp.where(place_ref[1] < 7, 1.0, 0.0)
    has_before = jnp.where(place_ref[1] > 0, 1.0, 0.0)
    inside = jnp.where(first_row, has_before, has_after)

    def hidden_rows(first, fine_first, k_first, count):
        parts = []
        for i in range(0, count, 2):
            two = []
            for j in (i, i + 1):
                k, o = (fine_first + j) // 4, (fine_first + j) % 4
                at = k_first + k - (1 if PHASES[o][0] else 0)
                at = pl.multiple_of(at * (2 * COARSE_WIDE), 2 * COARSE_WIDE)
                two_rows = coarse[pl.ds(at, 4 * COARSE_WIDE)]
                x = lift[first + j] + dot(up_ref[o], two_rows)[:WIDE]
                lift[first + j] = x
                two.append(x)
            parts.append(three(normed(rows_of(two))))
        made = dot(rows_of(parts), expand3[...])
        for i in range(count):
            for c in range(0, EXPANDED, 128):
                out = bend(made[i * WIDE : (i + 1) * WIDE, c : c + 128])
                hid[first + i, :128, c : c + 128] = out[:128]
                hid[first + i, 128:, c : c + 128] = out[128:] * inside

    @pl.when(step == 0)
    def _():
        hidden_rows(0, -1, 1, 2)

        @pl.when(place_ref[0] == 0)
        def _():
            hid[0] = jnp.zeros((WIDE, EXPANDED), F32)

    hidden_rows(8 * step + 2, 1, 2 * step + 1, 4)
    hidden_rows(8 * step + 6, 5, 2 * step + 1, 4)

    @pl.when((step == 3) & (place_ref[0] == 15))
    def _():
        hid[33] = jnp.zeros((WIDE, EXPANDED), F32)

    lifted_ref[...] = lift[pl.ds(8 * step + 1, 8), :128]

    for part in range(EXPANDED // 128):
        lanes = slice(part * 128, (part + 1) * 128)
        taps = [
            [jnp.broadcast_to((GELU_IN * GELU_OUT) * depth_ref[i, j : j + 1, lanes], (8, 128)) for j in range(3)]
            for i in range(3)
        ]

        def row(r, summed):
            def column(t):
                seen = [hid[8 * step + r + i, 8 * t : 8 * t + 8, lanes] for i in range(3)]
                return [
                    seen[0] * taps[0][j] + seen[1] * taps[1][j] + seen[2] * taps[2][j]
                    for j in range(3)
                ]

            first, last, halo = column(0), column(15), column(16)
            before = jnp.where(first_row, halo[0], pltpu.roll(last[0], 1, 0))
            end = jnp.where(last_row, halo[2], pltpu.roll(first[2], 7, 0))
            here = first
            for t in range(16):
                following = column(t + 1) if t < 14 else last
                out = bend(here[1] + before + (following[2] if t < 15 else end))
                active_ref[r, 8 * t : 8 * t + 8, lanes] = out
                summed = summed + out
                before, here = here[0], following
            return summed

        summed = total[:, lanes]
        for r in range(8):
            summed = row(r, summed)
        total[:, lanes] = summed

    @pl.when(step == 3)
    def _():
        squeezed = lax.dot_general(
            total[...], reduce_ref[...], (((1,), (1,)), ((), ())), precision=HIGHEST,
            preferred_element_type=F32,
        )
        squeezed = jnp.sum(squeezed, axis=0, keepdims=True)
        padded = lanes_of([squeezed, jnp.zeros((1, 128 - SQUEEZE), F32)])
        sum_ref[...] = jnp.broadcast_to(padded, sum_ref.shape)


def whole(shape):
    return pl.BlockSpec(shape, lambda *_: (0,) * len(shape))


def of_layer(array, layer):
    shape = (1,) + array.shape[1:]
    return pl.BlockSpec(shape, lambda *_: (layer,) + (0,) * (len(shape) - 1))


def lift_stage(place, args, copies):
    up = jnp.asarray(lifting(), BF16)
    args = args[:6] + (up,) + args[6:]
    return pl.pallas_call(
        lift_kernel,
        grid=(4,),
        in_specs=[pl.BlockSpec(memory_space=pltpu.SMEM)] + [whole(a.shape) for a in args],
        out_specs=[
            pl.BlockSpec((8, 128, CHANNELS), lambda s: (s, 0, 0)),
            pl.BlockSpec((8, 128, EXPANDED), lambda s: (s, 0, 0)),
            whole((copies, 128)),
        ],
        out_shape=[
            jax.ShapeDtypeStruct((32, 128, CHANNELS), F32),
            jax.ShapeDtypeStruct((32, 128, EXPANDED), F32),
            jax.ShapeDtypeStruct((copies, 128), F32),
        ],
        scratch_shapes=[
            pltpu.VMEM((34, WIDE, CHANNELS), F32),
            pltpu.VMEM((10, COARSE_WIDE, CHANNELS), F32),
            pltpu.VMEM((20 * COARSE_WIDE, CHANNELS), BF16),
            pltpu.VMEM((34, WIDE, EXPANDED), F32),
            pltpu.VMEM((3 * CHANNELS, EXPANDED), BF16),
            pltpu.VMEM((8, EXPANDED), F32),
        ],
        compiler_params=pltpu.CompilerParams(vmem_limit_bytes=VMEM_LIMIT),
        cost_estimate=pl.CostEstimate(
            flops=8_000_000_000, bytes_accessed=14_000_000, transcendentals=0
        ),
    )(place, *args)


def block_kernel(
    cells_total, fed, lifted_ref, active_ref, sums_ref, sexp_ref, project_ref, gains_ref, qkv_ref,
    aout_ref, min_ref, mout_ref, out_ref, project, sums, k3, qv3, out3, *feed_weights,
):
    @pl.when(pl.program_id(0) == 0)
    def _():
        pooled = jnp.sum(sums_ref[...], axis=0, keepdims=True) * (GELU_OUT / cells_total)
        squeezed = pooled[:, :SQUEEZE]
        squeezed = squeezed * jax.nn.sigmoid(squeezed)
        wide = jnp.broadcast_to(squeezed, (CHANNELS, SQUEEZE))
        gate = jnp.dot(wide, sexp_ref[...], precision=HIGHEST, preferred_element_type=F32)
        project[...] = deep_weight(project_ref[...] * (GELU_OUT * jax.nn.sigmoid(gate)).T)
        prepare_attention(qkv_ref, aout_ref, gains_ref[1:2], k3, qv3, out3)
        if fed:
            prepare_feed(min_ref, mout_ref, gains_ref[2:3], *feed_weights)

    for half in range(0, 8, PART // 128):
        rows = slice(half, half + PART // 128)
        halves = [split(active_ref[r]) for r in range(half, half + PART // 128)]
        wide = dot(rows_of([h[0] for h in halves]), project[...])
        rest = dot(rows_of([h[1] for h in halves]), project[:, :CHANNELS])
        added = wide[:, :CHANNELS] + (wide[:, CHANNELS:] + rest)
        sums[rows] = lifted_ref[rows] + added.reshape(PART // 128, 128, CHANNELS)

    def window(w):
        at = pl.ds(64 * (w % 2) + w // 2, WINDOW, stride=8)
        return rows_of([sums[r, at, :] for r in range(WINDOW)])

    def group(part):
        start = part * PART // CELLS
        pairs = [rows_of([window(w), window(w + 1)]) for w in range(start, start + 8, 2)]
        pairs = yield from attend(pairs, k3, qv3, out3)
        if fed:
            pairs = yield from feed(pairs, *feed_weights)
        for p, x in enumerate(pairs):
            out_ref[part * PART + p * PAIR : part * PART + (p + 1) * PAIR] = x

    staggered(group(part) for part in range(BLOCK_STEP // PART))


ATTENTION_SCRATCH = [
    pltpu.VMEM((3 * CHANNELS, CHANNELS), BF16),
    pltpu.VMEM((2 * CHANNELS, 3 * CHANNELS), BF16),
    pltpu.VMEM((3 * CHANNELS, CHANNELS), BF16),
]
FEED_SCRATCH = [
    pltpu.VMEM((3 * CHANNELS, MLP_HIDDEN), BF16),
    pltpu.VMEM((MLP_HIDDEN, 2 * CHANNELS), BF16),
]


def block_stage(chunk, fed, lifted, active, sums, se_expand, project, gains, weights, cells_total):
    per_row = 128 // (BLOCK_STEP // 8)
    steps = 4 // CHUNKS * per_row
    row_base = chunk * (4 // CHUNKS)
    rest = (sums, se_expand, project, gains)

    def strip(channels):
        return pl.BlockSpec(
            (8, BLOCK_STEP // 8, channels), lambda s: (row_base + s // per_row, s % per_row, 0)
        )

    def body(*refs):
        block_kernel(cells_total, fed, *refs)

    return pl.pallas_call(
        body,
        grid=(steps,),
        in_specs=[strip(CHANNELS), strip(EXPANDED)]
        + [whole(a.shape) for a in rest]
        + [of_layer(w, 0) for w in weights],
        out_specs=pl.BlockSpec((BLOCK_STEP, CHANNELS), lambda s: (s, 0)),
        out_shape=jax.ShapeDtypeStruct((steps * BLOCK_STEP, CHANNELS), F32),
        scratch_shapes=[
            pltpu.VMEM((EXPANDED, 2 * CHANNELS), BF16),
            pltpu.VMEM((8, 128, CHANNELS), F32),
        ]
        + ATTENTION_SCRATCH
        + (FEED_SCRATCH if fed else []),
        compiler_params=pltpu.CompilerParams(vmem_limit_bytes=VMEM_LIMIT),
        cost_estimate=pl.CostEstimate(
            flops=14_000_000_000, bytes_accessed=8_000_000, transcendentals=0
        ),
    )(lifted, active, *rest, *weights)


def grid_kernel(fed, x_ref, gains_ref, *refs):
    scratch = 5 if fed else 7
    out_ref, k3, qv3, out3, *feeds = refs[-scratch - 1 :]
    qkv_ref, aout_ref, *feed_refs = refs[: 4 if fed else 6]

    @pl.when(pl.program_id(0) == 0)
    def _():
        prepare_attention(qkv_ref, aout_ref, gains_ref[3:4], k3, qv3, out3)
        prepare_feed(*feed_refs[:2], gains_ref[4:5], *feeds[:2])
        if not fed:
            prepare_feed(*feed_refs[2:], gains_ref[2:3], *feeds[2:])

    stride = GRID_STEP // GROUP
    flat_in = x_ref.reshape(GRID_STEP, CHANNELS)
    flat_out = out_ref.reshape(GRID_STEP, CHANNELS)

    def group(part):
        first = part * PART // GROUP
        windows = [flat_in[pl.ds(first + p, GROUP, stride=stride), :] for p in range(PART // GROUP)]
        pairs = [rows_of(windows[i : i + 2]) for i in range(0, len(windows), 2)]
        if not fed:
            pairs = yield from feed(pairs, *feeds[2:])
        pairs = yield from attend(pairs, k3, qv3, out3)
        pairs = yield from feed(pairs, *feeds[:2])
        for p, x in enumerate(pairs):
            for i in range(2):
                window = first + 2 * p + i
                flat_out[pl.ds(window, GROUP, stride=stride), :] = x[i * GROUP : (i + 1) * GROUP]

    staggered(group(part) for part in range(GRID_STEP // PART))


def grid_stage(received, fed, gains, weights, chunk, earlier):
    per_device = received.shape[1]
    steps = per_device * GROUP // GRID_STEP
    shape = (GROUP, GRID_STEP // GROUP, CHANNELS)
    in_specs = [pl.BlockSpec(shape, lambda s: (0, s, 0)), whole(gains.shape)]
    in_specs += [of_layer(w, 1) for w in weights]
    args = (received, gains) + weights
    if not fed:
        in_specs += [of_layer(w, 0) for w in weights[2:]]
        args += weights[2:]
    aliases = {}
    if earlier is not None:
        in_specs.append(pl.BlockSpec(memory_space=pl.ANY))
        aliases = {len(args): 0}
        args += (earlier,)

    def body(*refs):
        grid_kernel(fed, *refs)

    return pl.pallas_call(
        body,
        grid=(steps,),
        in_specs=in_specs,
        out_specs=pl.BlockSpec(shape, lambda s: (0, chunk * steps + s, 0)),
        out_shape=jax.ShapeDtypeStruct((GROUP, CHUNKS * per_device, CHANNELS), F32),
        scratch_shapes=ATTENTION_SCRATCH + FEED_SCRATCH + ([] if fed else FEED_SCRATCH),
        input_output_aliases=aliases,
        compiler_params=pltpu.CompilerParams(vmem_limit_bytes=VMEM_LIMIT),
        cost_estimate=pl.CostEstimate(
            flops=14_000_000_000, bytes_accessed=4_000_000, transcendentals=0
        ),
    )(*args)


def by_pairs(edge, at, axis, count):
    even = at % 2 == 0
    swaps = []
    for first, last in ((0, even), (1, jnp.logical_not(even))):
        lower = [(i, i + 1) for i in range(first, count - 1, 2)]
        pairs = lower + [(b, a) for a, b in lower]
        swaps.append(lax.ppermute(edge(last), axis, pairs))
    return swaps


def per_device(
    field, context, ctx_weight, norm_gains, expand_weight, depth_weight, se_reduce, se_expand,
    project_weight, attn_qkv, attn_out, mlp_in, mlp_out,
):
    row_axis = ("rg", "core")
    rows, cols = 16, 8
    row = lax.axis_index(row_axis)
    col = lax.axis_index("col")

    def row_edge(last):
        fine = lax.dynamic_index_in_dim(field, jnp.where(last, 31, 0), 0, keepdims=False)
        of_context = lax.dynamic_index_in_dim(context, jnp.where(last, 7, 0), 0, keepdims=False)
        return jnp.concatenate([fine, of_context], axis=0)

    rows_a, rows_b = by_pairs(row_edge, row, row_axis, rows)
    odd = row % 2 == 1

    def column_edge(last):
        fine_at, coarse_at = jnp.where(last, 127, 0), jnp.where(last, 31, 0)

        def one(x, at):
            return lax.dynamic_slice_in_dim(x, at, 1, axis=x.ndim - 2).reshape(-1, CHANNELS)

        parts = []
        for start, stop, tile, at in ((0, 128, field, fine_at), (128, 160, context, coarse_at)):
            of_a, of_b = one(rows_a[start:stop], at), one(rows_b[start:stop], at)
            parts += [jnp.where(odd, of_a, of_b), one(tile, at), jnp.where(odd, of_b, of_a)]
        return jnp.concatenate(parts, axis=0)

    cols_a, cols_b = by_pairs(column_edge, col, "col", cols)
    place = jnp.stack([row, col]).astype(jnp.int32)
    lifted, active, partial = lift_stage(
        place,
        (
            field, context, rows_a, rows_b, cols_a, cols_b, ctx_weight, norm_gains, expand_weight,
            depth_weight, se_reduce.T,
        ),
        rows * cols,
    )

    def exchange(x, axes):
        return lax.all_to_all(x, axes, split_axis=0, concat_axis=0, tiled=True)

    sums = exchange(partial[:, None, :], ("rg", "core", "col"))[:, 0, :]

    weights = (attn_qkv, attn_out, mlp_in, mlp_out)
    cells_total = rows * cols * field.shape[0] * field.shape[1]
    group = ("rg", "col")
    sent = []
    for chunk in range(CHUNKS):
        mine = block_stage(
            chunk, chunk > 0, lifted, active, sums, se_expand, project_weight, norm_gains, weights,
            cells_total,
        )
        sent.append(exchange(mine.reshape(GROUP, -1, CHANNELS), group))
    attended = None
    for chunk in range(CHUNKS):
        attended = grid_stage(sent[chunk], chunk > 0, norm_gains, weights, chunk, attended)
    back = exchange(attended, group)
    halves = back.reshape(4 // CHUNKS, 16, 2, CHUNKS, WINDOW // 2, WINDOW, CHANNELS)
    return halves.transpose(3, 0, 2, 4, 1, 5, 6).reshape(field.shape)


def solution(mesh):
    fine = Mesh(mesh.devices.reshape(8, 2, 8), ("rg", "core", "col"))
    tiled = P(("rg", "core"), "col", None)
    return jax.shard_map(
        per_device,
        mesh=fine,
        in_specs=(tiled, tiled) + (P(),) * 11,
        out_specs=tiled,
        check_vma=False,
    )
```

```python
import math

import jax
import jax.numpy as jnp
import numpy as np
from jax import lax
from jax.experimental import pallas as pl
from jax.experimental.pallas import tpu as pltpu
from jax.sharding import Mesh
from jax.sharding import PartitionSpec as P

HEADS = 4
WINDOW = 8
CHANNELS = 128
EXPANDED = 512
MLP_HIDDEN = 512
SQUEEZE = 32
HEAD_DIM = CHANNELS // HEADS
CELLS = WINDOW * WINDOW
GROUP = 64
WIDE = 136
COARSE_WIDE = 48
EPSILON = 1e-05
F32 = jnp.float32
BF16 = jnp.bfloat16
HIGHEST = lax.Precision.HIGHEST
CHUNKS = 2
BLOCK_STEP = 1024
GRID_STEP = 2048
VMEM_LIMIT = 56 * 1024 * 1024

GELU_IN = (math.sqrt(2.0 / math.pi) * 0.044715) ** (1.0 / 3.0)
GELU_OUT = 0.5 / GELU_IN
GELU_LINEAR = math.sqrt(2.0 / math.pi) / GELU_IN


def bend(s):
    return s * (1.0 + jnp.tanh(s * (GELU_LINEAR + s * s)))


def split(x):
    high = x.astype(BF16)
    low = (x - high.astype(F32)).astype(BF16)
    return high, low


def dot(a, b):
    return jnp.dot(a, b, preferred_element_type=F32)


def rows_of(parts):
    return jnp.concatenate(parts, axis=0)


def lanes_of(parts):
    return jnp.concatenate(parts, axis=1)


def normed(x):
    shifted = x - jnp.mean(x, axis=-1, keepdims=True)
    spread = jnp.sum(shifted * shifted, axis=-1, keepdims=True)
    return shifted * lax.rsqrt(spread + CHANNELS * EPSILON)


def gained(weight, gain):
    column = jnp.broadcast_to(gain * math.sqrt(CHANNELS), (CHANNELS, CHANNELS)).T
    return lanes_of([weight[:, c : c + 128] * column for c in range(0, weight.shape[1], 128)])


def three(x):
    high, low = split(x)
    return lanes_of([high, low, high])


def stack_rows(weight):
    high, low = split(weight)
    return rows_of([high, high, low])


def deep_weight(weight):
    return lanes_of(split(weight))


def prepare_attention(qkv_ref, out_ref, gain, k3, qv3, out3):
    scale = math.log2(math.e) / math.sqrt(HEAD_DIM)
    k3[...] = stack_rows(gained(qkv_ref[0, :, CHANNELS : 2 * CHANNELS], gain))
    row_gain = gain * math.sqrt(CHANNELS)
    queries = qkv_ref[0, :, :CHANNELS].T * (row_gain * scale)
    values = qkv_ref[0, :, 2 * CHANNELS :].T * row_gain
    high, low = split(rows_of([queries, values]))
    qv3[...] = lanes_of([high, high, low])
    out3[...] = stack_rows(out_ref[0])


def prepare_feed(in_ref, mlp_ref, gain, in3, mlp_pair):
    in3[...] = stack_rows(gained(GELU_IN * in_ref[0], gain))
    mlp_pair[...] = deep_weight(GELU_OUT * mlp_ref[0])


PAIR = 2 * CELLS
PART = 512


def attend(pairs, k3, qv3, out3):
    left = lax.broadcasted_iota(jnp.int32, (HEAD_DIM, PAIR), 1) < CELLS
    left_all = lax.broadcasted_iota(jnp.int32, (CHANNELS, PAIR), 1) < CELLS
    zero = jnp.zeros((HEAD_DIM, PAIR), BF16)
    zero_block = jnp.zeros((2 * HEAD_DIM, PAIR), BF16)
    natural, turned = [], []
    for x in pairs:
        high, low = split(normed(x))
        natural.append(lanes_of([high, low, high]))
        high, low = high.T, low.T
        turned.append(rows_of([high, low, high]))
    yield
    keys = dot(rows_of(natural), k3[...])
    both = dot(qv3[...], lanes_of(turned))
    yield
    sides, value_sides = [], []

    def by_heads(straight, swapped):
        blocks = []
        for group in range(2):
            at = [slice(h * HEAD_DIM, (h + 1) * HEAD_DIM) for h in (2 * group, 2 * group + 1)]
            block = rows_of(
                [jnp.where(left, straight[at[0]], zero), jnp.where(left, zero, swapped[at[1]])]
            )
            blocks.append(lanes_of([zero_block, block] if group else [block, zero_block]))
        return rows_of(blocks)

    for p in range(len(pairs)):
        at = slice(p * PAIR, (p + 1) * PAIR)
        key3 = three(keys[at])
        high, low = split(both[:CHANNELS, at])
        high_swapped, low_swapped = pltpu.roll(high, CELLS, 1), pltpu.roll(low, CELLS, 1)
        for second in range(2):
            if second:
                h, l = by_heads(high_swapped, high), by_heads(low_swapped, low)
            else:
                h, l = by_heads(high, high_swapped), by_heads(low, low_swapped)
            sides.append((key3[second * CELLS : (second + 1) * CELLS], rows_of([h, h, l])))
        high, low = split(both[CHANNELS:, at])
        low = pltpu.roll(low, CELLS, 1)
        first, second = jnp.where(left_all, high, low), jnp.where(left_all, low, high)
        value_sides += [lanes_of([first, first]), lanes_of([second, second])]
    yield
    scores = [dot(key, query) for key, query in sides]
    yield
    weights, scales = [], []
    for score in scores:
        weight = jnp.exp2(score - jnp.max(score, axis=0, keepdims=True))
        scales.append(1.0 / jnp.sum(weight, axis=0, keepdims=True))
        high, low = split(weight)
        weights.append(rows_of([high, high, low, low]))
    yield
    mixed = [
        [dot(value[64 * g : 64 * g + 64], weight[:, 128 * g : 128 * g + 128]) for g in range(2)]
        for value, weight in zip(value_sides, weights)
    ]
    yield
    blended = []
    for p in range(len(pairs)):
        parts = []
        for h in range(HEADS):
            lanes = slice(128 * (h // 2), 128 * (h // 2) + 128)
            at = slice((h % 2) * HEAD_DIM, (h % 2 + 1) * HEAD_DIM)
            of_a, of_b = (
                mixed[2 * p + i][h // 2][at] * scales[2 * p + i][:, lanes] for i in range(2)
            )
            if h % 2:
                of_a = pltpu.roll(of_a, CELLS, 1)
            else:
                of_b = pltpu.roll(of_b, CELLS, 1)
            parts.append(jnp.where(left, of_a, of_b))
        blended.append(three(rows_of(parts).T))
    yield
    added = dot(rows_of(blended), out3[...])
    yield
    return [x + added[p * PAIR : (p + 1) * PAIR] for p, x in enumerate(pairs)]


def feed(pairs, in3, mlp_pair):
    parts = [three(normed(x)) for x in pairs]
    yield
    inner = dot(rows_of(parts), in3[...])
    yield
    high, low = split_blocks(inner, 64, bend)
    yield
    wide = dot(high, mlp_pair[...])
    rest = dot(low, mlp_pair[:, :CHANNELS])
    yield
    out = []
    for p, x in enumerate(pairs):
        at = slice(p * PAIR, (p + 1) * PAIR)
        out.append(x + (wide[at, :CHANNELS] + (wide[at, CHANNELS:] + rest[at])))
    return out


def staggered(groups):
    waiting, running = list(groups), []
    while waiting or running:
        if waiting:
            running.append(waiting.pop(0))
        for group in list(running):
            try:
                next(group)
            except StopIteration:
                running.remove(group)


def split_blocks(x, rows, make):
    highs, lows = [], []
    for r in range(0, x.shape[0], rows):
        made = [split(make(x[r : r + rows, c : c + 128])) for c in range(0, x.shape[1], 128)]
        highs.append(lanes_of([m[0] for m in made]))
        lows.append(lanes_of([m[1] for m in made]))
    return rows_of(highs), rows_of(lows)


def column_weights():
    fine = np.zeros((WIDE, COARSE_WIDE), np.float32)
    table = ((0.375, 0.625, 0.0), (0.125, 0.875, 0.0), (0.0, 0.875, 0.125), (0.0, 0.625, 0.375))

    def fill(at, column):
        k, o = column // 4, column % 4
        for step, weight in zip((-1, 0, 1), table[o]):
            if weight:
                fine[at, (k + step) % 40] = weight

    for column in range(128):
        fill(8 * (column % 16) + column // 16, column)
    fill(128, -1)
    fill(135, 128)
    return np.concatenate([fine, fine], axis=1)


ROW_WEIGHTS = ((0.375, 0.625, -1), (0.125, 0.875, -1), (0.875, 0.125, 0), (0.625, 0.375, 0))


def lift_kernel(
    place_ref, field_ref, context_ref, rows_a_ref, rows_b_ref, cols_a_ref, cols_b_ref, up_ref,
    ctxw_ref, gains_ref, expand_ref, depth_ref, reduce_ref, lifted_ref, active_ref, sum_ref,
    lift, ctx, coarse, hid, expand3, total,
):
    step = pl.program_id(0)
    sublane = lax.broadcasted_iota(jnp.int32, (8, 128), 0)
    first_row, last_row = sublane == 0, sublane == 7

    @pl.when(step == 0)
    def _():
        expand3[...] = stack_rows(gained(GELU_IN * expand_ref[...], gains_ref[0:1]))
        total[...] = jnp.zeros_like(total)
        for t in range(16):
            lift[1:33, 8 * t : 8 * t + 8] = field_ref[:, pl.ds(t, 8, stride=16), :]
        ctx[1:9, :32] = context_ref[...]

        def take_rows(above_ref, below_ref):
            for t in range(16):
                lift[0, 8 * t : 8 * t + 8] = above_ref[pl.ds(t, 8, stride=16), :]
                lift[33, 8 * t : 8 * t + 8] = below_ref[pl.ds(t, 8, stride=16), :]
            ctx[0, :32] = above_ref[128:]
            ctx[9, :32] = below_ref[128:]

        def take_columns(before_ref, after_ref):
            zero = jnp.zeros((8, 128), F32)
            for e in range(44):
                after = jnp.broadcast_to(after_ref[e : e + 1], (8, 128))
                before = jnp.broadcast_to(before_ref[e : e + 1], (8, 128))
                if e < 34:
                    lift[e, 128:] = jnp.where(first_row, before, jnp.where(last_row, after, zero))
                else:
                    ctx[e - 34, 32:40] = jnp.where(
                        first_row, after, jnp.where(last_row, before, zero)
                    )
                    ctx[e - 34, 40:] = zero

        pl.when(place_ref[0] % 2 == 0)(lambda: take_rows(rows_b_ref, rows_a_ref))
        pl.when(place_ref[0] % 2 == 1)(lambda: take_rows(rows_a_ref, rows_b_ref))
        pl.when(place_ref[1] % 2 == 0)(lambda: take_columns(cols_b_ref, cols_a_ref))
        pl.when(place_ref[1] % 2 == 1)(lambda: take_columns(cols_a_ref, cols_b_ref))
        weight = stack_rows(ctxw_ref[...])
        projected = dot(three(ctx[...].reshape(10 * COARSE_WIDE, CHANNELS)), weight)
        for k in range(10):
            high, low = split(projected[COARSE_WIDE * k : COARSE_WIDE * (k + 1)])
            coarse[k] = dot(up_ref[...], rows_of([high, low]))

    has_after = jnp.where(place_ref[1] < 7, 1.0, 0.0)
    has_before = jnp.where(place_ref[1] > 0, 1.0, 0.0)
    inside = jnp.where(first_row, has_before, has_after)

    def hidden_rows(first, fine_first, k_first, count):
        parts = []
        for i in range(0, count, 2):
            two = []
            for j in (i, i + 1):
                k, o = (fine_first + j) // 4, (fine_first + j) % 4
                lower, upper, shift = ROW_WEIGHTS[o]
                at = k_first + k + shift
                x = lift[first + j] + (lower * coarse[at] + upper * coarse[at + 1])
                lift[first + j] = x
                two.append(x)
            parts.append(three(normed(rows_of(two))))
        made = dot(rows_of(parts), expand3[...])
        for i in range(count):
            for c in range(0, EXPANDED, 128):
                out = bend(made[i * WIDE : (i + 1) * WIDE, c : c + 128])
                hid[first + i, :128, c : c + 128] = out[:128]
                hid[first + i, 128:, c : c + 128] = out[128:] * inside

    @pl.when(step == 0)
    def _():
        hidden_rows(0, -1, 1, 2)

        @pl.when(place_ref[0] == 0)
        def _():
            hid[0] = jnp.zeros((WIDE, EXPANDED), F32)

    hidden_rows(8 * step + 2, 1, 2 * step + 1, 4)
    hidden_rows(8 * step + 6, 5, 2 * step + 1, 4)

    @pl.when((step == 3) & (place_ref[0] == 15))
    def _():
        hid[33] = jnp.zeros((WIDE, EXPANDED), F32)

    lifted_ref[...] = lift[pl.ds(8 * step + 1, 8), :128]

    for part in range(EXPANDED // 128):
        lanes = slice(part * 128, (part + 1) * 128)
        taps = [
            [jnp.broadcast_to((GELU_IN * GELU_OUT) * depth_ref[i, j : j + 1, lanes], (8, 128)) for j in range(3)]
            for i in range(3)
        ]

        def row(r, summed):
            def column(t):
                seen = [hid[8 * step + r + i, 8 * t : 8 * t + 8, lanes] for i in range(3)]
                return [
                    seen[0] * taps[0][j] + seen[1] * taps[1][j] + seen[2] * taps[2][j]
                    for j in range(3)
                ]

            first, last, halo = column(0), column(15), column(16)
            before = jnp.where(first_row, halo[0], pltpu.roll(last[0], 1, 0))
            end = jnp.where(last_row, halo[2], pltpu.roll(first[2], 7, 0))
            here = first
            for t in range(16):
                following = column(t + 1) if t < 14 else last
                out = bend(here[1] + before + (following[2] if t < 15 else end))
                active_ref[r, part, 8 * t : 8 * t + 8] = out
                summed = summed + out
                before, here = here[0], following
            return summed

        summed = total[:, lanes]
        for r in range(8):
            summed = row(r, summed)
        total[:, lanes] = summed

    @pl.when(step == 3)
    def _():
        squeezed = lax.dot_general(
            total[...], reduce_ref[...], (((1,), (1,)), ((), ())), precision=HIGHEST,
            preferred_element_type=F32,
        )
        squeezed = jnp.sum(squeezed, axis=0, keepdims=True)
        padded = lanes_of([squeezed, jnp.zeros((1, 128 - SQUEEZE), F32)])
        sum_ref[...] = jnp.broadcast_to(padded, sum_ref.shape)


def whole(shape):
    return pl.BlockSpec(shape, lambda *_: (0,) * len(shape))


def of_layer(array, layer):
    shape = (1,) + array.shape[1:]
    return pl.BlockSpec(shape, lambda *_: (layer,) + (0,) * (len(shape) - 1))


def lift_stage(place, args, copies):
    up = jnp.asarray(column_weights(), BF16)
    args = args[:6] + (up,) + args[6:]
    return pl.pallas_call(
        lift_kernel,
        grid=(4,),
        in_specs=[pl.BlockSpec(memory_space=pltpu.SMEM)] + [whole(a.shape) for a in args],
        out_specs=[
            pl.BlockSpec((8, 128, CHANNELS), lambda s: (s, 0, 0)),
            pl.BlockSpec((8, EXPANDED // 128, 128, 128), lambda s: (s, 0, 0, 0)),
            whole((copies, 128)),
        ],
        out_shape=[
            jax.ShapeDtypeStruct((32, 128, CHANNELS), F32),
            jax.ShapeDtypeStruct((32, EXPANDED // 128, 128, 128), F32),
            jax.ShapeDtypeStruct((copies, 128), F32),
        ],
        scratch_shapes=[
            pltpu.VMEM((34, WIDE, CHANNELS), F32),
            pltpu.VMEM((10, COARSE_WIDE, CHANNELS), F32),
            pltpu.VMEM((10, WIDE, CHANNELS), F32),
            pltpu.VMEM((34, WIDE, EXPANDED), F32),
            pltpu.VMEM((3 * CHANNELS, EXPANDED), BF16),
            pltpu.VMEM((8, EXPANDED), F32),
        ],
        compiler_params=pltpu.CompilerParams(vmem_limit_bytes=VMEM_LIMIT),
        cost_estimate=pl.CostEstimate(
            flops=8_000_000_000, bytes_accessed=14_000_000, transcendentals=0
        ),
    )(place, *args)


def block_kernel(
    cells_total, fed, lifted_ref, active_ref, sums_ref, sexp_ref, project_ref, gains_ref, qkv_ref,
    aout_ref, min_ref, mout_ref, out_ref, project, k3, qv3, out3, *feed_weights,
):
    @pl.when(pl.program_id(0) == 0)
    def _():
        pooled = jnp.sum(sums_ref[...], axis=0, keepdims=True) * (GELU_OUT / cells_total)
        squeezed = pooled[:, :SQUEEZE]
        squeezed = squeezed * jax.nn.sigmoid(squeezed)
        wide = jnp.broadcast_to(squeezed, (CHANNELS, SQUEEZE))
        gate = jnp.dot(wide, sexp_ref[...], precision=HIGHEST, preferred_element_type=F32)
        project[...] = deep_weight(project_ref[...] * (GELU_OUT * jax.nn.sigmoid(gate)).T)
        prepare_attention(qkv_ref, aout_ref, gains_ref[1:2], k3, qv3, out3)
        if fed:
            prepare_feed(min_ref, mout_ref, gains_ref[2:3], *feed_weights)

    def window(w, load):
        at = pl.ds(64 * (w % 2) + w // 2, WINDOW, stride=8)
        return rows_of([load(r, at) for r in range(WINDOW)])

    def expanded(r, at):
        return lanes_of([active_ref[r, k, at, :] for k in range(EXPANDED // 128)])

    def projected(start):
        halves = [split(window(w, expanded)) for w in range(start, start + PART // CELLS)]
        yield
        wide = dot(rows_of([h[0] for h in halves]), project[...])
        rest = dot(rows_of([h[1] for h in halves]), project[:, :CHANNELS])
        yield
        pairs = []
        for p in range(PART // PAIR):
            at = slice(p * PAIR, (p + 1) * PAIR)
            x = rows_of(
                [window(start + 2 * p + i, lambda r, at: lifted_ref[r, at, :]) for i in range(2)]
            )
            pairs.append(x + (wide[at, :CHANNELS] + (wide[at, CHANNELS:] + rest[at])))
        return pairs

    def group(part):
        pairs = yield from projected(part * PART // CELLS)
        pairs = yield from attend(pairs, k3, qv3, out3)
        if fed:
            pairs = yield from feed(pairs, *feed_weights)
        for p, x in enumerate(pairs):
            out_ref[part * PART + p * PAIR : part * PART + (p + 1) * PAIR] = x

    staggered(group(part) for part in range(BLOCK_STEP // PART))


ATTENTION_SCRATCH = [
    pltpu.VMEM((3 * CHANNELS, CHANNELS), BF16),
    pltpu.VMEM((2 * CHANNELS, 3 * CHANNELS), BF16),
    pltpu.VMEM((3 * CHANNELS, CHANNELS), BF16),
]
FEED_SCRATCH = [
    pltpu.VMEM((3 * CHANNELS, MLP_HIDDEN), BF16),
    pltpu.VMEM((MLP_HIDDEN, 2 * CHANNELS), BF16),
]


def block_stage(chunk, fed, lifted, active, sums, se_expand, project, gains, weights, cells_total):
    steps = 4 // CHUNKS
    row_base = chunk * (4 // CHUNKS)
    rest = (sums, se_expand, project, gains)

    columns = BLOCK_STEP // 8
    strips = [
        pl.BlockSpec((8, columns, CHANNELS), lambda s: (row_base + s, 0, 0)),
        pl.BlockSpec((8, EXPANDED // 128, columns, 128), lambda s: (row_base + s, 0, 0, 0)),
    ]

    def body(*refs):
        block_kernel(cells_total, fed, *refs)

    return pl.pallas_call(
        body,
        grid=(steps,),
        in_specs=strips
        + [whole(a.shape) for a in rest]
        + [of_layer(w, 0) for w in weights],
        out_specs=pl.BlockSpec((BLOCK_STEP, CHANNELS), lambda s: (s, 0)),
        out_shape=jax.ShapeDtypeStruct((steps * BLOCK_STEP, CHANNELS), F32),
        scratch_shapes=[
            pltpu.VMEM((EXPANDED, 2 * CHANNELS), BF16),
        ]
        + ATTENTION_SCRATCH
        + (FEED_SCRATCH if fed else []),
        compiler_params=pltpu.CompilerParams(vmem_limit_bytes=VMEM_LIMIT),
        cost_estimate=pl.CostEstimate(
            flops=14_000_000_000, bytes_accessed=8_000_000, transcendentals=0
        ),
    )(lifted, active, *rest, *weights)


def grid_kernel(fed, x_ref, gains_ref, *refs):
    scratch = 5 if fed else 7
    out_ref, k3, qv3, out3, *feeds = refs[-scratch - 1 :]
    qkv_ref, aout_ref, *feed_refs = refs[: 4 if fed else 6]

    @pl.when(pl.program_id(0) == 0)
    def _():
        prepare_attention(qkv_ref, aout_ref, gains_ref[3:4], k3, qv3, out3)
        prepare_feed(*feed_refs[:2], gains_ref[4:5], *feeds[:2])
        if not fed:
            prepare_feed(*feed_refs[2:], gains_ref[2:3], *feeds[2:])

    stride = GRID_STEP // GROUP
    flat_in = x_ref.reshape(GRID_STEP, CHANNELS)
    flat_out = out_ref.reshape(GRID_STEP, CHANNELS)

    def group(part):
        first = part * PART // GROUP
        windows = [flat_in[pl.ds(first + p, GROUP, stride=stride), :] for p in range(PART // GROUP)]
        pairs = [rows_of(windows[i : i + 2]) for i in range(0, len(windows), 2)]
        if not fed:
            pairs = yield from feed(pairs, *feeds[2:])
        pairs = yield from attend(pairs, k3, qv3, out3)
        pairs = yield from feed(pairs, *feeds[:2])
        for p, x in enumerate(pairs):
            for i in range(2):
                window = first + 2 * p + i
                flat_out[pl.ds(window, GROUP, stride=stride), :] = x[i * GROUP : (i + 1) * GROUP]

    staggered(group(part) for part in range(GRID_STEP // PART))


def grid_stage(received, fed, gains, weights, chunk, earlier):
    per_device = received.shape[1]
    steps = per_device * GROUP // GRID_STEP
    shape = (GROUP, GRID_STEP // GROUP, CHANNELS)
    in_specs = [pl.BlockSpec(shape, lambda s: (0, s, 0)), whole(gains.shape)]
    in_specs += [of_layer(w, 1) for w in weights]
    args = (received, gains) + weights
    if not fed:
        in_specs += [of_layer(w, 0) for w in weights[2:]]
        args += weights[2:]
    aliases = {}
    if earlier is not None:
        in_specs.append(pl.BlockSpec(memory_space=pl.ANY))
        aliases = {len(args): 0}
        args += (earlier,)

    def body(*refs):
        grid_kernel(fed, *refs)

    return pl.pallas_call(
        body,
        grid=(steps,),
        in_specs=in_specs,
        out_specs=pl.BlockSpec(shape, lambda s: (0, chunk * steps + s, 0)),
        out_shape=jax.ShapeDtypeStruct((GROUP, CHUNKS * per_device, CHANNELS), F32),
        scratch_shapes=ATTENTION_SCRATCH + FEED_SCRATCH + ([] if fed else FEED_SCRATCH),
        input_output_aliases=aliases,
        compiler_params=pltpu.CompilerParams(vmem_limit_bytes=VMEM_LIMIT),
        cost_estimate=pl.CostEstimate(
            flops=14_000_000_000, bytes_accessed=4_000_000, transcendentals=0
        ),
    )(*args)


def by_pairs(edge, at, axis, count):
    even = at % 2 == 0
    swaps = []
    for first, last in ((0, even), (1, jnp.logical_not(even))):
        lower = [(i, i + 1) for i in range(first, count - 1, 2)]
        pairs = lower + [(b, a) for a, b in lower]
        swaps.append(lax.ppermute(edge(last), axis, pairs))
    return swaps


def per_device(
    field, context, ctx_weight, norm_gains, expand_weight, depth_weight, se_reduce, se_expand,
    project_weight, attn_qkv, attn_out, mlp_in, mlp_out,
):
    row_axis = ("rg", "core")
    rows, cols = 16, 8
    row = lax.axis_index(row_axis)
    col = lax.axis_index("col")

    def row_edge(last):
        fine = lax.dynamic_index_in_dim(field, jnp.where(last, 31, 0), 0, keepdims=False)
        of_context = lax.dynamic_index_in_dim(context, jnp.where(last, 7, 0), 0, keepdims=False)
        return jnp.concatenate([fine, of_context], axis=0)

    rows_a, rows_b = by_pairs(row_edge, row, row_axis, rows)
    odd = row % 2 == 1

    def column_edge(last):
        fine_at, coarse_at = jnp.where(last, 127, 0), jnp.where(last, 31, 0)

        def one(x, at):
            return lax.dynamic_slice_in_dim(x, at, 1, axis=x.ndim - 2).reshape(-1, CHANNELS)

        parts = []
        for start, stop, tile, at in ((0, 128, field, fine_at), (128, 160, context, coarse_at)):
            of_a, of_b = one(rows_a[start:stop], at), one(rows_b[start:stop], at)
            parts += [jnp.where(odd, of_a, of_b), one(tile, at), jnp.where(odd, of_b, of_a)]
        return jnp.concatenate(parts, axis=0)

    cols_a, cols_b = by_pairs(column_edge, col, "col", cols)
    place = jnp.stack([row, col]).astype(jnp.int32)
    lifted, active, partial = lift_stage(
        place,
        (
            field, context, rows_a, rows_b, cols_a, cols_b, ctx_weight, norm_gains, expand_weight,
            depth_weight, se_reduce.T,
        ),
        8,
    )

    def exchange(x, axes):
        return lax.all_to_all(x, axes, split_axis=0, concat_axis=0, tiled=True)

    group = ("rg", "col")
    chip = partial[:1] + lax.ppermute(partial[:1], "core", [(0, 1), (1, 0)])
    sums = exchange(jnp.broadcast_to(chip, (GROUP, 1, 128)), group)[:, 0, :]

    weights = (attn_qkv, attn_out, mlp_in, mlp_out)
    cells_total = rows * cols * field.shape[0] * field.shape[1]
    sent = []
    for chunk in range(CHUNKS):
        mine = block_stage(
            chunk, chunk > 0, lifted, active, sums, se_expand, project_weight, norm_gains, weights,
            cells_total,
        )
        sent.append(exchange(mine.reshape(GROUP, -1, CHANNELS), group))
    attended = None
    for chunk in range(CHUNKS):
        attended = grid_stage(sent[chunk], chunk > 0, norm_gains, weights, chunk, attended)
    back = exchange(attended, group)
    halves = back.reshape(4 // CHUNKS, 16, 2, CHUNKS, WINDOW // 2, WINDOW, CHANNELS)
    return halves.transpose(3, 0, 2, 4, 1, 5, 6).reshape(field.shape)


def solution(mesh):
    fine = Mesh(mesh.devices.reshape(8, 2, 8), ("rg", "core", "col"))
    tiled = P(("rg", "core"), "col", None)
    return jax.shard_map(
        per_device,
        mesh=fine,
        in_specs=(tiled, tiled) + (P(),) * 11,
        out_specs=tiled,
        check_vma=False,
    )
```

```python
import math

import jax
import jax.numpy as jnp
import numpy as np
from jax import lax
from jax.experimental import pallas as pl
from jax.experimental.pallas import tpu as pltpu
from jax.sharding import Mesh
from jax.sharding import PartitionSpec as P

HEADS = 4
WINDOW = 8
CHANNELS = 128
EXPANDED = 512
MLP_HIDDEN = 512
SQUEEZE = 32
HEAD_DIM = CHANNELS // HEADS
CELLS = WINDOW * WINDOW
GROUP = 64
WIDE = 136
COARSE_WIDE = 48
EPSILON = 1e-05
F32 = jnp.float32
BF16 = jnp.bfloat16
HIGHEST = lax.Precision.HIGHEST
CHUNKS = 2
BLOCK_STEP = 1024
GRID_STEP = 2048
VMEM_LIMIT = 56 * 1024 * 1024

GELU_IN = (math.sqrt(2.0 / math.pi) * 0.044715) ** (1.0 / 3.0)
GELU_OUT = 0.5 / GELU_IN
GELU_LINEAR = math.sqrt(2.0 / math.pi) / GELU_IN


def bend(s):
    return s * (1.0 + jnp.tanh(s * (GELU_LINEAR + s * s)))


def split(x):
    high = x.astype(BF16)
    low = (x - high.astype(F32)).astype(BF16)
    return high, low


def dot(a, b):
    return jnp.dot(a, b, preferred_element_type=F32)


def rows_of(parts):
    return jnp.concatenate(parts, axis=0)


def lanes_of(parts):
    return jnp.concatenate(parts, axis=1)


def normed(x):
    shifted = x - jnp.mean(x, axis=-1, keepdims=True)
    spread = jnp.sum(shifted * shifted, axis=-1, keepdims=True)
    return shifted * lax.rsqrt(spread + CHANNELS * EPSILON)


def gained(weight, gain):
    column = jnp.broadcast_to(gain * math.sqrt(CHANNELS), (CHANNELS, CHANNELS)).T
    return lanes_of([weight[:, c : c + 128] * column for c in range(0, weight.shape[1], 128)])


def three(x):
    high, low = split(x)
    return lanes_of([high, low, high])


def stack_rows(weight):
    high, low = split(weight)
    return rows_of([high, high, low])


def deep_weight(weight):
    return lanes_of(split(weight))


def prepare_attention(qkv_ref, out_ref, gain, k3, qv3, out3):
    scale = math.log2(math.e) / math.sqrt(HEAD_DIM)
    k3[...] = stack_rows(gained(qkv_ref[0, :, CHANNELS : 2 * CHANNELS], gain))
    row_gain = gain * math.sqrt(CHANNELS)
    queries = qkv_ref[0, :, :CHANNELS].T * (row_gain * scale)
    values = qkv_ref[0, :, 2 * CHANNELS :].T * row_gain
    high, low = split(rows_of([queries, values]))
    qv3[...] = lanes_of([high, high, low])
    out3[...] = stack_rows(out_ref[0])


def prepare_feed(in_ref, mlp_ref, gain, in3, mlp_pair):
    in3[...] = stack_rows(gained(GELU_IN * in_ref[0], gain))
    mlp_pair[...] = deep_weight(GELU_OUT * mlp_ref[0])


PAIR = 2 * CELLS
PART = 512


def attend(pairs, k3, qv3, out3):
    left = lax.broadcasted_iota(jnp.int32, (HEAD_DIM, PAIR), 1) < CELLS
    left_all = lax.broadcasted_iota(jnp.int32, (CHANNELS, PAIR), 1) < CELLS
    zero = jnp.zeros((HEAD_DIM, PAIR), BF16)
    zero_block = jnp.zeros((2 * HEAD_DIM, PAIR), BF16)
    natural, turned = [], []
    for x in pairs:
        high, low = split(normed(x))
        natural.append(lanes_of([high, low, high]))
        high, low = high.T, low.T
        turned.append(rows_of([high, low, high]))
    yield
    keys = dot(rows_of(natural), k3[...])
    both = dot(qv3[...], lanes_of(turned))
    yield
    sides, value_sides = [], []

    def by_heads(straight, swapped):
        blocks = []
        for group in range(2):
            at = [slice(h * HEAD_DIM, (h + 1) * HEAD_DIM) for h in (2 * group, 2 * group + 1)]
            block = rows_of(
                [jnp.where(left, straight[at[0]], zero), jnp.where(left, zero, swapped[at[1]])]
            )
            blocks.append(lanes_of([zero_block, block] if group else [block, zero_block]))
        return rows_of(blocks)

    for p in range(len(pairs)):
        at = slice(p * PAIR, (p + 1) * PAIR)
        key3 = three(keys[at])
        high, low = split(both[:CHANNELS, at])
        high_swapped, low_swapped = pltpu.roll(high, CELLS, 1), pltpu.roll(low, CELLS, 1)
        for second in range(2):
            if second:
                h, l = by_heads(high_swapped, high), by_heads(low_swapped, low)
            else:
                h, l = by_heads(high, high_swapped), by_heads(low, low_swapped)
            sides.append((key3[second * CELLS : (second + 1) * CELLS], rows_of([h, h, l])))
        high, low = split(both[CHANNELS:, at])
        low = pltpu.roll(low, CELLS, 1)
        first, second = jnp.where(left_all, high, low), jnp.where(left_all, low, high)
        value_sides += [lanes_of([first, first]), lanes_of([second, second])]
    yield
    scores = [dot(key, query) for key, query in sides]
    yield
    weights, scales = [], []
    for score in scores:
        weight = jnp.exp2(score - jnp.max(score, axis=0, keepdims=True))
        scales.append(1.0 / jnp.sum(weight, axis=0, keepdims=True))
        high, low = split(weight)
        weights.append(rows_of([high, high, low, low]))
    yield
    mixed = [
        [dot(value[64 * g : 64 * g + 64], weight[:, 128 * g : 128 * g + 128]) for g in range(2)]
        for value, weight in zip(value_sides, weights)
    ]
    yield
    blended = []
    for p in range(len(pairs)):
        parts = []
        for h in range(HEADS):
            lanes = slice(128 * (h // 2), 128 * (h // 2) + 128)
            at = slice((h % 2) * HEAD_DIM, (h % 2 + 1) * HEAD_DIM)
            of_a, of_b = (
                mixed[2 * p + i][h // 2][at] * scales[2 * p + i][:, lanes] for i in range(2)
            )
            if h % 2:
                of_a = pltpu.roll(of_a, CELLS, 1)
            else:
                of_b = pltpu.roll(of_b, CELLS, 1)
            parts.append(jnp.where(left, of_a, of_b))
        blended.append(three(rows_of(parts).T))
    yield
    added = dot(rows_of(blended), out3[...])
    yield
    return [x + added[p * PAIR : (p + 1) * PAIR] for p, x in enumerate(pairs)]


def feed(pairs, in3, mlp_pair):
    parts = [three(normed(x)) for x in pairs]
    yield
    inner = dot(rows_of(parts), in3[...])
    yield
    high, low = split_blocks(inner, 64, bend)
    yield
    wide = dot(high, mlp_pair[...])
    rest = dot(low, mlp_pair[:, :CHANNELS])
    yield
    out = []
    for p, x in enumerate(pairs):
        at = slice(p * PAIR, (p + 1) * PAIR)
        out.append(x + (wide[at, :CHANNELS] + (wide[at, CHANNELS:] + rest[at])))
    return out


def staggered(groups):
    waiting, running = list(groups), []
    while waiting or running:
        if waiting:
            running.append(waiting.pop(0))
        for group in list(running):
            try:
                next(group)
            except StopIteration:
                running.remove(group)


def split_blocks(x, rows, make):
    highs, lows = [], []
    for r in range(0, x.shape[0], rows):
        made = [split(make(x[r : r + rows, c : c + 128])) for c in range(0, x.shape[1], 128)]
        highs.append(lanes_of([m[0] for m in made]))
        lows.append(lanes_of([m[1] for m in made]))
    return rows_of(highs), rows_of(lows)


def column_weights():
    fine = np.zeros((WIDE, COARSE_WIDE), np.float32)
    table = ((0.375, 0.625, 0.0), (0.125, 0.875, 0.0), (0.0, 0.875, 0.125), (0.0, 0.625, 0.375))

    def fill(at, column):
        k, o = column // 4, column % 4
        for step, weight in zip((-1, 0, 1), table[o]):
            if weight:
                fine[at, (k + step) % 40] = weight

    for column in range(128):
        fill(8 * (column % 16) + column // 16, column)
    fill(128, -1)
    fill(135, 128)
    return np.concatenate([fine, fine], axis=1)


ROW_WEIGHTS = ((0.375, 0.625, -1), (0.125, 0.875, -1), (0.875, 0.125, 0), (0.625, 0.375, 0))


def lift_kernel(
    place_ref, field_ref, context_ref, rows_a_ref, rows_b_ref, cols_a_ref, cols_b_ref, up_ref,
    ctxw_ref, gains_ref, expand_ref, depth_ref, reduce_ref, lifted_ref, active_ref, sum_ref,
    field, ends, sides, lift, ctx, coarse, hid, expand3, total, sems,
):
    step = pl.program_id(0)

    def arrival(k):
        at = pl.ds(0, 9) if k == 0 else pl.ds(8 * k + 1, 8 if k < 3 else 7)
        return pltpu.make_async_copy(field_ref.at[at], field.at[at], sems.at[k])

    sublane = lax.broadcasted_iota(jnp.int32, (8, 128), 0)
    first_row, last_row = sublane == 0, sublane == 7

    @pl.when(step == 0)
    def _():
        for k in range(4):
            arrival(k).start()
        expand3[...] = stack_rows(gained(GELU_IN * expand_ref[...], gains_ref[0:1]))
        total[...] = jnp.zeros_like(total)
        ctx[1:9, :32] = context_ref[...]

        def take_rows(above_ref, below_ref):
            for t in range(16):
                ends[0, 8 * t : 8 * t + 8] = above_ref[pl.ds(t, 8, stride=16), :]
                ends[1, 8 * t : 8 * t + 8] = below_ref[pl.ds(t, 8, stride=16), :]
            ctx[0, :32] = above_ref[128:]
            ctx[9, :32] = below_ref[128:]

        def take_columns(before_ref, after_ref):
            zero = jnp.zeros((8, 128), F32)
            for e in range(44):
                after = jnp.broadcast_to(after_ref[e : e + 1], (8, 128))
                before = jnp.broadcast_to(before_ref[e : e + 1], (8, 128))
                if e < 34:
                    sides[e] = jnp.where(first_row, before, jnp.where(last_row, after, zero))
                else:
                    ctx[e - 34, 32:40] = jnp.where(
                        first_row, after, jnp.where(last_row, before, zero)
                    )
                    ctx[e - 34, 40:] = zero

        pl.when(place_ref[0] % 2 == 0)(lambda: take_rows(rows_b_ref, rows_a_ref))
        pl.when(place_ref[0] % 2 == 1)(lambda: take_rows(rows_a_ref, rows_b_ref))
        pl.when(place_ref[1] % 2 == 0)(lambda: take_columns(cols_b_ref, cols_a_ref))
        pl.when(place_ref[1] % 2 == 1)(lambda: take_columns(cols_a_ref, cols_b_ref))
        weight = stack_rows(ctxw_ref[...])
        projected = dot(three(ctx[...].reshape(10 * COARSE_WIDE, CHANNELS)), weight)
        for k in range(10):
            high, low = split(projected[COARSE_WIDE * k : COARSE_WIDE * (k + 1)])
            coarse[k] = dot(up_ref[...], rows_of([high, low]))

    has_after = jnp.where(place_ref[1] < 7, 1.0, 0.0)
    has_before = jnp.where(place_ref[1] > 0, 1.0, 0.0)
    inside = jnp.where(first_row, has_before, has_after)

    for k in range(4):
        pl.when(step == k)(lambda k=k: arrival(k).wait())

    def hidden_rows(first, fine_first, k_first, count):
        parts = []
        for i in range(0, count, 2):
            two = []
            for j in (i, i + 1):
                k, o = (fine_first + j) // 4, (fine_first + j) % 4
                lower, upper, shift = ROW_WEIGHTS[o]
                at = k_first + k + shift
                up = lower * coarse[at] + upper * coarse[at + 1]
                if fine_first + j < 0:
                    own = ends[0]
                else:
                    f = jnp.minimum(first + j - 1, 31)
                    own = rows_of([field[f, pl.ds(t, 8, stride=16), :] for t in range(16)])
                    if fine_first + j == 8:
                        own = jnp.where(step == 3, ends[1], own)
                x = rows_of([own, sides[first + j]]) + up
                lift[first + j] = x[:128]
                two.append(x)
            parts.append(three(normed(rows_of(two))))
        made = dot(rows_of(parts), expand3[...])
        for i in range(count):
            for c in range(0, EXPANDED, 128):
                out = bend(made[i * WIDE : (i + 1) * WIDE, c : c + 128])
                hid[first + i, :128, c : c + 128] = out[:128]
                hid[first + i, 128:, c : c + 128] = out[128:] * inside

    @pl.when(step == 0)
    def _():
        hidden_rows(0, -1, 1, 2)

        @pl.when(place_ref[0] == 0)
        def _():
            hid[0] = jnp.zeros((WIDE, EXPANDED), F32)

    hidden_rows(8 * step + 2, 1, 2 * step + 1, 4)
    hidden_rows(8 * step + 6, 5, 2 * step + 1, 4)

    @pl.when((step == 3) & (place_ref[0] == 15))
    def _():
        hid[33] = jnp.zeros((WIDE, EXPANDED), F32)

    lifted_ref[...] = lift[pl.ds(8 * step + 1, 8)]

    for part in range(EXPANDED // 128):
        lanes = slice(part * 128, (part + 1) * 128)
        taps = [
            [jnp.broadcast_to((GELU_IN * GELU_OUT) * depth_ref[i, j : j + 1, lanes], (8, 128)) for j in range(3)]
            for i in range(3)
        ]

        def row(r, summed):
            def column(t):
                seen = [hid[8 * step + r + i, 8 * t : 8 * t + 8, lanes] for i in range(3)]
                return [
                    seen[0] * taps[0][j] + seen[1] * taps[1][j] + seen[2] * taps[2][j]
                    for j in range(3)
                ]

            first, last, halo = column(0), column(15), column(16)
            before = jnp.where(first_row, halo[0], pltpu.roll(last[0], 1, 0))
            end = jnp.where(last_row, halo[2], pltpu.roll(first[2], 7, 0))
            here = first
            for t in range(16):
                following = column(t + 1) if t < 14 else last
                out = bend(here[1] + before + (following[2] if t < 15 else end))
                active_ref[r, part, 8 * t : 8 * t + 8] = out
                summed = summed + out
                before, here = here[0], following
            return summed

        summed = total[:, lanes]
        for r in range(8):
            summed = row(r, summed)
        total[:, lanes] = summed

    @pl.when(step == 3)
    def _():
        squeezed = lax.dot_general(
            total[...], reduce_ref[...], (((1,), (1,)), ((), ())), precision=HIGHEST,
            preferred_element_type=F32,
        )
        squeezed = jnp.sum(squeezed, axis=0, keepdims=True)
        padded = lanes_of([squeezed, jnp.zeros((1, 128 - SQUEEZE), F32)])
        sum_ref[...] = jnp.broadcast_to(padded, sum_ref.shape)


def whole(shape):
    return pl.BlockSpec(shape, lambda *_: (0,) * len(shape))


def of_layer(array, layer):
    shape = (1,) + array.shape[1:]
    return pl.BlockSpec(shape, lambda *_: (layer,) + (0,) * (len(shape) - 1))


def lift_stage(place, args, copies):
    up = jnp.asarray(column_weights(), BF16)
    args = args[:6] + (up,) + args[6:]
    return pl.pallas_call(
        lift_kernel,
        grid=(4,),
        in_specs=[pl.BlockSpec(memory_space=pltpu.SMEM), pl.BlockSpec(memory_space=pl.ANY)]
        + [whole(a.shape) for a in args[1:]],
        out_specs=[
            pl.BlockSpec((8, 128, CHANNELS), lambda s: (s, 0, 0)),
            pl.BlockSpec((8, EXPANDED // 128, 128, 128), lambda s: (s, 0, 0, 0)),
            whole((copies, 128)),
        ],
        out_shape=[
            jax.ShapeDtypeStruct((32, 128, CHANNELS), F32),
            jax.ShapeDtypeStruct((32, EXPANDED // 128, 128, 128), F32),
            jax.ShapeDtypeStruct((copies, 128), F32),
        ],
        scratch_shapes=[
            pltpu.VMEM((32, 128, CHANNELS), F32),
            pltpu.VMEM((2, 128, CHANNELS), F32),
            pltpu.VMEM((34, 8, CHANNELS), F32),
            pltpu.VMEM((34, 128, CHANNELS), F32),
            pltpu.VMEM((10, COARSE_WIDE, CHANNELS), F32),
            pltpu.VMEM((10, WIDE, CHANNELS), F32),
            pltpu.VMEM((34, WIDE, EXPANDED), F32),
            pltpu.VMEM((3 * CHANNELS, EXPANDED), BF16),
            pltpu.VMEM((8, EXPANDED), F32),
            pltpu.SemaphoreType.DMA((4,)),
        ],
        compiler_params=pltpu.CompilerParams(vmem_limit_bytes=VMEM_LIMIT),
        cost_estimate=pl.CostEstimate(
            flops=8_000_000_000, bytes_accessed=14_000_000, transcendentals=0
        ),
    )(place, *args)


def block_kernel(
    cells_total, fed, lifted_ref, active_ref, sums_ref, sexp_ref, project_ref, gains_ref, qkv_ref,
    aout_ref, min_ref, mout_ref, out_ref, project, k3, qv3, out3, *feed_weights,
):
    @pl.when(pl.program_id(0) == 0)
    def _():
        pooled = jnp.sum(sums_ref[...], axis=0, keepdims=True) * (GELU_OUT / cells_total)
        squeezed = pooled[:, :SQUEEZE]
        squeezed = squeezed * jax.nn.sigmoid(squeezed)
        wide = jnp.broadcast_to(squeezed, (CHANNELS, SQUEEZE))
        gate = jnp.dot(wide, sexp_ref[...], precision=HIGHEST, preferred_element_type=F32)
        project[...] = deep_weight(project_ref[...] * (GELU_OUT * jax.nn.sigmoid(gate)).T)
        prepare_attention(qkv_ref, aout_ref, gains_ref[1:2], k3, qv3, out3)
        if fed:
            prepare_feed(min_ref, mout_ref, gains_ref[2:3], *feed_weights)

    def window(w, load):
        at = pl.ds(64 * (w % 2) + w // 2, WINDOW, stride=8)
        return rows_of([load(r, at) for r in range(WINDOW)])

    def expanded(r, at):
        return lanes_of([active_ref[r, k, at, :] for k in range(EXPANDED // 128)])

    def projected(start):
        halves = [split(window(w, expanded)) for w in range(start, start + PART // CELLS)]
        yield
        wide = dot(rows_of([h[0] for h in halves]), project[...])
        rest = dot(rows_of([h[1] for h in halves]), project[:, :CHANNELS])
        yield
        pairs = []
        for p in range(PART // PAIR):
            at = slice(p * PAIR, (p + 1) * PAIR)
            x = rows_of(
                [window(start + 2 * p + i, lambda r, at: lifted_ref[r, at, :]) for i in range(2)]
            )
            pairs.append(x + (wide[at, :CHANNELS] + (wide[at, CHANNELS:] + rest[at])))
        return pairs

    def group(part):
        pairs = yield from projected(part * PART // CELLS)
        pairs = yield from attend(pairs, k3, qv3, out3)
        if fed:
            pairs = yield from feed(pairs, *feed_weights)
        for p, x in enumerate(pairs):
            out_ref[part * PART + p * PAIR : part * PART + (p + 1) * PAIR] = x

    staggered(group(part) for part in range(BLOCK_STEP // PART))


ATTENTION_SCRATCH = [
    pltpu.VMEM((3 * CHANNELS, CHANNELS), BF16),
    pltpu.VMEM((2 * CHANNELS, 3 * CHANNELS), BF16),
    pltpu.VMEM((3 * CHANNELS, CHANNELS), BF16),
]
FEED_SCRATCH = [
    pltpu.VMEM((3 * CHANNELS, MLP_HIDDEN), BF16),
    pltpu.VMEM((MLP_HIDDEN, 2 * CHANNELS), BF16),
]


def block_stage(chunk, fed, lifted, active, sums, se_expand, project, gains, weights, cells_total):
    steps = 4 // CHUNKS
    row_base = chunk * (4 // CHUNKS)
    rest = (sums, se_expand, project, gains)

    columns = BLOCK_STEP // 8
    strips = [
        pl.BlockSpec((8, columns, CHANNELS), lambda s: (row_base + s, 0, 0)),
        pl.BlockSpec((8, EXPANDED // 128, columns, 128), lambda s: (row_base + s, 0, 0, 0)),
    ]

    def body(*refs):
        block_kernel(cells_total, fed, *refs)

    return pl.pallas_call(
        body,
        grid=(steps,),
        in_specs=strips
        + [whole(a.shape) for a in rest]
        + [of_layer(w, 0) for w in weights],
        out_specs=pl.BlockSpec((BLOCK_STEP, CHANNELS), lambda s: (s, 0)),
        out_shape=jax.ShapeDtypeStruct((steps * BLOCK_STEP, CHANNELS), F32),
        scratch_shapes=[
            pltpu.VMEM((EXPANDED, 2 * CHANNELS), BF16),
        ]
        + ATTENTION_SCRATCH
        + (FEED_SCRATCH if fed else []),
        compiler_params=pltpu.CompilerParams(vmem_limit_bytes=VMEM_LIMIT),
        cost_estimate=pl.CostEstimate(
            flops=14_000_000_000, bytes_accessed=8_000_000, transcendentals=0
        ),
    )(lifted, active, *rest, *weights)


def grid_kernel(fed, x_ref, gains_ref, *refs):
    scratch = 5 if fed else 7
    out_ref, k3, qv3, out3, *feeds = refs[-scratch - 1 :]
    qkv_ref, aout_ref, *feed_refs = refs[: 4 if fed else 6]

    @pl.when(pl.program_id(0) == 0)
    def _():
        prepare_attention(qkv_ref, aout_ref, gains_ref[3:4], k3, qv3, out3)
        prepare_feed(*feed_refs[:2], gains_ref[4:5], *feeds[:2])
        if not fed:
            prepare_feed(*feed_refs[2:], gains_ref[2:3], *feeds[2:])

    stride = GRID_STEP // GROUP
    flat_in = x_ref.reshape(GRID_STEP, CHANNELS)
    flat_out = out_ref.reshape(GRID_STEP, CHANNELS)

    def group(part):
        first = part * PART // GROUP
        windows = [flat_in[pl.ds(first + p, GROUP, stride=stride), :] for p in range(PART // GROUP)]
        pairs = [rows_of(windows[i : i + 2]) for i in range(0, len(windows), 2)]
        if not fed:
            pairs = yield from feed(pairs, *feeds[2:])
        pairs = yield from attend(pairs, k3, qv3, out3)
        pairs = yield from feed(pairs, *feeds[:2])
        for p, x in enumerate(pairs):
            for i in range(2):
                window = first + 2 * p + i
                flat_out[pl.ds(window, GROUP, stride=stride), :] = x[i * GROUP : (i + 1) * GROUP]

    staggered(group(part) for part in range(GRID_STEP // PART))


def grid_stage(received, fed, gains, weights, chunk, earlier):
    per_device = received.shape[1]
    steps = per_device * GROUP // GRID_STEP
    shape = (GROUP, GRID_STEP // GROUP, CHANNELS)
    in_specs = [pl.BlockSpec(shape, lambda s: (0, s, 0)), whole(gains.shape)]
    in_specs += [of_layer(w, 1) for w in weights]
    args = (received, gains) + weights
    if not fed:
        in_specs += [of_layer(w, 0) for w in weights[2:]]
        args += weights[2:]
    aliases = {}
    if earlier is not None:
        in_specs.append(pl.BlockSpec(memory_space=pl.ANY))
        aliases = {len(args): 0}
        args += (earlier,)

    def body(*refs):
        grid_kernel(fed, *refs)

    return pl.pallas_call(
        body,
        grid=(steps,),
        in_specs=in_specs,
        out_specs=pl.BlockSpec(shape, lambda s: (0, chunk * steps + s, 0)),
        out_shape=jax.ShapeDtypeStruct((GROUP, CHUNKS * per_device, CHANNELS), F32),
        scratch_shapes=ATTENTION_SCRATCH + FEED_SCRATCH + ([] if fed else FEED_SCRATCH),
        input_output_aliases=aliases,
        compiler_params=pltpu.CompilerParams(vmem_limit_bytes=VMEM_LIMIT),
        cost_estimate=pl.CostEstimate(
            flops=14_000_000_000, bytes_accessed=4_000_000, transcendentals=0
        ),
    )(*args)


def by_pairs(edge, at, axis, count):
    even = at % 2 == 0
    swaps = []
    for first, last in ((1, jnp.logical_not(even)), (0, even)):
        lower = [(i, i + 1) for i in range(first, count - 1, 2)]
        pairs = lower + [(b, a) for a, b in lower]
        swaps.append(lax.ppermute(edge(last), axis, pairs))
    return swaps[::-1]


def per_device(
    field, context, ctx_weight, norm_gains, expand_weight, depth_weight, se_reduce, se_expand,
    project_weight, attn_qkv, attn_out, mlp_in, mlp_out,
):
    row_axis = ("rg", "core")
    rows, cols = 16, 8
    row = lax.axis_index(row_axis)
    col = lax.axis_index("col")

    def row_edge(last):
        fine = lax.dynamic_index_in_dim(field, jnp.where(last, 31, 0), 0, keepdims=False)
        of_context = lax.dynamic_index_in_dim(context, jnp.where(last, 7, 0), 0, keepdims=False)
        return jnp.concatenate([fine, of_context], axis=0)

    rows_a, rows_b = by_pairs(row_edge, row, row_axis, rows)
    odd = row % 2 == 1

    def column_edge(last):
        fine_at, coarse_at = jnp.where(last, 127, 0), jnp.where(last, 31, 0)

        def one(x, at):
            return lax.dynamic_slice_in_dim(x, at, 1, axis=x.ndim - 2).reshape(-1, CHANNELS)

        parts = []
        for start, stop, tile, at in ((0, 128, field, fine_at), (128, 160, context, coarse_at)):
            of_a, of_b = one(rows_a[start:stop], at), one(rows_b[start:stop], at)
            parts += [jnp.where(odd, of_a, of_b), one(tile, at), jnp.where(odd, of_b, of_a)]
        return jnp.concatenate(parts, axis=0)

    cols_a, cols_b = by_pairs(column_edge, col, "col", cols)
    place = jnp.stack([row, col]).astype(jnp.int32)
    lifted, active, partial = lift_stage(
        place,
        (
            field, context, rows_a, rows_b, cols_a, cols_b, ctx_weight, norm_gains, expand_weight,
            depth_weight, se_reduce.T,
        ),
        rows * cols,
    )

    def exchange(x, axes):
        return lax.all_to_all(x, axes, split_axis=0, concat_axis=0, tiled=True)

    group = ("rg", "col")
    sums = exchange(partial[:, None, :], ("rg", "core", "col"))[:, 0, :]

    weights = (attn_qkv, attn_out, mlp_in, mlp_out)
    cells_total = rows * cols * field.shape[0] * field.shape[1]
    sent = []
    for chunk in range(CHUNKS):
        mine = block_stage(
            chunk, chunk > 0, lifted, active, sums, se_expand, project_weight, norm_gains, weights,
            cells_total,
        )
        sent.append(exchange(mine.reshape(GROUP, -1, CHANNELS), group))
    attended = None
    for chunk in range(CHUNKS):
        attended = grid_stage(sent[chunk], chunk > 0, norm_gains, weights, chunk, attended)
    back = exchange(attended, group)
    halves = back.reshape(4 // CHUNKS, 16, 2, CHUNKS, WINDOW // 2, WINDOW, CHANNELS)
    return halves.transpose(3, 0, 2, 4, 1, 5, 6).reshape(field.shape)


def solution(mesh):
    fine = Mesh(mesh.devices.reshape(8, 2, 8), ("rg", "core", "col"))
    tiled = P(("rg", "core"), "col", None)
    return jax.shard_map(
        per_device,
        mesh=fine,
        in_specs=(tiled, tiled) + (P(),) * 11,
        out_specs=tiled,
        check_vma=False,
    )
```

```python
import math

import jax
import jax.numpy as jnp
import numpy as np
from jax import lax
from jax.experimental import pallas as pl
from jax.experimental.pallas import tpu as pltpu
from jax.sharding import Mesh
from jax.sharding import PartitionSpec as P

HEADS = 4
WINDOW = 8
CHANNELS = 128
EXPANDED = 512
MLP_HIDDEN = 512
SQUEEZE = 32
HEAD_DIM = CHANNELS // HEADS
CELLS = WINDOW * WINDOW
GROUP = 64
WIDE = 136
COARSE_WIDE = 48
EPSILON = 1e-05
F32 = jnp.float32
BF16 = jnp.bfloat16
HIGHEST = lax.Precision.HIGHEST
CHUNKS = 2
BLOCK_STEP = 1024
GRID_STEP = 2048
VMEM_LIMIT = 56 * 1024 * 1024

GELU_IN = (math.sqrt(2.0 / math.pi) * 0.044715) ** (1.0 / 3.0)
GELU_OUT = 0.5 / GELU_IN
GELU_LINEAR = math.sqrt(2.0 / math.pi) / GELU_IN


def bend(s):
    return s * (1.0 + jnp.tanh(s * (GELU_LINEAR + s * s)))


def split(x):
    high = x.astype(BF16)
    low = (x - high.astype(F32)).astype(BF16)
    return high, low


def dot(a, b):
    return jnp.dot(a, b, preferred_element_type=F32)


def rows_of(parts):
    return jnp.concatenate(parts, axis=0)


def lanes_of(parts):
    return jnp.concatenate(parts, axis=1)


def normed(x):
    shifted = x - jnp.mean(x, axis=-1, keepdims=True)
    spread = jnp.sum(shifted * shifted, axis=-1, keepdims=True)
    return shifted * lax.rsqrt(spread + CHANNELS * EPSILON)


def gained(weight, gain):
    column = jnp.broadcast_to(gain * math.sqrt(CHANNELS), (CHANNELS, CHANNELS)).T
    return lanes_of([weight[:, c : c + 128] * column for c in range(0, weight.shape[1], 128)])


def three(x):
    high, low = split(x)
    return lanes_of([high, low, high])


def stack_rows(weight):
    high, low = split(weight)
    return rows_of([high, high, low])


def deep_weight(weight):
    return lanes_of(split(weight))


def prepare_attention(qkv_ref, out_ref, gain, k3, qv3, out3):
    scale = math.log2(math.e) / math.sqrt(HEAD_DIM)
    k3[...] = stack_rows(gained(qkv_ref[0, :, CHANNELS : 2 * CHANNELS], gain))
    row_gain = gain * math.sqrt(CHANNELS)
    queries = qkv_ref[0, :, :CHANNELS].T * (row_gain * scale)
    values = qkv_ref[0, :, 2 * CHANNELS :].T * row_gain
    high, low = split(rows_of([queries, values]))
    qv3[...] = lanes_of([high, high, low])
    out3[...] = stack_rows(out_ref[0])


def prepare_feed(in_ref, mlp_ref, gain, in3, mlp_pair):
    in3[...] = stack_rows(gained(GELU_IN * in_ref[0], gain))
    mlp_pair[...] = deep_weight(GELU_OUT * mlp_ref[0])


PAIR = 2 * CELLS
PART = 512


def attend(pairs, k3, qv3, out3):
    left = lax.broadcasted_iota(jnp.int32, (HEAD_DIM, PAIR), 1) < CELLS
    left_all = lax.broadcasted_iota(jnp.int32, (CHANNELS, PAIR), 1) < CELLS
    zero = jnp.zeros((HEAD_DIM, PAIR), BF16)
    zero_block = jnp.zeros((2 * HEAD_DIM, PAIR), BF16)
    natural, turned = [], []
    for x in pairs:
        high, low = split(normed(x))
        natural.append(lanes_of([high, low, high]))
        high, low = high.T, low.T
        turned.append(rows_of([high, low, high]))
    yield
    keys = dot(rows_of(natural), k3[...])
    both = dot(qv3[...], lanes_of(turned))
    yield
    sides, value_sides = [], []

    def by_heads(straight, swapped):
        blocks = []
        for group in range(2):
            at = [slice(h * HEAD_DIM, (h + 1) * HEAD_DIM) for h in (2 * group, 2 * group + 1)]
            block = rows_of(
                [jnp.where(left, straight[at[0]], zero), jnp.where(left, zero, swapped[at[1]])]
            )
            blocks.append(lanes_of([zero_block, block] if group else [block, zero_block]))
        return rows_of(blocks)

    for p in range(len(pairs)):
        at = slice(p * PAIR, (p + 1) * PAIR)
        key3 = three(keys[at])
        high, low = split(both[:CHANNELS, at])
        high_swapped, low_swapped = pltpu.roll(high, CELLS, 1), pltpu.roll(low, CELLS, 1)
        for second in range(2):
            if second:
                h, l = by_heads(high_swapped, high), by_heads(low_swapped, low)
            else:
                h, l = by_heads(high, high_swapped), by_heads(low, low_swapped)
            sides.append((key3[second * CELLS : (second + 1) * CELLS], rows_of([h, h, l])))
        high, low = split(both[CHANNELS:, at])
        low = pltpu.roll(low, CELLS, 1)
        first, second = jnp.where(left_all, high, low), jnp.where(left_all, low, high)
        value_sides += [lanes_of([first, first]), lanes_of([second, second])]
    yield
    scores = [dot(key, query) for key, query in sides]
    yield
    weights, scales = [], []
    for score in scores:
        weight = jnp.exp2(score - jnp.max(score, axis=0, keepdims=True))
        scales.append(1.0 / jnp.sum(weight, axis=0, keepdims=True))
        high, low = split(weight)
        weights.append(rows_of([high, high, low, low]))
    yield
    mixed = [
        [dot(value[64 * g : 64 * g + 64], weight[:, 128 * g : 128 * g + 128]) for g in range(2)]
        for value, weight in zip(value_sides, weights)
    ]
    yield
    blended = []
    for p in range(len(pairs)):
        parts = []
        for h in range(HEADS):
            lanes = slice(128 * (h // 2), 128 * (h // 2) + 128)
            at = slice((h % 2) * HEAD_DIM, (h % 2 + 1) * HEAD_DIM)
            of_a, of_b = (
                mixed[2 * p + i][h // 2][at] * scales[2 * p + i][:, lanes] for i in range(2)
            )
            if h % 2:
                of_a = pltpu.roll(of_a, CELLS, 1)
            else:
                of_b = pltpu.roll(of_b, CELLS, 1)
            parts.append(jnp.where(left, of_a, of_b))
        blended.append(three(rows_of(parts).T))
    yield
    added = dot(rows_of(blended), out3[...])
    yield
    return [x + added[p * PAIR : (p + 1) * PAIR] for p, x in enumerate(pairs)]


def feed(pairs, in3, mlp_pair):
    parts = [three(normed(x)) for x in pairs]
    yield
    inner = dot(rows_of(parts), in3[...])
    yield
    high, low = split_blocks(inner, 64, bend)
    yield
    wide = dot(high, mlp_pair[...])
    rest = dot(low, mlp_pair[:, :CHANNELS])
    yield
    out = []
    for p, x in enumerate(pairs):
        at = slice(p * PAIR, (p + 1) * PAIR)
        out.append(x + (wide[at, :CHANNELS] + (wide[at, CHANNELS:] + rest[at])))
    return out


def staggered(groups):
    waiting, running = list(groups), []
    while waiting or running:
        if waiting:
            running.append(waiting.pop(0))
        for group in list(running):
            try:
                next(group)
            except StopIteration:
                running.remove(group)


def split_blocks(x, rows, make):
    highs, lows = [], []
    for r in range(0, x.shape[0], rows):
        made = [split(make(x[r : r + rows, c : c + 128])) for c in range(0, x.shape[1], 128)]
        highs.append(lanes_of([m[0] for m in made]))
        lows.append(lanes_of([m[1] for m in made]))
    return rows_of(highs), rows_of(lows)


def column_weights():
    fine = np.zeros((WIDE, COARSE_WIDE), np.float32)
    table = ((0.375, 0.625, 0.0), (0.125, 0.875, 0.0), (0.0, 0.875, 0.125), (0.0, 0.625, 0.375))

    def fill(at, column):
        k, o = column // 4, column % 4
        for step, weight in zip((-1, 0, 1), table[o]):
            if weight:
                fine[at, (k + step) % 40] = weight

    for column in range(128):
        fill(8 * (column % 16) + column // 16, column)
    fill(128, -1)
    fill(135, 128)
    return np.concatenate([fine, fine], axis=1)


ROW_WEIGHTS = ((0.375, 0.625, -1), (0.125, 0.875, -1), (0.875, 0.125, 0), (0.625, 0.375, 0))


def lift_kernel(
    place_ref, field_ref, context_ref, rows_a_ref, rows_b_ref, cols_a_ref, cols_b_ref, up_ref,
    ctxw_ref, gains_ref, expand_ref, depth_ref, reduce_ref, lifted_ref, active_hbm, sum_ref,
    active, field, ends, sides, lift, ctx, coarse, hid, expand3, total, sems, leave_sems,
):
    step = pl.program_id(0)

    def arrival(k):
        at = pl.ds(0, 9) if k == 0 else pl.ds(8 * k + 1, 8 if k < 3 else 7)
        return pltpu.make_async_copy(field_ref.at[at], field.at[at], sems.at[k])

    def leaving(k, part):
        at = (pl.ds(8 * k, 8), part)
        return pltpu.make_async_copy(active.at[at], active_hbm.at[at], leave_sems.at[k, part])

    sublane = lax.broadcasted_iota(jnp.int32, (8, 128), 0)
    first_row, last_row = sublane == 0, sublane == 7

    @pl.when(step == 0)
    def _():
        for k in range(4):
            arrival(k).start()
        expand3[...] = stack_rows(gained(GELU_IN * expand_ref[...], gains_ref[0:1]))
        total[...] = jnp.zeros_like(total)
        ctx[1:9, :32] = context_ref[...]

        def take_rows(above_ref, below_ref):
            for t in range(16):
                ends[0, 8 * t : 8 * t + 8] = above_ref[pl.ds(t, 8, stride=16), :]
                ends[1, 8 * t : 8 * t + 8] = below_ref[pl.ds(t, 8, stride=16), :]
            ctx[0, :32] = above_ref[128:]
            ctx[9, :32] = below_ref[128:]

        def take_columns(before_ref, after_ref):
            zero = jnp.zeros((8, 128), F32)
            for e in range(44):
                after = jnp.broadcast_to(after_ref[e : e + 1], (8, 128))
                before = jnp.broadcast_to(before_ref[e : e + 1], (8, 128))
                if e < 34:
                    sides[e] = jnp.where(first_row, before, jnp.where(last_row, after, zero))
                else:
                    ctx[e - 34, 32:40] = jnp.where(
                        first_row, after, jnp.where(last_row, before, zero)
                    )
                    ctx[e - 34, 40:] = zero

        pl.when(place_ref[0] % 2 == 0)(lambda: take_rows(rows_b_ref, rows_a_ref))
        pl.when(place_ref[0] % 2 == 1)(lambda: take_rows(rows_a_ref, rows_b_ref))
        pl.when(place_ref[1] % 2 == 0)(lambda: take_columns(cols_b_ref, cols_a_ref))
        pl.when(place_ref[1] % 2 == 1)(lambda: take_columns(cols_a_ref, cols_b_ref))
        weight = stack_rows(ctxw_ref[...])
        projected = dot(three(ctx[...].reshape(10 * COARSE_WIDE, CHANNELS)), weight)
        for k in range(10):
            high, low = split(projected[COARSE_WIDE * k : COARSE_WIDE * (k + 1)])
            coarse[k] = dot(up_ref[...], rows_of([high, low]))

    has_after = jnp.where(place_ref[1] < 7, 1.0, 0.0)
    has_before = jnp.where(place_ref[1] > 0, 1.0, 0.0)
    inside = jnp.where(first_row, has_before, has_after)

    for k in range(4):
        pl.when(step == k)(lambda k=k: arrival(k).wait())

    def hidden_rows(first, fine_first, k_first, count):
        parts = []
        for i in range(0, count, 2):
            two = []
            for j in (i, i + 1):
                k, o = (fine_first + j) // 4, (fine_first + j) % 4
                lower, upper, shift = ROW_WEIGHTS[o]
                at = k_first + k + shift
                up = lower * coarse[at] + upper * coarse[at + 1]
                if fine_first + j < 0:
                    own = ends[0]
                else:
                    f = jnp.minimum(first + j - 1, 31)
                    own = rows_of([field[f, pl.ds(t, 8, stride=16), :] for t in range(16)])
                    if fine_first + j == 8:
                        own = jnp.where(step == 3, ends[1], own)
                x = rows_of([own, sides[first + j]]) + up
                lift[first + j] = x[:128]
                two.append(x)
            parts.append(three(normed(rows_of(two))))
        made = dot(rows_of(parts), expand3[...])
        for i in range(count):
            for c in range(0, EXPANDED, 128):
                out = bend(made[i * WIDE : (i + 1) * WIDE, c : c + 128])
                hid[first + i, :128, c : c + 128] = out[:128]
                hid[first + i, 128:, c : c + 128] = out[128:] * inside

    @pl.when(step == 0)
    def _():
        hidden_rows(0, -1, 1, 2)

        @pl.when(place_ref[0] == 0)
        def _():
            hid[0] = jnp.zeros((WIDE, EXPANDED), F32)

    hidden_rows(8 * step + 2, 1, 2 * step + 1, 4)
    hidden_rows(8 * step + 6, 5, 2 * step + 1, 4)

    @pl.when((step == 3) & (place_ref[0] == 15))
    def _():
        hid[33] = jnp.zeros((WIDE, EXPANDED), F32)

    lifted_ref[...] = lift[pl.ds(8 * step + 1, 8)]

    for part in range(EXPANDED // 128):
        lanes = slice(part * 128, (part + 1) * 128)
        taps = [
            [jnp.broadcast_to((GELU_IN * GELU_OUT) * depth_ref[i, j : j + 1, lanes], (8, 128)) for j in range(3)]
            for i in range(3)
        ]

        def row(r, summed):
            def column(t):
                seen = [hid[8 * step + r + i, 8 * t : 8 * t + 8, lanes] for i in range(3)]
                return [
                    seen[0] * taps[0][j] + seen[1] * taps[1][j] + seen[2] * taps[2][j]
                    for j in range(3)
                ]

            first, last, halo = column(0), column(15), column(16)
            before = jnp.where(first_row, halo[0], pltpu.roll(last[0], 1, 0))
            end = jnp.where(last_row, halo[2], pltpu.roll(first[2], 7, 0))
            here = first
            for t in range(16):
                following = column(t + 1) if t < 14 else last
                out = bend(here[1] + before + (following[2] if t < 15 else end))
                active[8 * step + r, part, 8 * t : 8 * t + 8] = out
                summed = summed + out
                before, here = here[0], following
            return summed

        summed = total[:, lanes]
        for r in range(8):
            summed = row(r, summed)
        total[:, lanes] = summed
        leaving(step, part).start()

    @pl.when(step == 3)
    def _():
        squeezed = lax.dot_general(
            total[...], reduce_ref[...], (((1,), (1,)), ((), ())), precision=HIGHEST,
            preferred_element_type=F32,
        )
        squeezed = jnp.sum(squeezed, axis=0, keepdims=True)
        padded = lanes_of([squeezed, jnp.zeros((1, 128 - SQUEEZE), F32)])
        sum_ref[...] = jnp.broadcast_to(padded, sum_ref.shape)
        for k in range(4):
            for part in range(4):
                leaving(k, part).wait()


def whole(shape):
    return pl.BlockSpec(shape, lambda *_: (0,) * len(shape))


def of_layer(array, layer):
    shape = (1,) + array.shape[1:]
    return pl.BlockSpec(shape, lambda *_: (layer,) + (0,) * (len(shape) - 1))


def lift_stage(place, args, copies):
    up = jnp.asarray(column_weights(), BF16)
    args = args[:6] + (up,) + args[6:]
    return pl.pallas_call(
        lift_kernel,
        grid=(4,),
        in_specs=[pl.BlockSpec(memory_space=pltpu.SMEM), pl.BlockSpec(memory_space=pl.ANY)]
        + [whole(a.shape) for a in args[1:]],
        out_specs=[
            pl.BlockSpec((8, 128, CHANNELS), lambda s: (s, 0, 0)),
            pl.BlockSpec(memory_space=pl.ANY),
            whole((copies, 128)),
        ],
        out_shape=[
            jax.ShapeDtypeStruct((32, 128, CHANNELS), F32),
            jax.ShapeDtypeStruct((32, EXPANDED // 128, 128, 128), F32),
            jax.ShapeDtypeStruct((copies, 128), F32),
        ],
        scratch_shapes=[
            pltpu.VMEM((32, EXPANDED // 128, 128, 128), F32),
            pltpu.VMEM((32, 128, CHANNELS), F32),
            pltpu.VMEM((2, 128, CHANNELS), F32),
            pltpu.VMEM((34, 8, CHANNELS), F32),
            pltpu.VMEM((34, 128, CHANNELS), F32),
            pltpu.VMEM((10, COARSE_WIDE, CHANNELS), F32),
            pltpu.VMEM((10, WIDE, CHANNELS), F32),
            pltpu.VMEM((34, WIDE, EXPANDED), F32),
            pltpu.VMEM((3 * CHANNELS, EXPANDED), BF16),
            pltpu.VMEM((8, EXPANDED), F32),
            pltpu.SemaphoreType.DMA((4,)),
            pltpu.SemaphoreType.DMA((4, 4)),
        ],
        compiler_params=pltpu.CompilerParams(vmem_limit_bytes=VMEM_LIMIT),
        cost_estimate=pl.CostEstimate(
            flops=8_000_000_000, bytes_accessed=14_000_000, transcendentals=0
        ),
    )(place, *args)


def block_kernel(
    cells_total, fed, lifted_ref, active_ref, sums_ref, sexp_ref, project_ref, gains_ref, qkv_ref,
    aout_ref, min_ref, mout_ref, out_ref, project, k3, qv3, out3, *feed_weights,
):
    @pl.when(pl.program_id(0) == 0)
    def _():
        pooled = jnp.sum(sums_ref[...], axis=0, keepdims=True) * (GELU_OUT / cells_total)
        squeezed = pooled[:, :SQUEEZE]
        squeezed = squeezed * jax.nn.sigmoid(squeezed)
        wide = jnp.broadcast_to(squeezed, (CHANNELS, SQUEEZE))
        gate = jnp.dot(wide, sexp_ref[...], precision=HIGHEST, preferred_element_type=F32)
        project[...] = deep_weight(project_ref[...] * (GELU_OUT * jax.nn.sigmoid(gate)).T)
        prepare_attention(qkv_ref, aout_ref, gains_ref[1:2], k3, qv3, out3)
        if fed:
            prepare_feed(min_ref, mout_ref, gains_ref[2:3], *feed_weights)

    def window(w, load):
        at = pl.ds(64 * (w % 2) + w // 2, WINDOW, stride=8)
        return rows_of([load(r, at) for r in range(WINDOW)])

    def expanded(r, at):
        return lanes_of([active_ref[r, k, at, :] for k in range(EXPANDED // 128)])

    def projected(start):
        halves = [split(window(w, expanded)) for w in range(start, start + PART // CELLS)]
        yield
        wide = dot(rows_of([h[0] for h in halves]), project[...])
        rest = dot(rows_of([h[1] for h in halves]), project[:, :CHANNELS])
        yield
        pairs = []
        for p in range(PART // PAIR):
            at = slice(p * PAIR, (p + 1) * PAIR)
            x = rows_of(
                [window(start + 2 * p + i, lambda r, at: lifted_ref[r, at, :]) for i in range(2)]
            )
            pairs.append(x + (wide[at, :CHANNELS] + (wide[at, CHANNELS:] + rest[at])))
        return pairs

    def group(part):
        pairs = yield from projected(part * PART // CELLS)
        pairs = yield from attend(pairs, k3, qv3, out3)
        if fed:
            pairs = yield from feed(pairs, *feed_weights)
        for p, x in enumerate(pairs):
            out_ref[part * PART + p * PAIR : part * PART + (p + 1) * PAIR] = x

    staggered(group(part) for part in range(BLOCK_STEP // PART))


ATTENTION_SCRATCH = [
    pltpu.VMEM((3 * CHANNELS, CHANNELS), BF16),
    pltpu.VMEM((2 * CHANNELS, 3 * CHANNELS), BF16),
    pltpu.VMEM((3 * CHANNELS, CHANNELS), BF16),
]
FEED_SCRATCH = [
    pltpu.VMEM((3 * CHANNELS, MLP_HIDDEN), BF16),
    pltpu.VMEM((MLP_HIDDEN, 2 * CHANNELS), BF16),
]


def block_stage(chunk, fed, lifted, active, sums, se_expand, project, gains, weights, cells_total):
    steps = 4 // CHUNKS
    row_base = chunk * (4 // CHUNKS)
    rest = (sums, se_expand, project, gains)

    columns = BLOCK_STEP // 8
    strips = [
        pl.BlockSpec((8, columns, CHANNELS), lambda s: (row_base + s, 0, 0)),
        pl.BlockSpec((8, EXPANDED // 128, columns, 128), lambda s: (row_base + s, 0, 0, 0)),
    ]

    def body(*refs):
        block_kernel(cells_total, fed, *refs)

    return pl.pallas_call(
        body,
        grid=(steps,),
        in_specs=strips
        + [whole(a.shape) for a in rest]
        + [of_layer(w, 0) for w in weights],
        out_specs=pl.BlockSpec((BLOCK_STEP, CHANNELS), lambda s: (s, 0)),
        out_shape=jax.ShapeDtypeStruct((steps * BLOCK_STEP, CHANNELS), F32),
        scratch_shapes=[
            pltpu.VMEM((EXPANDED, 2 * CHANNELS), BF16),
        ]
        + ATTENTION_SCRATCH
        + (FEED_SCRATCH if fed else []),
        compiler_params=pltpu.CompilerParams(vmem_limit_bytes=VMEM_LIMIT),
        cost_estimate=pl.CostEstimate(
            flops=14_000_000_000, bytes_accessed=8_000_000, transcendentals=0
        ),
    )(lifted, active, *rest, *weights)


def grid_kernel(fed, chunk, x_hbm, gains_ref, *refs):
    scratch = 8 if fed else 10
    out_hbm, x_all, out_all, sems, k3, qv3, out3, *feeds = refs[-scratch - 1 :]
    qkv_ref, aout_ref, *feed_refs = refs[: 4 if fed else 6]
    stride = x_all.shape[1]
    per_part = PART // GROUP
    parts = GRID_STEP // PART

    def arrival(part):
        at = (slice(None), pl.ds(part * per_part, per_part))
        return pltpu.make_async_copy(x_hbm.at[at], x_all.at[at], sems.at[0, part])

    def leaving(part):
        here = (slice(None), pl.ds(part * per_part, per_part))
        there = (slice(None), pl.ds(chunk * stride + part * per_part, per_part))
        return pltpu.make_async_copy(out_all.at[here], out_hbm.at[there], sems.at[1, part])

    for part in range(parts):
        arrival(part).start()
    prepare_attention(qkv_ref, aout_ref, gains_ref[3:4], k3, qv3, out3)
    prepare_feed(*feed_refs[:2], gains_ref[4:5], *feeds[:2])
    if not fed:
        prepare_feed(*feed_refs[2:], gains_ref[2:3], *feeds[2:])

    flat_in = x_all.reshape(GRID_STEP, CHANNELS)
    flat_out = out_all.reshape(GRID_STEP, CHANNELS)

    def group(part):
        first = part * per_part
        arrival(part).wait()
        windows = [flat_in[pl.ds(first + p, GROUP, stride=stride), :] for p in range(per_part)]
        pairs = [rows_of(windows[i : i + 2]) for i in range(0, len(windows), 2)]
        if not fed:
            pairs = yield from feed(pairs, *feeds[2:])
        pairs = yield from attend(pairs, k3, qv3, out3)
        pairs = yield from feed(pairs, *feeds[:2])
        for p, x in enumerate(pairs):
            for i in range(2):
                window = first + 2 * p + i
                flat_out[pl.ds(window, GROUP, stride=stride), :] = x[i * GROUP : (i + 1) * GROUP]
        leaving(part).start()

    staggered(group(part) for part in range(parts))
    for part in range(parts):
        leaving(part).wait()


def grid_stage(received, fed, gains, weights, chunk, earlier):
    per_device = received.shape[1]
    in_hbm = pl.BlockSpec(memory_space=pl.ANY)
    in_specs = [in_hbm, whole(gains.shape)] + [of_layer(w, 1) for w in weights]
    args = (received, gains) + weights
    if not fed:
        in_specs += [of_layer(w, 0) for w in weights[2:]]
        args += weights[2:]
    aliases = {}
    if earlier is not None:
        in_specs.append(in_hbm)
        aliases = {len(args): 0}
        args += (earlier,)

    def body(*refs):
        grid_kernel(fed, chunk, *refs)

    return pl.pallas_call(
        body,
        grid=(1,),
        in_specs=in_specs,
        out_specs=in_hbm,
        out_shape=jax.ShapeDtypeStruct((GROUP, CHUNKS * per_device, CHANNELS), F32),
        scratch_shapes=[pltpu.VMEM(received.shape, F32)] * 2
        + [pltpu.SemaphoreType.DMA((2, GRID_STEP // PART))]
        + ATTENTION_SCRATCH
        + FEED_SCRATCH
        + ([] if fed else FEED_SCRATCH),
        input_output_aliases=aliases,
        compiler_params=pltpu.CompilerParams(vmem_limit_bytes=VMEM_LIMIT),
        cost_estimate=pl.CostEstimate(
            flops=14_000_000_000, bytes_accessed=4_000_000, transcendentals=0
        ),
    )(*args)


def by_pairs(edge, at, axis, count):
    even = at % 2 == 0
    swaps = []
    for first, last in ((1, jnp.logical_not(even)), (0, even)):
        lower = [(i, i + 1) for i in range(first, count - 1, 2)]
        pairs = lower + [(b, a) for a, b in lower]
        swaps.append(lax.ppermute(edge(last), axis, pairs))
    return swaps[::-1]


def per_device(
    field, context, ctx_weight, norm_gains, expand_weight, depth_weight, se_reduce, se_expand,
    project_weight, attn_qkv, attn_out, mlp_in, mlp_out,
):
    row_axis = ("rg", "core")
    rows, cols = 16, 8
    row = lax.axis_index(row_axis)
    col = lax.axis_index("col")

    def row_edge(last):
        fine = lax.dynamic_index_in_dim(field, jnp.where(last, 31, 0), 0, keepdims=False)
        of_context = lax.dynamic_index_in_dim(context, jnp.where(last, 7, 0), 0, keepdims=False)
        return jnp.concatenate([fine, of_context], axis=0)

    rows_a, rows_b = by_pairs(row_edge, row, row_axis, rows)
    odd = row % 2 == 1

    def column_edge(last):
        fine_at, coarse_at = jnp.where(last, 127, 0), jnp.where(last, 31, 0)

        def one(x, at):
            return lax.dynamic_slice_in_dim(x, at, 1, axis=x.ndim - 2).reshape(-1, CHANNELS)

        parts = []
        for start, stop, tile, at in ((0, 128, field, fine_at), (128, 160, context, coarse_at)):
            of_a, of_b = one(rows_a[start:stop], at), one(rows_b[start:stop], at)
            parts += [jnp.where(odd, of_a, of_b), one(tile, at), jnp.where(odd, of_b, of_a)]
        return jnp.concatenate(parts, axis=0)

    cols_a, cols_b = by_pairs(column_edge, col, "col", cols)
    place = jnp.stack([row, col]).astype(jnp.int32)
    lifted, active, partial = lift_stage(
        place,
        (
            field, context, rows_a, rows_b, cols_a, cols_b, ctx_weight, norm_gains, expand_weight,
            depth_weight, se_reduce.T,
        ),
        rows * cols,
    )

    def exchange(x, axes):
        return lax.all_to_all(x, axes, split_axis=0, concat_axis=0, tiled=True)

    group = ("rg", "col")
    sums = exchange(partial[:, None, :], ("rg", "core", "col"))[:, 0, :]

    weights = (attn_qkv, attn_out, mlp_in, mlp_out)
    cells_total = rows * cols * field.shape[0] * field.shape[1]
    sent = []
    for chunk in range(CHUNKS):
        mine = block_stage(
            chunk, chunk > 0, lifted, active, sums, se_expand, project_weight, norm_gains, weights,
            cells_total,
        )
        sent.append(exchange(mine.reshape(GROUP, -1, CHANNELS), group))
    attended = None
    for chunk in range(CHUNKS):
        attended = grid_stage(sent[chunk], chunk > 0, norm_gains, weights, chunk, attended)
    back = exchange(attended, group)
    halves = back.reshape(4 // CHUNKS, 16, 2, CHUNKS, WINDOW // 2, WINDOW, CHANNELS)
    return halves.transpose(3, 0, 2, 4, 1, 5, 6).reshape(field.shape)


def solution(mesh):
    fine = Mesh(mesh.devices.reshape(8, 2, 8), ("rg", "core", "col"))
    tiled = P(("rg", "core"), "col", None)
    return jax.shard_map(
        per_device,
        mesh=fine,
        in_specs=(tiled, tiled) + (P(),) * 11,
        out_specs=tiled,
        check_vma=False,
    )
```

```python
import math

import jax
import jax.numpy as jnp
import numpy as np
from jax import lax
from jax.experimental import pallas as pl
from jax.experimental.pallas import tpu as pltpu
from jax.sharding import Mesh
from jax.sharding import PartitionSpec as P

HEADS = 4
WINDOW = 8
CHANNELS = 128
EXPANDED = 512
MLP_HIDDEN = 512
SQUEEZE = 32
HEAD_DIM = CHANNELS // HEADS
CELLS = WINDOW * WINDOW
GROUP = 64
WIDE = 136
COARSE_WIDE = 48
EPSILON = 1e-05
F32 = jnp.float32
BF16 = jnp.bfloat16
HIGHEST = lax.Precision.HIGHEST
CHUNKS = 2
BLOCK_STEP = 1024
GRID_STEP = 2048
VMEM_LIMIT = 56 * 1024 * 1024

GELU_IN = (math.sqrt(2.0 / math.pi) * 0.044715) ** (1.0 / 3.0)
GELU_OUT = 0.5 / GELU_IN
GELU_LINEAR = math.sqrt(2.0 / math.pi) / GELU_IN


def bend(s):
    return s * (1.0 + jnp.tanh(s * (GELU_LINEAR + s * s)))


def split(x):
    high = x.astype(BF16)
    low = (x - high.astype(F32)).astype(BF16)
    return high, low


def dot(a, b):
    return jnp.dot(a, b, preferred_element_type=F32)


def rows_of(parts):
    return jnp.concatenate(parts, axis=0)


def lanes_of(parts):
    return jnp.concatenate(parts, axis=1)


def normed(x):
    shifted = x - jnp.mean(x, axis=-1, keepdims=True)
    spread = jnp.sum(shifted * shifted, axis=-1, keepdims=True)
    return shifted * lax.rsqrt(spread + CHANNELS * EPSILON)


def gained(weight, gain):
    column = jnp.broadcast_to(gain * math.sqrt(CHANNELS), (CHANNELS, CHANNELS)).T
    return lanes_of([weight[:, c : c + 128] * column for c in range(0, weight.shape[1], 128)])


def three(x):
    high, low = split(x)
    return lanes_of([high, low, high])


def stack_rows(weight):
    high, low = split(weight)
    return rows_of([high, high, low])


def deep_weight(weight):
    return lanes_of(split(weight))


def prepare_attention(qkv_ref, out_ref, gain, k3, qv3, out3):
    scale = math.log2(math.e) / math.sqrt(HEAD_DIM)
    k3[...] = stack_rows(gained(qkv_ref[0, :, CHANNELS : 2 * CHANNELS], gain))
    row_gain = gain * math.sqrt(CHANNELS)
    queries = qkv_ref[0, :, :CHANNELS].T * (row_gain * scale)
    values = qkv_ref[0, :, 2 * CHANNELS :].T * row_gain
    high, low = split(rows_of([queries, values]))
    qv3[...] = lanes_of([high, high, low])
    out3[...] = stack_rows(out_ref[0])


def prepare_feed(in_ref, mlp_ref, gain, in3, mlp_pair):
    in3[...] = stack_rows(gained(GELU_IN * in_ref[0], gain))
    mlp_pair[...] = deep_weight(GELU_OUT * mlp_ref[0])


PAIR = 2 * CELLS
PART = 1024


def attend(pairs, k3, qv3, out3):
    left = lax.broadcasted_iota(jnp.int32, (HEAD_DIM, PAIR), 1) < CELLS
    left_all = lax.broadcasted_iota(jnp.int32, (CHANNELS, PAIR), 1) < CELLS
    zero = jnp.zeros((HEAD_DIM, PAIR), BF16)
    zero_block = jnp.zeros((2 * HEAD_DIM, PAIR), BF16)
    natural, turned = [], []
    for x in pairs:
        high, low = split(normed(x))
        natural.append(lanes_of([high, low, high]))
        high, low = high.T, low.T
        turned.append(rows_of([high, low, high]))
    yield
    keys = dot(rows_of(natural), k3[...])
    both = dot(qv3[...], lanes_of(turned))
    yield
    sides, value_sides = [], []

    def by_heads(straight, swapped):
        blocks = []
        for group in range(2):
            at = [slice(h * HEAD_DIM, (h + 1) * HEAD_DIM) for h in (2 * group, 2 * group + 1)]
            block = rows_of(
                [jnp.where(left, straight[at[0]], zero), jnp.where(left, zero, swapped[at[1]])]
            )
            blocks.append(lanes_of([zero_block, block] if group else [block, zero_block]))
        return rows_of(blocks)

    for p in range(len(pairs)):
        at = slice(p * PAIR, (p + 1) * PAIR)
        key3 = three(keys[at])
        high, low = split(both[:CHANNELS, at])
        high_swapped, low_swapped = pltpu.roll(high, CELLS, 1), pltpu.roll(low, CELLS, 1)
        for second in range(2):
            if second:
                h, l = by_heads(high_swapped, high), by_heads(low_swapped, low)
            else:
                h, l = by_heads(high, high_swapped), by_heads(low, low_swapped)
            sides.append((key3[second * CELLS : (second + 1) * CELLS], rows_of([h, h, l])))
        high, low = split(both[CHANNELS:, at])
        low = pltpu.roll(low, CELLS, 1)
        first, second = jnp.where(left_all, high, low), jnp.where(left_all, low, high)
        value_sides += [lanes_of([first, first]), lanes_of([second, second])]
    yield
    scores = [dot(key, query) for key, query in sides]
    yield
    weights, scales = [], []
    for score in scores:
        weight = jnp.exp2(score - jnp.max(score, axis=0, keepdims=True))
        scales.append(1.0 / jnp.sum(weight, axis=0, keepdims=True))
        high, low = split(weight)
        weights.append(rows_of([high, high, low, low]))
    yield
    mixed = [
        [dot(value[64 * g : 64 * g + 64], weight[:, 128 * g : 128 * g + 128]) for g in range(2)]
        for value, weight in zip(value_sides, weights)
    ]
    yield
    blended = []
    for p in range(len(pairs)):
        parts = []
        for h in range(HEADS):
            lanes = slice(128 * (h // 2), 128 * (h // 2) + 128)
            at = slice((h % 2) * HEAD_DIM, (h % 2 + 1) * HEAD_DIM)
            of_a, of_b = (
                mixed[2 * p + i][h // 2][at] * scales[2 * p + i][:, lanes] for i in range(2)
            )
            if h % 2:
                of_a = pltpu.roll(of_a, CELLS, 1)
            else:
                of_b = pltpu.roll(of_b, CELLS, 1)
            parts.append(jnp.where(left, of_a, of_b))
        blended.append(three(rows_of(parts).T))
    yield
    added = dot(rows_of(blended), out3[...])
    yield
    return [x + added[p * PAIR : (p + 1) * PAIR] for p, x in enumerate(pairs)]


def feed(pairs, in3, mlp_pair):
    parts = [three(normed(x)) for x in pairs]
    yield
    inner = dot(rows_of(parts), in3[...])
    yield
    high, low = split_blocks(inner, 64, bend)
    yield
    wide = dot(high, mlp_pair[...])
    rest = dot(low, mlp_pair[:, :CHANNELS])
    yield
    out = []
    for p, x in enumerate(pairs):
        at = slice(p * PAIR, (p + 1) * PAIR)
        out.append(x + (wide[at, :CHANNELS] + (wide[at, CHANNELS:] + rest[at])))
    return out


def staggered(groups):
    waiting, running = list(groups), []
    while waiting or running:
        if waiting:
            running.append(waiting.pop(0))
        for group in list(running):
            try:
                next(group)
            except StopIteration:
                running.remove(group)


def split_blocks(x, rows, make):
    highs, lows = [], []
    for r in range(0, x.shape[0], rows):
        made = [split(make(x[r : r + rows, c : c + 128])) for c in range(0, x.shape[1], 128)]
        highs.append(lanes_of([m[0] for m in made]))
        lows.append(lanes_of([m[1] for m in made]))
    return rows_of(highs), rows_of(lows)


def column_weights():
    fine = np.zeros((WIDE, COARSE_WIDE), np.float32)
    table = ((0.375, 0.625, 0.0), (0.125, 0.875, 0.0), (0.0, 0.875, 0.125), (0.0, 0.625, 0.375))

    def fill(at, column):
        k, o = column // 4, column % 4
        for step, weight in zip((-1, 0, 1), table[o]):
            if weight:
                fine[at, (k + step) % 40] = weight

    for column in range(128):
        fill(8 * (column % 16) + column // 16, column)
    fill(128, -1)
    fill(135, 128)
    return np.concatenate([fine, fine], axis=1)


ROW_WEIGHTS = ((0.375, 0.625, -1), (0.125, 0.875, -1), (0.875, 0.125, 0), (0.625, 0.375, 0))


def lift_kernel(
    place_ref, field_ref, context_ref, rows_a_ref, rows_b_ref, cols_a_ref, cols_b_ref, up_ref,
    ctxw_ref, gains_ref, expand_ref, depth_ref, reduce_ref, lifted_ref, active_hbm, sum_ref,
    active, field, ends, sides, lift, ctx, coarse, hid, expand3, total, sems, leave_sems,
):
    step = pl.program_id(0)

    def arrival(k):
        at = pl.ds(0, 9) if k == 0 else pl.ds(8 * k + 1, 8 if k < 3 else 7)
        return pltpu.make_async_copy(field_ref.at[at], field.at[at], sems.at[k])

    def leaving(k, part):
        at = (pl.ds(8 * k, 8), part)
        return pltpu.make_async_copy(active.at[at], active_hbm.at[at], leave_sems.at[k, part])

    sublane = lax.broadcasted_iota(jnp.int32, (8, 128), 0)
    first_row, last_row = sublane == 0, sublane == 7

    @pl.when(step == 0)
    def _():
        for k in range(4):
            arrival(k).start()
        expand3[...] = stack_rows(gained(GELU_IN * expand_ref[...], gains_ref[0:1]))
        total[...] = jnp.zeros_like(total)
        ctx[1:9, :32] = context_ref[...]

        def take_rows(above_ref, below_ref):
            for t in range(16):
                ends[0, 8 * t : 8 * t + 8] = above_ref[pl.ds(t, 8, stride=16), :]
                ends[1, 8 * t : 8 * t + 8] = below_ref[pl.ds(t, 8, stride=16), :]
            ctx[0, :32] = above_ref[128:]
            ctx[9, :32] = below_ref[128:]

        def take_columns(before_ref, after_ref):
            zero = jnp.zeros((8, 128), F32)
            for e in range(44):
                after = jnp.broadcast_to(after_ref[e : e + 1], (8, 128))
                before = jnp.broadcast_to(before_ref[e : e + 1], (8, 128))
                if e < 34:
                    sides[e] = jnp.where(first_row, before, jnp.where(last_row, after, zero))
                else:
                    ctx[e - 34, 32:40] = jnp.where(
                        first_row, after, jnp.where(last_row, before, zero)
                    )
                    ctx[e - 34, 40:] = zero

        pl.when(place_ref[0] % 2 == 0)(lambda: take_rows(rows_b_ref, rows_a_ref))
        pl.when(place_ref[0] % 2 == 1)(lambda: take_rows(rows_a_ref, rows_b_ref))
        pl.when(place_ref[1] % 2 == 0)(lambda: take_columns(cols_b_ref, cols_a_ref))
        pl.when(place_ref[1] % 2 == 1)(lambda: take_columns(cols_a_ref, cols_b_ref))
        weight = stack_rows(ctxw_ref[...])
        projected = dot(three(ctx[...].reshape(10 * COARSE_WIDE, CHANNELS)), weight)
        for k in range(10):
            high, low = split(projected[COARSE_WIDE * k : COARSE_WIDE * (k + 1)])
            coarse[k] = dot(up_ref[...], rows_of([high, low]))

    has_after = jnp.where(place_ref[1] < 7, 1.0, 0.0)
    has_before = jnp.where(place_ref[1] > 0, 1.0, 0.0)
    inside = jnp.where(first_row, has_before, has_after)

    for k in range(4):
        pl.when(step == k)(lambda k=k: arrival(k).wait())

    def hidden_rows(first, fine_first, k_first, count):
        parts = []
        for i in range(0, count, 2):
            two = []
            for j in (i, i + 1):
                k, o = (fine_first + j) // 4, (fine_first + j) % 4
                lower, upper, shift = ROW_WEIGHTS[o]
                at = k_first + k + shift
                up = lower * coarse[at] + upper * coarse[at + 1]
                if fine_first + j < 0:
                    own = ends[0]
                else:
                    f = jnp.minimum(first + j - 1, 31)
                    own = rows_of([field[f, pl.ds(t, 8, stride=16), :] for t in range(16)])
                    if fine_first + j == 8:
                        own = jnp.where(step == 3, ends[1], own)
                x = rows_of([own, sides[first + j]]) + up
                lift[first + j] = x[:128]
                two.append(x)
            parts.append(three(normed(rows_of(two))))
        made = dot(rows_of(parts), expand3[...])
        for i in range(count):
            for c in range(0, EXPANDED, 128):
                out = bend(made[i * WIDE : (i + 1) * WIDE, c : c + 128])
                hid[first + i, :128, c : c + 128] = out[:128]
                hid[first + i, 128:, c : c + 128] = out[128:] * inside

    @pl.when(step == 0)
    def _():
        hidden_rows(0, -1, 1, 2)

        @pl.when(place_ref[0] == 0)
        def _():
            hid[0] = jnp.zeros((WIDE, EXPANDED), F32)

    hidden_rows(8 * step + 2, 1, 2 * step + 1, 8)

    @pl.when((step == 3) & (place_ref[0] == 15))
    def _():
        hid[33] = jnp.zeros((WIDE, EXPANDED), F32)

    lifted_ref[...] = lift[pl.ds(8 * step + 1, 8)]

    for part in range(EXPANDED // 128):
        lanes = slice(part * 128, (part + 1) * 128)
        taps = [
            [jnp.broadcast_to((GELU_IN * GELU_OUT) * depth_ref[i, j : j + 1, lanes], (8, 128)) for j in range(3)]
            for i in range(3)
        ]

        def row(r, summed):
            def column(t):
                seen = [hid[8 * step + r + i, 8 * t : 8 * t + 8, lanes] for i in range(3)]
                return [
                    seen[0] * taps[0][j] + seen[1] * taps[1][j] + seen[2] * taps[2][j]
                    for j in range(3)
                ]

            first, last, halo = column(0), column(15), column(16)
            before = jnp.where(first_row, halo[0], pltpu.roll(last[0], 1, 0))
            end = jnp.where(last_row, halo[2], pltpu.roll(first[2], 7, 0))
            here = first
            for t in range(16):
                following = column(t + 1) if t < 14 else last
                out = bend(here[1] + before + (following[2] if t < 15 else end))
                active[8 * step + r, part, 8 * t : 8 * t + 8] = out
                summed = summed + out
                before, here = here[0], following
            return summed

        summed = total[:, lanes]
        for r in range(8):
            summed = row(r, summed)
        total[:, lanes] = summed
        leaving(step, part).start()

    @pl.when(step == 3)
    def _():
        squeezed = lax.dot_general(
            total[...], reduce_ref[...], (((1,), (1,)), ((), ())), precision=HIGHEST,
            preferred_element_type=F32,
        )
        squeezed = jnp.sum(squeezed, axis=0, keepdims=True)
        padded = lanes_of([squeezed, jnp.zeros((1, 128 - SQUEEZE), F32)])
        sum_ref[...] = jnp.broadcast_to(padded, sum_ref.shape)
        for k in range(4):
            for part in range(4):
                leaving(k, part).wait()


def whole(shape):
    return pl.BlockSpec(shape, lambda *_: (0,) * len(shape))


def of_layer(array, layer):
    shape = (1,) + array.shape[1:]
    return pl.BlockSpec(shape, lambda *_: (layer,) + (0,) * (len(shape) - 1))


def lift_stage(place, args, copies):
    up = jnp.asarray(column_weights(), BF16)
    args = args[:6] + (up,) + args[6:]
    return pl.pallas_call(
        lift_kernel,
        grid=(4,),
        in_specs=[pl.BlockSpec(memory_space=pltpu.SMEM), pl.BlockSpec(memory_space=pl.ANY)]
        + [whole(a.shape) for a in args[1:]],
        out_specs=[
            pl.BlockSpec((8, 128, CHANNELS), lambda s: (s, 0, 0)),
            pl.BlockSpec(memory_space=pl.ANY),
            whole((copies, 128)),
        ],
        out_shape=[
            jax.ShapeDtypeStruct((32, 128, CHANNELS), F32),
            jax.ShapeDtypeStruct((32, EXPANDED // 128, 128, 128), F32),
            jax.ShapeDtypeStruct((copies, 128), F32),
        ],
        scratch_shapes=[
            pltpu.VMEM((32, EXPANDED // 128, 128, 128), F32),
            pltpu.VMEM((32, 128, CHANNELS), F32),
            pltpu.VMEM((2, 128, CHANNELS), F32),
            pltpu.VMEM((34, 8, CHANNELS), F32),
            pltpu.VMEM((34, 128, CHANNELS), F32),
            pltpu.VMEM((10, COARSE_WIDE, CHANNELS), F32),
            pltpu.VMEM((10, WIDE, CHANNELS), F32),
            pltpu.VMEM((34, WIDE, EXPANDED), F32),
            pltpu.VMEM((3 * CHANNELS, EXPANDED), BF16),
            pltpu.VMEM((8, EXPANDED), F32),
            pltpu.SemaphoreType.DMA((4,)),
            pltpu.SemaphoreType.DMA((4, 4)),
        ],
        compiler_params=pltpu.CompilerParams(vmem_limit_bytes=VMEM_LIMIT),
        cost_estimate=pl.CostEstimate(
            flops=8_000_000_000, bytes_accessed=14_000_000, transcendentals=0
        ),
    )(place, *args)


def block_kernel(
    cells_total, fed, lifted_ref, active_ref, sums_ref, sexp_ref, project_ref, gains_ref, qkv_ref,
    aout_ref, min_ref, mout_ref, out_ref, project, k3, qv3, out3, *feed_weights,
):
    @pl.when(pl.program_id(0) == 0)
    def _():
        pooled = jnp.sum(sums_ref[...], axis=0, keepdims=True) * (GELU_OUT / cells_total)
        squeezed = pooled[:, :SQUEEZE]
        squeezed = squeezed * jax.nn.sigmoid(squeezed)
        wide = jnp.broadcast_to(squeezed, (CHANNELS, SQUEEZE))
        gate = jnp.dot(wide, sexp_ref[...], precision=HIGHEST, preferred_element_type=F32)
        project[...] = deep_weight(project_ref[...] * (GELU_OUT * jax.nn.sigmoid(gate)).T)
        prepare_attention(qkv_ref, aout_ref, gains_ref[1:2], k3, qv3, out3)
        if fed:
            prepare_feed(min_ref, mout_ref, gains_ref[2:3], *feed_weights)

    def window(w, load):
        at = pl.ds(64 * (w % 2) + w // 2, WINDOW, stride=8)
        return rows_of([load(r, at) for r in range(WINDOW)])

    def expanded(r, at):
        return lanes_of([active_ref[r, k, at, :] for k in range(EXPANDED // 128)])

    def projected(start):
        halves = [split(window(w, expanded)) for w in range(start, start + PART // CELLS)]
        yield
        wide = dot(rows_of([h[0] for h in halves]), project[...])
        rest = dot(rows_of([h[1] for h in halves]), project[:, :CHANNELS])
        yield
        pairs = []
        for p in range(PART // PAIR):
            at = slice(p * PAIR, (p + 1) * PAIR)
            x = rows_of(
                [window(start + 2 * p + i, lambda r, at: lifted_ref[r, at, :]) for i in range(2)]
            )
            pairs.append(x + (wide[at, :CHANNELS] + (wide[at, CHANNELS:] + rest[at])))
        return pairs

    def group(part):
        pairs = yield from projected(part * PART // CELLS)
        pairs = yield from attend(pairs, k3, qv3, out3)
        if fed:
            pairs = yield from feed(pairs, *feed_weights)
        for p, x in enumerate(pairs):
            out_ref[part * PART + p * PAIR : part * PART + (p + 1) * PAIR] = x

    staggered(group(part) for part in range(BLOCK_STEP // PART))


ATTENTION_SCRATCH = [
    pltpu.VMEM((3 * CHANNELS, CHANNELS), BF16),
    pltpu.VMEM((2 * CHANNELS, 3 * CHANNELS), BF16),
    pltpu.VMEM((3 * CHANNELS, CHANNELS), BF16),
]
FEED_SCRATCH = [
    pltpu.VMEM((3 * CHANNELS, MLP_HIDDEN), BF16),
    pltpu.VMEM((MLP_HIDDEN, 2 * CHANNELS), BF16),
]


def block_stage(chunk, fed, lifted, active, sums, se_expand, project, gains, weights, cells_total):
    steps = 4 // CHUNKS
    row_base = chunk * (4 // CHUNKS)
    rest = (sums, se_expand, project, gains)

    columns = BLOCK_STEP // 8
    strips = [
        pl.BlockSpec((8, columns, CHANNELS), lambda s: (row_base + s, 0, 0)),
        pl.BlockSpec((8, EXPANDED // 128, columns, 128), lambda s: (row_base + s, 0, 0, 0)),
    ]

    def body(*refs):
        block_kernel(cells_total, fed, *refs)

    return pl.pallas_call(
        body,
        grid=(steps,),
        in_specs=strips
        + [whole(a.shape) for a in rest]
        + [of_layer(w, 0) for w in weights],
        out_specs=pl.BlockSpec((BLOCK_STEP, CHANNELS), lambda s: (s, 0)),
        out_shape=jax.ShapeDtypeStruct((steps * BLOCK_STEP, CHANNELS), F32),
        scratch_shapes=[
            pltpu.VMEM((EXPANDED, 2 * CHANNELS), BF16),
        ]
        + ATTENTION_SCRATCH
        + (FEED_SCRATCH if fed else []),
        compiler_params=pltpu.CompilerParams(vmem_limit_bytes=VMEM_LIMIT),
        cost_estimate=pl.CostEstimate(
            flops=14_000_000_000, bytes_accessed=8_000_000, transcendentals=0
        ),
    )(lifted, active, *rest, *weights)


def grid_kernel(fed, x_ref, gains_ref, *refs):
    scratch = 5 if fed else 7
    out_ref, k3, qv3, out3, *feeds = refs[-scratch - 1 :]
    qkv_ref, aout_ref, *feed_refs = refs[: 4 if fed else 6]

    @pl.when(pl.program_id(0) == 0)
    def _():
        prepare_attention(qkv_ref, aout_ref, gains_ref[3:4], k3, qv3, out3)
        prepare_feed(*feed_refs[:2], gains_ref[4:5], *feeds[:2])
        if not fed:
            prepare_feed(*feed_refs[2:], gains_ref[2:3], *feeds[2:])

    stride = GRID_STEP // GROUP
    flat_in = x_ref.reshape(GRID_STEP, CHANNELS)
    flat_out = out_ref.reshape(GRID_STEP, CHANNELS)

    def group(part):
        first = part * PART // GROUP
        windows = [flat_in[pl.ds(first + p, GROUP, stride=stride), :] for p in range(PART // GROUP)]
        pairs = [rows_of(windows[i : i + 2]) for i in range(0, len(windows), 2)]
        if not fed:
            pairs = yield from feed(pairs, *feeds[2:])
        pairs = yield from attend(pairs, k3, qv3, out3)
        pairs = yield from feed(pairs, *feeds[:2])
        for p, x in enumerate(pairs):
            for i in range(2):
                window = first + 2 * p + i
                flat_out[pl.ds(window, GROUP, stride=stride), :] = x[i * GROUP : (i + 1) * GROUP]

    staggered(group(part) for part in range(GRID_STEP // PART))


def grid_stage(received, fed, gains, weights, chunk, earlier):
    per_device = received.shape[1]
    steps = per_device * GROUP // GRID_STEP
    shape = (GROUP, GRID_STEP // GROUP, CHANNELS)
    in_specs = [pl.BlockSpec(shape, lambda s: (0, s, 0)), whole(gains.shape)]
    in_specs += [of_layer(w, 1) for w in weights]
    args = (received, gains) + weights
    if not fed:
        in_specs += [of_layer(w, 0) for w in weights[2:]]
        args += weights[2:]
    aliases = {}
    if earlier is not None:
        in_specs.append(pl.BlockSpec(memory_space=pl.ANY))
        aliases = {len(args): 0}
        args += (earlier,)

    def body(*refs):
        grid_kernel(fed, *refs)

    return pl.pallas_call(
        body,
        grid=(steps,),
        in_specs=in_specs,
        out_specs=pl.BlockSpec(shape, lambda s: (0, chunk * steps + s, 0)),
        out_shape=jax.ShapeDtypeStruct((GROUP, CHUNKS * per_device, CHANNELS), F32),
        scratch_shapes=ATTENTION_SCRATCH + FEED_SCRATCH + ([] if fed else FEED_SCRATCH),
        input_output_aliases=aliases,
        compiler_params=pltpu.CompilerParams(vmem_limit_bytes=VMEM_LIMIT),
        cost_estimate=pl.CostEstimate(
            flops=14_000_000_000, bytes_accessed=4_000_000, transcendentals=0
        ),
    )(*args)


def by_pairs(edge, at, axis, count):
    even = at % 2 == 0
    swaps = []
    for first, last in ((1, jnp.logical_not(even)), (0, even)):
        lower = [(i, i + 1) for i in range(first, count - 1, 2)]
        pairs = lower + [(b, a) for a, b in lower]
        swaps.append(lax.ppermute(edge(last), axis, pairs))
    return swaps[::-1]


def per_device(
    field, context, ctx_weight, norm_gains, expand_weight, depth_weight, se_reduce, se_expand,
    project_weight, attn_qkv, attn_out, mlp_in, mlp_out,
):
    row_axis = ("rg", "core")
    rows, cols = 16, 8
    row = lax.axis_index(row_axis)
    col = lax.axis_index("col")

    def row_edge(last):
        fine = lax.dynamic_index_in_dim(field, jnp.where(last, 31, 0), 0, keepdims=False)
        of_context = lax.dynamic_index_in_dim(context, jnp.where(last, 7, 0), 0, keepdims=False)
        return jnp.concatenate([fine, of_context], axis=0)

    rows_a, rows_b = by_pairs(row_edge, row, row_axis, rows)
    odd = row % 2 == 1

    def column_edge(last):
        fine_at, coarse_at = jnp.where(last, 127, 0), jnp.where(last, 31, 0)

        def one(x, at):
            return lax.dynamic_slice_in_dim(x, at, 1, axis=x.ndim - 2).reshape(-1, CHANNELS)

        parts = []
        for start, stop, tile, at in ((0, 128, field, fine_at), (128, 160, context, coarse_at)):
            of_a, of_b = one(rows_a[start:stop], at), one(rows_b[start:stop], at)
            parts += [jnp.where(odd, of_a, of_b), one(tile, at), jnp.where(odd, of_b, of_a)]
        return jnp.concatenate(parts, axis=0)

    cols_a, cols_b = by_pairs(column_edge, col, "col", cols)
    place = jnp.stack([row, col]).astype(jnp.int32)
    lifted, active, partial = lift_stage(
        place,
        (
            field, context, rows_a, rows_b, cols_a, cols_b, ctx_weight, norm_gains, expand_weight,
            depth_weight, se_reduce.T,
        ),
        rows * cols,
    )

    def exchange(x, axes):
        return lax.all_to_all(x, axes, split_axis=0, concat_axis=0, tiled=True)

    group = ("rg", "col")
    sums = exchange(partial[:, None, :], ("rg", "core", "col"))[:, 0, :]

    weights = (attn_qkv, attn_out, mlp_in, mlp_out)
    cells_total = rows * cols * field.shape[0] * field.shape[1]
    sent = []
    for chunk in range(CHUNKS):
        mine = block_stage(
            chunk, chunk > 0, lifted, active, sums, se_expand, project_weight, norm_gains, weights,
            cells_total,
        )
        sent.append(exchange(mine.reshape(GROUP, -1, CHANNELS), group))
    attended = None
    for chunk in range(CHUNKS):
        attended = grid_stage(sent[chunk], chunk > 0, norm_gains, weights, chunk, attended)
    back = exchange(attended, group)
    halves = back.reshape(4 // CHUNKS, 16, 2, CHUNKS, WINDOW // 2, WINDOW, CHANNELS)
    return halves.transpose(3, 0, 2, 4, 1, 5, 6).reshape(field.shape)


def solution(mesh):
    fine = Mesh(mesh.devices.reshape(8, 2, 8), ("rg", "core", "col"))
    tiled = P(("rg", "core"), "col", None)
    return jax.shard_map(
        per_device,
        mesh=fine,
        in_specs=(tiled, tiled) + (P(),) * 11,
        out_specs=tiled,
        check_vma=False,
    )
```

```python
import math

import jax
import jax.numpy as jnp
import numpy as np
from jax import lax
from jax.experimental import pallas as pl
from jax.experimental.pallas import tpu as pltpu
from jax.sharding import Mesh
from jax.sharding import PartitionSpec as P

HEADS = 4
WINDOW = 8
CHANNELS = 128
EXPANDED = 512
MLP_HIDDEN = 512
SQUEEZE = 32
HEAD_DIM = CHANNELS // HEADS
CELLS = WINDOW * WINDOW
GROUP = 64
WIDE = 136
COARSE_WIDE = 48
EPSILON = 1e-05
F32 = jnp.float32
BF16 = jnp.bfloat16
HIGHEST = lax.Precision.HIGHEST
CHUNKS = 2
BLOCK_STEP = 1024
GRID_STEP = 2048
VMEM_LIMIT = 56 * 1024 * 1024

GELU_IN = (math.sqrt(2.0 / math.pi) * 0.044715) ** (1.0 / 3.0)
GELU_OUT = 0.5 / GELU_IN
GELU_LINEAR = math.sqrt(2.0 / math.pi) / GELU_IN


def bend(s):
    return s * (1.0 + jnp.tanh(s * (GELU_LINEAR + s * s)))


def split(x):
    high = x.astype(BF16)
    low = (x - high.astype(F32)).astype(BF16)
    return high, low


def dot(a, b):
    return jnp.dot(a, b, preferred_element_type=F32)


def rows_of(parts):
    return jnp.concatenate(parts, axis=0)


def lanes_of(parts):
    return jnp.concatenate(parts, axis=1)


def normed(x):
    shifted = x - jnp.mean(x, axis=-1, keepdims=True)
    spread = jnp.sum(shifted * shifted, axis=-1, keepdims=True)
    return shifted * lax.rsqrt(spread + CHANNELS * EPSILON)


def gained(weight, gain):
    column = jnp.broadcast_to(gain * math.sqrt(CHANNELS), (CHANNELS, CHANNELS)).T
    return lanes_of([weight[:, c : c + 128] * column for c in range(0, weight.shape[1], 128)])


def three(x):
    high, low = split(x)
    return lanes_of([high, low, high])


def stack_rows(weight):
    high, low = split(weight)
    return rows_of([high, high, low])


def deep_weight(weight):
    return lanes_of(split(weight))


def prepare_attention(qkv_ref, out_ref, gain, k3, qv3, out3):
    scale = math.log2(math.e) / math.sqrt(HEAD_DIM)
    k3[...] = stack_rows(gained(qkv_ref[0, :, CHANNELS : 2 * CHANNELS], gain))
    row_gain = gain * math.sqrt(CHANNELS)
    queries = qkv_ref[0, :, :CHANNELS].T * (row_gain * scale)
    values = qkv_ref[0, :, 2 * CHANNELS :].T * row_gain
    high, low = split(rows_of([queries, values]))
    qv3[...] = lanes_of([high, high, low])
    out3[...] = stack_rows(out_ref[0])


def prepare_feed(in_ref, mlp_ref, gain, in3, mlp_pair):
    in3[...] = stack_rows(gained(GELU_IN * in_ref[0], gain))
    mlp_pair[...] = deep_weight(GELU_OUT * mlp_ref[0])


PAIR = 2 * CELLS
PART = 256


def attend(pairs, k3, qv3, out3):
    left = lax.broadcasted_iota(jnp.int32, (HEAD_DIM, PAIR), 1) < CELLS
    left_all = lax.broadcasted_iota(jnp.int32, (CHANNELS, PAIR), 1) < CELLS
    zero = jnp.zeros((HEAD_DIM, PAIR), BF16)
    zero_block = jnp.zeros((2 * HEAD_DIM, PAIR), BF16)
    natural, turned = [], []
    for x in pairs:
        high, low = split(normed(x))
        natural.append(lanes_of([high, low, high]))
        high, low = high.T, low.T
        turned.append(rows_of([high, low, high]))
    yield
    keys = dot(rows_of(natural), k3[...])
    both = dot(qv3[...], lanes_of(turned))
    yield
    sides, value_sides = [], []

    def by_heads(straight, swapped):
        blocks = []
        for group in range(2):
            at = [slice(h * HEAD_DIM, (h + 1) * HEAD_DIM) for h in (2 * group, 2 * group + 1)]
            block = rows_of(
                [jnp.where(left, straight[at[0]], zero), jnp.where(left, zero, swapped[at[1]])]
            )
            blocks.append(lanes_of([zero_block, block] if group else [block, zero_block]))
        return rows_of(blocks)

    for p in range(len(pairs)):
        at = slice(p * PAIR, (p + 1) * PAIR)
        key3 = three(keys[at])
        high, low = split(both[:CHANNELS, at])
        high_swapped, low_swapped = pltpu.roll(high, CELLS, 1), pltpu.roll(low, CELLS, 1)
        for second in range(2):
            if second:
                h, l = by_heads(high_swapped, high), by_heads(low_swapped, low)
            else:
                h, l = by_heads(high, high_swapped), by_heads(low, low_swapped)
            sides.append((key3[second * CELLS : (second + 1) * CELLS], rows_of([h, h, l])))
        high, low = split(both[CHANNELS:, at])
        low = pltpu.roll(low, CELLS, 1)
        first, second = jnp.where(left_all, high, low), jnp.where(left_all, low, high)
        value_sides += [lanes_of([first, first]), lanes_of([second, second])]
    yield
    scores = [dot(key, query) for key, query in sides]
    yield
    weights, scales = [], []
    for score in scores:
        weight = jnp.exp2(score - jnp.max(score, axis=0, keepdims=True))
        scales.append(1.0 / jnp.sum(weight, axis=0, keepdims=True))
        high, low = split(weight)
        weights.append(rows_of([high, high, low, low]))
    yield
    mixed = [
        [dot(value[64 * g : 64 * g + 64], weight[:, 128 * g : 128 * g + 128]) for g in range(2)]
        for value, weight in zip(value_sides, weights)
    ]
    yield
    blended = []
    for p in range(len(pairs)):
        parts = []
        for h in range(HEADS):
            lanes = slice(128 * (h // 2), 128 * (h // 2) + 128)
            at = slice((h % 2) * HEAD_DIM, (h % 2 + 1) * HEAD_DIM)
            of_a, of_b = (
                mixed[2 * p + i][h // 2][at] * scales[2 * p + i][:, lanes] for i in range(2)
            )
            if h % 2:
                of_a = pltpu.roll(of_a, CELLS, 1)
            else:
                of_b = pltpu.roll(of_b, CELLS, 1)
            parts.append(jnp.where(left, of_a, of_b))
        blended.append(three(rows_of(parts).T))
    yield
    added = dot(rows_of(blended), out3[...])
    yield
    return [x + added[p * PAIR : (p + 1) * PAIR] for p, x in enumerate(pairs)]


def feed(pairs, in3, mlp_pair):
    parts = [three(normed(x)) for x in pairs]
    yield
    inner = dot(rows_of(parts), in3[...])
    yield
    high, low = split_blocks(inner, 64, bend)
    yield
    wide = dot(high, mlp_pair[...])
    rest = dot(low, mlp_pair[:, :CHANNELS])
    yield
    out = []
    for p, x in enumerate(pairs):
        at = slice(p * PAIR, (p + 1) * PAIR)
        out.append(x + (wide[at, :CHANNELS] + (wide[at, CHANNELS:] + rest[at])))
    return out


def staggered(groups):
    waiting, running = list(groups), []
    while waiting or running:
        if waiting:
            running.append(waiting.pop(0))
        for group in list(running):
            try:
                next(group)
            except StopIteration:
                running.remove(group)


def split_blocks(x, rows, make):
    highs, lows = [], []
    for r in range(0, x.shape[0], rows):
        made = [split(make(x[r : r + rows, c : c + 128])) for c in range(0, x.shape[1], 128)]
        highs.append(lanes_of([m[0] for m in made]))
        lows.append(lanes_of([m[1] for m in made]))
    return rows_of(highs), rows_of(lows)


def column_weights():
    fine = np.zeros((WIDE, COARSE_WIDE), np.float32)
    table = ((0.375, 0.625, 0.0), (0.125, 0.875, 0.0), (0.0, 0.875, 0.125), (0.0, 0.625, 0.375))

    def fill(at, column):
        k, o = column // 4, column % 4
        for step, weight in zip((-1, 0, 1), table[o]):
            if weight:
                fine[at, (k + step) % 40] = weight

    for column in range(128):
        fill(8 * (column % 16) + column // 16, column)
    fill(128, -1)
    fill(135, 128)
    return np.concatenate([fine, fine], axis=1)


ROW_WEIGHTS = ((0.375, 0.625, -1), (0.125, 0.875, -1), (0.875, 0.125, 0), (0.625, 0.375, 0))


def lift_kernel(
    place_ref, field_ref, context_ref, rows_a_ref, rows_b_ref, cols_a_ref, cols_b_ref, up_ref,
    ctxw_ref, gains_ref, expand_ref, depth_ref, reduce_ref, lifted_ref, active_hbm, sum_ref,
    active, field, ends, sides, lift, ctx, coarse, hid, expand3, total, sems, leave_sems,
):
    step = pl.program_id(0)

    def arrival(k):
        at = pl.ds(0, 9) if k == 0 else pl.ds(8 * k + 1, 8 if k < 3 else 7)
        return pltpu.make_async_copy(field_ref.at[at], field.at[at], sems.at[k])

    def leaving(k, part):
        at = (pl.ds(8 * k, 8), part)
        return pltpu.make_async_copy(active.at[at], active_hbm.at[at], leave_sems.at[k, part])

    sublane = lax.broadcasted_iota(jnp.int32, (8, 128), 0)
    first_row, last_row = sublane == 0, sublane == 7

    @pl.when(step == 0)
    def _():
        for k in range(4):
            arrival(k).start()
        expand3[...] = stack_rows(gained(GELU_IN * expand_ref[...], gains_ref[0:1]))
        total[...] = jnp.zeros_like(total)
        ctx[1:9, :32] = context_ref[...]

        def take_rows(above_ref, below_ref):
            for t in range(16):
                ends[0, 8 * t : 8 * t + 8] = above_ref[pl.ds(t, 8, stride=16), :]
                ends[1, 8 * t : 8 * t + 8] = below_ref[pl.ds(t, 8, stride=16), :]
            ctx[0, :32] = above_ref[128:]
            ctx[9, :32] = below_ref[128:]

        def take_columns(before_ref, after_ref):
            zero = jnp.zeros((8, 128), F32)
            for e in range(44):
                after = jnp.broadcast_to(after_ref[e : e + 1], (8, 128))
                before = jnp.broadcast_to(before_ref[e : e + 1], (8, 128))
                if e < 34:
                    sides[e] = jnp.where(first_row, before, jnp.where(last_row, after, zero))
                else:
                    ctx[e - 34, 32:40] = jnp.where(
                        first_row, after, jnp.where(last_row, before, zero)
                    )
                    ctx[e - 34, 40:] = zero

        pl.when(place_ref[0] % 2 == 0)(lambda: take_rows(rows_b_ref, rows_a_ref))
        pl.when(place_ref[0] % 2 == 1)(lambda: take_rows(rows_a_ref, rows_b_ref))
        pl.when(place_ref[1] % 2 == 0)(lambda: take_columns(cols_b_ref, cols_a_ref))
        pl.when(place_ref[1] % 2 == 1)(lambda: take_columns(cols_a_ref, cols_b_ref))
        weight = stack_rows(ctxw_ref[...])
        projected = dot(three(ctx[...].reshape(10 * COARSE_WIDE, CHANNELS)), weight)
        for k in range(10):
            high, low = split(projected[COARSE_WIDE * k : COARSE_WIDE * (k + 1)])
            coarse[k] = dot(up_ref[...], rows_of([high, low]))

    has_after = jnp.where(place_ref[1] < 7, 1.0, 0.0)
    has_before = jnp.where(place_ref[1] > 0, 1.0, 0.0)
    inside = jnp.where(first_row, has_before, has_after)

    for k in range(4):
        pl.when(step == k)(lambda k=k: arrival(k).wait())

    def hidden_rows(first, fine_first, k_first, count):
        parts = []
        for i in range(0, count, 2):
            two = []
            for j in (i, i + 1):
                k, o = (fine_first + j) // 4, (fine_first + j) % 4
                lower, upper, shift = ROW_WEIGHTS[o]
                at = k_first + k + shift
                up = lower * coarse[at] + upper * coarse[at + 1]
                if fine_first + j < 0:
                    own = ends[0]
                else:
                    f = jnp.minimum(first + j - 1, 31)
                    own = rows_of([field[f, pl.ds(t, 8, stride=16), :] for t in range(16)])
                    if fine_first + j == 8:
                        own = jnp.where(step == 3, ends[1], own)
                x = rows_of([own, sides[first + j]]) + up
                lift[first + j] = x[:128]
                two.append(x)
            parts.append(three(normed(rows_of(two))))
        made = dot(rows_of(parts), expand3[...])
        for i in range(count):
            for c in range(0, EXPANDED, 128):
                out = bend(made[i * WIDE : (i + 1) * WIDE, c : c + 128])
                hid[first + i, :128, c : c + 128] = out[:128]
                hid[first + i, 128:, c : c + 128] = out[128:] * inside

    @pl.when(step == 0)
    def _():
        hidden_rows(0, -1, 1, 2)

        @pl.when(place_ref[0] == 0)
        def _():
            hid[0] = jnp.zeros((WIDE, EXPANDED), F32)

    hidden_rows(8 * step + 2, 1, 2 * step + 1, 4)
    hidden_rows(8 * step + 6, 5, 2 * step + 1, 4)

    @pl.when((step == 3) & (place_ref[0] == 15))
    def _():
        hid[33] = jnp.zeros((WIDE, EXPANDED), F32)

    lifted_ref[...] = lift[pl.ds(8 * step + 1, 8)]

    for part in range(EXPANDED // 128):
        lanes = slice(part * 128, (part + 1) * 128)
        taps = [
            [jnp.broadcast_to((GELU_IN * GELU_OUT) * depth_ref[i, j : j + 1, lanes], (8, 128)) for j in range(3)]
            for i in range(3)
        ]

        def row(r, summed):
            def column(t):
                seen = [hid[8 * step + r + i, 8 * t : 8 * t + 8, lanes] for i in range(3)]
                return [
                    seen[0] * taps[0][j] + seen[1] * taps[1][j] + seen[2] * taps[2][j]
                    for j in range(3)
                ]

            first, last, halo = column(0), column(15), column(16)
            before = jnp.where(first_row, halo[0], pltpu.roll(last[0], 1, 0))
            end = jnp.where(last_row, halo[2], pltpu.roll(first[2], 7, 0))
            here = first
            for t in range(16):
                following = column(t + 1) if t < 14 else last
                out = bend(here[1] + before + (following[2] if t < 15 else end))
                active[8 * step + r, part, 8 * t : 8 * t + 8] = out
                summed = summed + out
                before, here = here[0], following
            return summed

        summed = total[:, lanes]
        for r in range(8):
            summed = row(r, summed)
        total[:, lanes] = summed
        leaving(step, part).start()

    @pl.when(step == 3)
    def _():
        squeezed = lax.dot_general(
            total[...], reduce_ref[...], (((1,), (1,)), ((), ())), precision=HIGHEST,
            preferred_element_type=F32,
        )
        squeezed = jnp.sum(squeezed, axis=0, keepdims=True)
        padded = lanes_of([squeezed, jnp.zeros((1, 128 - SQUEEZE), F32)])
        sum_ref[...] = jnp.broadcast_to(padded, sum_ref.shape)
        for k in range(4):
            for part in range(4):
                leaving(k, part).wait()


def whole(shape):
    return pl.BlockSpec(shape, lambda *_: (0,) * len(shape))


def of_layer(array, layer):
    shape = (1,) + array.shape[1:]
    return pl.BlockSpec(shape, lambda *_: (layer,) + (0,) * (len(shape) - 1))


def lift_stage(place, args, copies):
    up = jnp.asarray(column_weights(), BF16)
    args = args[:6] + (up,) + args[6:]
    return pl.pallas_call(
        lift_kernel,
        grid=(4,),
        in_specs=[pl.BlockSpec(memory_space=pltpu.SMEM), pl.BlockSpec(memory_space=pl.ANY)]
        + [whole(a.shape) for a in args[1:]],
        out_specs=[
            pl.BlockSpec((8, 128, CHANNELS), lambda s: (s, 0, 0)),
            pl.BlockSpec(memory_space=pl.ANY),
            whole((copies, 128)),
        ],
        out_shape=[
            jax.ShapeDtypeStruct((32, 128, CHANNELS), F32),
            jax.ShapeDtypeStruct((32, EXPANDED // 128, 128, 128), F32),
            jax.ShapeDtypeStruct((copies, 128), F32),
        ],
        scratch_shapes=[
            pltpu.VMEM((32, EXPANDED // 128, 128, 128), F32),
            pltpu.VMEM((32, 128, CHANNELS), F32),
            pltpu.VMEM((2, 128, CHANNELS), F32),
            pltpu.VMEM((34, 8, CHANNELS), F32),
            pltpu.VMEM((34, 128, CHANNELS), F32),
            pltpu.VMEM((10, COARSE_WIDE, CHANNELS), F32),
            pltpu.VMEM((10, WIDE, CHANNELS), F32),
            pltpu.VMEM((34, WIDE, EXPANDED), F32),
            pltpu.VMEM((3 * CHANNELS, EXPANDED), BF16),
            pltpu.VMEM((8, EXPANDED), F32),
            pltpu.SemaphoreType.DMA((4,)),
            pltpu.SemaphoreType.DMA((4, 4)),
        ],
        compiler_params=pltpu.CompilerParams(vmem_limit_bytes=VMEM_LIMIT),
        cost_estimate=pl.CostEstimate(
            flops=8_000_000_000, bytes_accessed=14_000_000, transcendentals=0
        ),
    )(place, *args)


def block_kernel(
    cells_total, fed, lifted_ref, active_ref, sums_ref, sexp_ref, project_ref, gains_ref, qkv_ref,
    aout_ref, min_ref, mout_ref, out_ref, project, k3, qv3, out3, *feed_weights,
):
    @pl.when(pl.program_id(0) == 0)
    def _():
        pooled = jnp.sum(sums_ref[...], axis=0, keepdims=True) * (GELU_OUT / cells_total)
        squeezed = pooled[:, :SQUEEZE]
        squeezed = squeezed * jax.nn.sigmoid(squeezed)
        wide = jnp.broadcast_to(squeezed, (CHANNELS, SQUEEZE))
        gate = jnp.dot(wide, sexp_ref[...], precision=HIGHEST, preferred_element_type=F32)
        project[...] = deep_weight(project_ref[...] * (GELU_OUT * jax.nn.sigmoid(gate)).T)
        prepare_attention(qkv_ref, aout_ref, gains_ref[1:2], k3, qv3, out3)
        if fed:
            prepare_feed(min_ref, mout_ref, gains_ref[2:3], *feed_weights)

    def window(w, load):
        at = pl.ds(64 * (w % 2) + w // 2, WINDOW, stride=8)
        return rows_of([load(r, at) for r in range(WINDOW)])

    def expanded(r, at):
        return lanes_of([active_ref[r, k, at, :] for k in range(EXPANDED // 128)])

    def projected(start):
        halves = [split(window(w, expanded)) for w in range(start, start + PART // CELLS)]
        yield
        wide = dot(rows_of([h[0] for h in halves]), project[...])
        rest = dot(rows_of([h[1] for h in halves]), project[:, :CHANNELS])
        yield
        pairs = []
        for p in range(PART // PAIR):
            at = slice(p * PAIR, (p + 1) * PAIR)
            x = rows_of(
                [window(start + 2 * p + i, lambda r, at: lifted_ref[r, at, :]) for i in range(2)]
            )
            pairs.append(x + (wide[at, :CHANNELS] + (wide[at, CHANNELS:] + rest[at])))
        return pairs

    def group(part):
        pairs = yield from projected(part * PART // CELLS)
        pairs = yield from attend(pairs, k3, qv3, out3)
        if fed:
            pairs = yield from feed(pairs, *feed_weights)
        for p, x in enumerate(pairs):
            out_ref[part * PART + p * PAIR : part * PART + (p + 1) * PAIR] = x

    staggered(group(part) for part in range(BLOCK_STEP // PART))


ATTENTION_SCRATCH = [
    pltpu.VMEM((3 * CHANNELS, CHANNELS), BF16),
    pltpu.VMEM((2 * CHANNELS, 3 * CHANNELS), BF16),
    pltpu.VMEM((3 * CHANNELS, CHANNELS), BF16),
]
FEED_SCRATCH = [
    pltpu.VMEM((3 * CHANNELS, MLP_HIDDEN), BF16),
    pltpu.VMEM((MLP_HIDDEN, 2 * CHANNELS), BF16),
]


def block_stage(chunk, fed, lifted, active, sums, se_expand, project, gains, weights, cells_total):
    steps = 4 // CHUNKS
    row_base = chunk * (4 // CHUNKS)
    rest = (sums, se_expand, project, gains)

    columns = BLOCK_STEP // 8
    strips = [
        pl.BlockSpec((8, columns, CHANNELS), lambda s: (row_base + s, 0, 0)),
        pl.BlockSpec((8, EXPANDED // 128, columns, 128), lambda s: (row_base + s, 0, 0, 0)),
    ]

    def body(*refs):
        block_kernel(cells_total, fed, *refs)

    return pl.pallas_call(
        body,
        grid=(steps,),
        in_specs=strips
        + [whole(a.shape) for a in rest]
        + [of_layer(w, 0) for w in weights],
        out_specs=pl.BlockSpec((BLOCK_STEP, CHANNELS), lambda s: (s, 0)),
        out_shape=jax.ShapeDtypeStruct((steps * BLOCK_STEP, CHANNELS), F32),
        scratch_shapes=[
            pltpu.VMEM((EXPANDED, 2 * CHANNELS), BF16),
        ]
        + ATTENTION_SCRATCH
        + (FEED_SCRATCH if fed else []),
        compiler_params=pltpu.CompilerParams(vmem_limit_bytes=VMEM_LIMIT),
        cost_estimate=pl.CostEstimate(
            flops=14_000_000_000, bytes_accessed=8_000_000, transcendentals=0
        ),
    )(lifted, active, *rest, *weights)


def grid_kernel(fed, x_ref, gains_ref, *refs):
    scratch = 5 if fed else 7
    out_ref, k3, qv3, out3, *feeds = refs[-scratch - 1 :]
    qkv_ref, aout_ref, *feed_refs = refs[: 4 if fed else 6]

    @pl.when(pl.program_id(0) == 0)
    def _():
        prepare_attention(qkv_ref, aout_ref, gains_ref[3:4], k3, qv3, out3)
        prepare_feed(*feed_refs[:2], gains_ref[4:5], *feeds[:2])
        if not fed:
            prepare_feed(*feed_refs[2:], gains_ref[2:3], *feeds[2:])

    stride = GRID_STEP // GROUP
    flat_in = x_ref.reshape(GRID_STEP, CHANNELS)
    flat_out = out_ref.reshape(GRID_STEP, CHANNELS)

    def group(part):
        first = part * PART // GROUP
        windows = [flat_in[pl.ds(first + p, GROUP, stride=stride), :] for p in range(PART // GROUP)]
        pairs = [rows_of(windows[i : i + 2]) for i in range(0, len(windows), 2)]
        if not fed:
            pairs = yield from feed(pairs, *feeds[2:])
        pairs = yield from attend(pairs, k3, qv3, out3)
        pairs = yield from feed(pairs, *feeds[:2])
        for p, x in enumerate(pairs):
            for i in range(2):
                window = first + 2 * p + i
                flat_out[pl.ds(window, GROUP, stride=stride), :] = x[i * GROUP : (i + 1) * GROUP]

    staggered(group(part) for part in range(GRID_STEP // PART))


def grid_stage(received, fed, gains, weights, chunk, earlier):
    per_device = received.shape[1]
    steps = per_device * GROUP // GRID_STEP
    shape = (GROUP, GRID_STEP // GROUP, CHANNELS)
    in_specs = [pl.BlockSpec(shape, lambda s: (0, s, 0)), whole(gains.shape)]
    in_specs += [of_layer(w, 1) for w in weights]
    args = (received, gains) + weights
    if not fed:
        in_specs += [of_layer(w, 0) for w in weights[2:]]
        args += weights[2:]
    aliases = {}
    if earlier is not None:
        in_specs.append(pl.BlockSpec(memory_space=pl.ANY))
        aliases = {len(args): 0}
        args += (earlier,)

    def body(*refs):
        grid_kernel(fed, *refs)

    return pl.pallas_call(
        body,
        grid=(steps,),
        in_specs=in_specs,
        out_specs=pl.BlockSpec(shape, lambda s: (0, chunk * steps + s, 0)),
        out_shape=jax.ShapeDtypeStruct((GROUP, CHUNKS * per_device, CHANNELS), F32),
        scratch_shapes=ATTENTION_SCRATCH + FEED_SCRATCH + ([] if fed else FEED_SCRATCH),
        input_output_aliases=aliases,
        compiler_params=pltpu.CompilerParams(vmem_limit_bytes=VMEM_LIMIT),
        cost_estimate=pl.CostEstimate(
            flops=14_000_000_000, bytes_accessed=4_000_000, transcendentals=0
        ),
    )(*args)


def by_pairs(edge, at, axis, count):
    even = at % 2 == 0
    swaps = []
    for first, last in ((1, jnp.logical_not(even)), (0, even)):
        lower = [(i, i + 1) for i in range(first, count - 1, 2)]
        pairs = lower + [(b, a) for a, b in lower]
        swaps.append(lax.ppermute(edge(last), axis, pairs))
    return swaps[::-1]


def per_device(
    field, context, ctx_weight, norm_gains, expand_weight, depth_weight, se_reduce, se_expand,
    project_weight, attn_qkv, attn_out, mlp_in, mlp_out,
):
    row_axis = ("rg", "core")
    rows, cols = 16, 8
    row = lax.axis_index(row_axis)
    col = lax.axis_index("col")

    def row_edge(last):
        fine = lax.dynamic_index_in_dim(field, jnp.where(last, 31, 0), 0, keepdims=False)
        of_context = lax.dynamic_index_in_dim(context, jnp.where(last, 7, 0), 0, keepdims=False)
        return jnp.concatenate([fine, of_context], axis=0)

    rows_a, rows_b = by_pairs(row_edge, row, row_axis, rows)
    odd = row % 2 == 1

    def column_edge(last):
        fine_at, coarse_at = jnp.where(last, 127, 0), jnp.where(last, 31, 0)

        def one(x, at):
            return lax.dynamic_slice_in_dim(x, at, 1, axis=x.ndim - 2).reshape(-1, CHANNELS)

        parts = []
        for start, stop, tile, at in ((0, 128, field, fine_at), (128, 160, context, coarse_at)):
            of_a, of_b = one(rows_a[start:stop], at), one(rows_b[start:stop], at)
            parts += [jnp.where(odd, of_a, of_b), one(tile, at), jnp.where(odd, of_b, of_a)]
        return jnp.concatenate(parts, axis=0)

    cols_a, cols_b = by_pairs(column_edge, col, "col", cols)
    place = jnp.stack([row, col]).astype(jnp.int32)
    lifted, active, partial = lift_stage(
        place,
        (
            field, context, rows_a, rows_b, cols_a, cols_b, ctx_weight, norm_gains, expand_weight,
            depth_weight, se_reduce.T,
        ),
        rows * cols,
    )

    def exchange(x, axes):
        return lax.all_to_all(x, axes, split_axis=0, concat_axis=0, tiled=True)

    group = ("rg", "col")
    sums = exchange(partial[:, None, :], ("rg", "core", "col"))[:, 0, :]

    weights = (attn_qkv, attn_out, mlp_in, mlp_out)
    cells_total = rows * cols * field.shape[0] * field.shape[1]
    sent = []
    for chunk in range(CHUNKS):
        mine = block_stage(
            chunk, chunk > 0, lifted, active, sums, se_expand, project_weight, norm_gains, weights,
            cells_total,
        )
        sent.append(exchange(mine.reshape(GROUP, -1, CHANNELS), group))
    attended = None
    for chunk in range(CHUNKS):
        attended = grid_stage(sent[chunk], chunk > 0, norm_gains, weights, chunk, attended)
    back = exchange(attended, group)
    halves = back.reshape(4 // CHUNKS, 16, 2, CHUNKS, WINDOW // 2, WINDOW, CHANNELS)
    return halves.transpose(3, 0, 2, 4, 1, 5, 6).reshape(field.shape)


def solution(mesh):
    fine = Mesh(mesh.devices.reshape(8, 2, 8), ("rg", "core", "col"))
    tiled = P(("rg", "core"), "col", None)
    return jax.shard_map(
        per_device,
        mesh=fine,
        in_specs=(tiled, tiled) + (P(),) * 11,
        out_specs=tiled,
        check_vma=False,
    )
```
